32 devices in a mesh: frame: 8 (over z, x), batch: 4 (over y, core).
Axes of the slice: x: 2, y: 2, z: 4, core: 2. Of those that a mesh axis runs over, the one named last changes fastest.
Arguments:
- clean: float32 [2, 4, 32, 3, 256], P(None, 'batch', 'frame'), may hold values from -6 to 6
- noise: float32 [2, 4, 32, 3, 256], P(None, 'batch', 'frame'), may hold values from -6 to 6
- timesteps: int32 [2, 4, 1], replicated, may hold values from 0 to 999
- frame_counts: int32 [2, 4, 1], replicated, may hold values from 8 to 32, as said below
- conv_weight: float32 [9216, 256], P('frame', 'batch'), may hold values from -0.125 to 0.125
- conv_first: float32 [9216, 256], P('frame', 'batch'), may hold values from -1.9073486e-05 to 1.9073486e-05
- conv_second: float32 [9216, 256], P('frame', 'batch'), may hold values from 3.9805537e-13 to 6.634256e-12
- proj_in: float32 [512, 768], P('frame', 'batch'), may hold values from -0.375 to 0.375
- proj_in_first: float32 [512, 768], P('frame', 'batch'), may hold values from -1.9073486e-05 to 1.9073486e-05
- proj_in_second: float32 [512, 768], P('frame', 'batch'), may hold values from 3.9805537e-13 to 6.634256e-12
- proj_out: float32 [512, 256], P('frame', 'batch'), may hold values from -1 to 1
- proj_out_first: float32 [512, 256], P('frame', 'batch'), may hold values from -1.9073486e-05 to 1.9073486e-05
- proj_out_second: float32 [512, 256], P('frame', 'batch'), may hold values from 3.9805537e-13 to 6.634256e-12
- time_weight: float32 [512, 256], P('frame', 'batch'), may hold values from -0.375 to 0.375
- time_first: float32 [512, 256], P('frame', 'batch'), may hold values from -1.9073486e-05 to 1.9073486e-05
- time_second: float32 [512, 256], P('frame', 'batch'), may hold values from 3.9805537e-13 to 6.634256e-12
- in_weight: float32 [3, 256], replicated, may hold values from -3.5 to 3.5
- in_first: float32 [3, 256], replicated, may hold values from -0.00012207031 to 0.00012207031
- in_second: float32 [3, 256], replicated, may hold values from 1.4648438e-12 to 2.4414063e-11
- out_weight: float32 [3, 256], replicated, may hold values from -0.375 to 0.375
- out_first: float32 [3, 256], replicated, may hold values from -0.00036621094 to 0.00036621094
- out_second: float32 [3, 256], replicated, may hold values from 1.4648438e-10 to 2.4414062e-09
- gains: float32 [7, 256], replicated, may hold values from 0.4 to 2.6
- gains_first: float32 [7, 256], replicated, may hold values from -0.00012207031 to 0.00012207031
- gains_second: float32 [7, 256], replicated, may hold values from 1.4648438e-12 to 2.4414063e-11
- rel_bias: float32 [4, 32], replicated, may hold values from -4 to 4
- rel_bias_first: float32 [4, 32], replicated, may hold values from -3.8146973e-06 to 3.8146973e-06
- rel_bias_second: float32 [4, 32], replicated, may hold values from 1.4648437e-14 to 2.4414062e-13
Outputs:
- loss_sum: float32 [], replicated
- pixel_count: float32 [], replicated
- grad_norm: float32 [], replicated
- conv_new: float32 [9216, 256], P('frame', 'batch')
- conv_first_new: float32 [9216, 256], P('frame', 'batch')
- conv_second_new: float32 [9216, 256], P('frame', 'batch')
- proj_in_new: float32 [512, 768], P('frame', 'batch')
- proj_in_first_new: float32 [512, 768], P('frame', 'batch')
- proj_in_second_new: float32 [512, 768], P('frame', 'batch')
- proj_out_new: float32 [512, 256], P('frame', 'batch')
- proj_out_first_new: float32 [512, 256], P('frame', 'batch')
- proj_out_second_new: float32 [512, 256], P('frame', 'batch')
- time_new: float32 [512, 256], P('frame', 'batch')
- time_first_new: float32 [512, 256], P('frame', 'batch')
- time_second_new: float32 [512, 256], P('frame', 'batch')
- in_new: float32 [3, 256], replicated
- in_first_new: float32 [3, 256], replicated
- in_second_new: float32 [3, 256], replicated
- out_new: float32 [3, 256], replicated
- out_first_new: float32 [3, 256], replicated
- out_second_new: float32 [3, 256], replicated
- gains_new: float32 [7, 256], replicated
- gains_first_new: float32 [7, 256], replicated
- gains_second_new: float32 [7, 256], replicated
- rel_bias_new: float32 [4, 32], replicated
- rel_bias_first_new: float32 [4, 32], replicated
- rel_bias_second_new: float32 [4, 32], replicated
The draws below stay inside these ranges and needn't reach their ends.
Inputs may be any that keep to these rules, and one draw needn't show every extreme that they name: `frame_counts`: each value is 8, 16 or 32; in every draw some video has 32 valid frames.
All inputs are finite; a program needn't handle non-finite values.
Results may differ from the reference program's by a relative error of at most 0.012.
The reference program's roundings to bfloat16 on the way count: a program that leaves them out, or rounds other values in their place, can miss the bound.
Values may be sent and summed in bfloat16 or wider, within the bound.
A program may use at most 256 MiB of HBM per device.

```python
import math
import jax
import jax.numpy as jnp
from jax import lax

D = 256
HEADS = 4
BUCKETS = 32
FRAMES = 32
SIDE = 16
MICRO = 2
TSTEPS = 1000
STEP = 10
P_SIZE = 256
GROUPS = 4
GROUP_FRAMES = 32
GROUP_VIDEOS = 1


def draw_frame_counts(key, part):
    key = jax.random.fold_in(key, 11)
    key_levels, key_spot = jax.random.split(key)
    total_videos = MICRO * GROUPS * GROUP_VIDEOS
    levels = jax.random.randint(key_levels, (total_videos,), 0, 3)
    chosen = jax.random.randint(key_spot, (), 0, total_videos)
    levels = jnp.where(jnp.arange(total_videos) == chosen, 2, levels)
    counts = FRAMES // 4 * jnp.where(levels == 2, 4, levels + 1)
    return counts.reshape(MICRO, GROUPS, GROUP_VIDEOS).astype(jnp.int32)


def draw_gains(key, part):
    key = jax.random.fold_in(key, 7)
    rising = 0.6 * 3.0 ** (jnp.arange(D, dtype=jnp.float32) / D)
    factor = jax.random.uniform(key, (7, D), jnp.float32, 0.8, 1.25)
    return (rising[None, :] * factor).astype(jnp.float32)


def set_ends(values, key, low, high):
    longest = values.shape.index(max(values.shape))
    spots = []
    for shift in (0, 1):
        where = [jax.random.randint(jax.random.fold_in(key, axis), (), 0, length) for axis, length in enumerate(values.shape)]
        where[longest] = (where[longest] + shift) % values.shape[longest]
        spots.append(tuple(where))
    return values.at[spots[0]].set(low).at[spots[1]].set(high)


def level_of(stream_key, extent, cuts, smallest, high):
    def one(position, parts):
        draws = jax.random.uniform(jax.random.fold_in(jax.random.fold_in(stream_key, 6), position), (parts,), jnp.float32, smallest / len(cuts), high / len(cuts))
        return jnp.repeat(jnp.exp(draws), extent[position] // parts).reshape((-1,) + (1,) * (len(extent) - position - 1))

    gain = one(*cuts[0])
    for cut in cuts[1:]:
        gain = gain * one(*cut)
    return gain


def gaussian(stream_key, shape, scale, bound, shards=(), held_as=jnp.bfloat16):
    level = level_of(stream_key, shape, shards, -0.22, 0.18) if shards else 1.0
    array = jax.random.normal(stream_key, shape, jnp.float32) * scale * level
    return jnp.minimum(jnp.maximum(array, -bound), bound).astype(held_as)


def setup_inputs(seed: int = 0) -> dict:
    seeds = jax.random.split(jax.random.key(seed), 29)
    return {
        "clean": gaussian(seeds[0], (MICRO, GROUPS, GROUP_FRAMES, 3, P_SIZE), 1.0, 6.0, ((1, 4), (2, 8)), jnp.float32),
        "noise": gaussian(seeds[1], (MICRO, GROUPS, GROUP_FRAMES, 3, P_SIZE), 1.0, 6.0, ((1, 4), (2, 8)), jnp.float32),
        "timesteps": set_ends(jax.random.randint(seeds[2], (MICRO, GROUPS, GROUP_VIDEOS), 0, TSTEPS), jax.random.fold_in(seeds[2], 1), 0, TSTEPS - 1).astype(jnp.int32),
        "frame_counts": draw_frame_counts(jax.random.fold_in(seeds[28], 71), 0),
        "conv_weight": gaussian(seeds[4], (36 * D, D), (9 * D) ** -0.5, 0.125, ((0, 8), (1, 4)), jnp.float32),
        "conv_first": gaussian(seeds[5], (36 * D, D), (0.0056 / (46 * D * D) ** 0.5), 1.9073486328125e-05, ((0, 8), (1, 4)), jnp.float32),
        "conv_second": jnp.clip(jnp.exp(math.log(6.634256078524858e-12) - 2.8134107 * jax.random.uniform(seeds[6], (36 * D, D), jnp.float32) ** level_of(seeds[6], (36 * D, D), ((0, 8), (1, 4)), -0.2, 0.2)), 3.98055367964098e-13, 6.634256078524858e-12),
        "proj_in": gaussian(seeds[7], (2 * D, 3 * D), D ** -0.5, 0.375, ((0, 8), (1, 4)), jnp.float32),
        "proj_in_first": gaussian(seeds[8], (2 * D, 3 * D), (0.0056 / (46 * D * D) ** 0.5), 1.9073486328125e-05, ((0, 8), (1, 4)), jnp.float32),
        "proj_in_second": jnp.clip(jnp.exp(math.log(6.634256078524858e-12) - 2.8134107 * jax.random.uniform(seeds[9], (2 * D, 3 * D), jnp.float32) ** level_of(seeds[9], (2 * D, 3 * D), ((0, 8), (1, 4)), -0.2, 0.2)), 3.98055367964098e-13, 6.634256078524858e-12),
        "proj_out": gaussian(seeds[10], (2 * D, D), (D // 8) ** -0.5, 1.0, ((0, 8), (1, 4)), jnp.float32),
        "proj_out_first": gaussian(seeds[11], (2 * D, D), (0.0056 / (46 * D * D) ** 0.5), 1.9073486328125e-05, ((0, 8), (1, 4)), jnp.float32),
        "proj_out_second": jnp.clip(jnp.exp(math.log(6.634256078524858e-12) - 2.8134107 * jax.random.uniform(seeds[12], (2 * D, D), jnp.float32) ** level_of(seeds[12], (2 * D, D), ((0, 8), (1, 4)), -0.2, 0.2)), 3.98055367964098e-13, 6.634256078524858e-12),
        "time_weight": gaussian(seeds[13], (2 * D, D), D ** -0.5, 0.375, ((0, 8), (1, 4)), jnp.float32),
        "time_first": gaussian(seeds[14], (2 * D, D), (0.0056 / (46 * D * D) ** 0.5), 1.9073486328125e-05, ((0, 8), (1, 4)), jnp.float32),
        "time_second": jnp.clip(jnp.exp(math.log(6.634256078524858e-12) - 2.8134107 * jax.random.uniform(seeds[15], (2 * D, D), jnp.float32) ** level_of(seeds[15], (2 * D, D), ((0, 8), (1, 4)), -0.2, 0.2)), 3.98055367964098e-13, 6.634256078524858e-12),
        "in_weight": gaussian(seeds[16], (3, D), 3 ** -0.5, 3.5, (), jnp.float32),
        "in_first": gaussian(seeds[17], (3, D), (0.0019 / (32 * D) ** 0.5), 0.00012207031, (), jnp.float32),
        "in_second": jnp.clip(jnp.exp(jax.random.uniform(seeds[18], (3, D), jnp.float32, math.log(1.464843762781498e-12), math.log(2.4414062785305113e-11))), 1.464843762781498e-12, 2.4414062785305113e-11),
        "out_weight": gaussian(seeds[19], (3, D), D ** -0.5, 0.375, (), jnp.float32),
        "out_first": gaussian(seeds[20], (3, D), (0.0056 / (32 * D) ** 0.5), 0.00036621094, (), jnp.float32),
        "out_second": jnp.clip(jnp.exp(jax.random.uniform(seeds[21], (3, D), jnp.float32, math.log(1.4648438018127763e-10), math.log(2.4414061883248905e-09))), 1.4648438018127763e-10, 2.4414061883248905e-09),
        "gains": draw_gains(jax.random.fold_in(seeds[28], 71), 0),
        "gains_first": gaussian(seeds[23], (7, D), (0.0019 / (32 * D) ** 0.5), 0.00012207031, (), jnp.float32),
        "gains_second": jnp.clip(jnp.exp(jax.random.uniform(seeds[24], (7, D), jnp.float32, math.log(1.464843762781498e-12), math.log(2.4414062785305113e-11))), 1.464843762781498e-12, 2.4414062785305113e-11),
        "rel_bias": gaussian(seeds[25], (HEADS, BUCKETS), 1.0, 4.0, (), jnp.float32),
        "rel_bias_first": gaussian(seeds[26], (HEADS, BUCKETS), (0.000056 / (32 * D) ** 0.5), 3.814697265625e-06, (), jnp.float32),
        "rel_bias_second": jnp.clip(jnp.exp(jax.random.uniform(seeds[27], (HEADS, BUCKETS), jnp.float32, math.log(1.464843701795126e-14), math.log(2.441406180952316e-13))), 1.464843701795126e-14, 2.441406180952316e-13),
    }


HIGH = lax.Precision.HIGHEST
EPS_NORM = 1e-06
CLIP = 0.05
BETA_ONE = 0.9
BETA_TWO = 0.999
ADAM_EPS = 1e-08
DECAY = 0.01
RATES = (0.02, 0.06, 0.18, 0.06, 0.6, 0.06, 1.0, 1.0)
NEG = -1000000000.0

@jax.custom_vjp
def low(v):
    return lax.optimization_barrier(v.astype(jnp.bfloat16)).astype(jnp.float32)

@jax.custom_vjp
def low_back(v):
    return v

def low_keep(v):
    return (low(v), None)

def low_pass(kept, grad):
    return (grad,)

def back_keep(v):
    return (v, None)

def back_low(kept, grad):
    return (low(grad),)
low.defvjp(low_keep, low_pass)
low_back.defvjp(back_keep, back_low)

def swish(values):
    return values * jax.nn.sigmoid(values)

def rms_norm(values, gain_vec):
    return values * lax.rsqrt(lax.optimization_barrier(jnp.mean(values * values, -1, keepdims=True)) + EPS_NORM) * gain_vec

def conv_apply(acts, kernel):
    frames, pixels, width = acts.shape
    frame_grid = acts.reshape(frames, SIDE, SIDE, width)
    padded = jnp.pad(frame_grid, ((0, 0), (1, 1), (1, 1), (0, 0)))
    columns = jnp.concatenate([padded[:, offset // 3:offset // 3 + SIDE, offset % 3:offset % 3 + SIDE] for offset in range(9)], -1)
    result = jnp.matmul(columns.reshape(frames * pixels, 9 * width), kernel, precision=HIGH)
    return result.reshape(frames, pixels, width)

def bucket_table():
    offsets = jnp.arange(FRAMES)
    distance = offsets[None, :] - offsets[:, None]
    return (jnp.minimum(jnp.abs(distance), 15) + 16 * (distance > 0).astype(jnp.int32)).astype(jnp.int32)

def attend(packed, bias_mat, valid):
    batch, length, _ = packed.shape
    split_heads = packed.reshape(batch, length, 3, HEADS, D // HEADS)
    scores = low_back(jnp.einsum('blhe,bmhe->bhlm', split_heads[:, :, 0], split_heads[:, :, 1], precision=HIGH) / math.sqrt(D // HEADS)) + bias_mat
    scores = jnp.where(valid[:, None, None, :], scores, NEG)
    shifted = jnp.exp(scores - lax.optimization_barrier(jnp.max(scores, -1, keepdims=True)))
    attn_probs = low(shifted / lax.optimization_barrier(jnp.sum(shifted, -1, keepdims=True)))
    mixture = jnp.einsum('bhlm,bmhe->blhe', attn_probs, split_heads[:, :, 2], precision=HIGH)
    return low(low_back(mixture.reshape(batch, length, D)))

def video_loss(params, one_clean, one_noise, one_step, one_count, pixel_total):
    conv_w, proj_in, proj_out, time_w, in_w, out_w, gains, rel_bias = params
    levels = one_step.astype(jnp.float32)
    alpha_bar = jnp.cos(0.5 * math.pi * (levels + 1.0) / (TSTEPS + 1.0)) ** 2
    noisy_input = jnp.sqrt(alpha_bar) * one_clean + jnp.sqrt(1.0 - alpha_bar) * one_noise
    hidden = jnp.einsum('fcp,cd->fpd', noisy_input, in_w, precision=HIGH)
    half_width = D // 2
    frequency = jnp.exp(-math.log(10000.0) * jnp.arange(half_width, dtype=jnp.float32) / half_width)
    embedding = low(jnp.concatenate([jnp.sin(levels * frequency), jnp.cos(levels * frequency)]))
    time_bias = swish(jnp.einsum('d,jde->je', embedding, low(time_w).reshape(2, D, D), precision=HIGH))
    kernels = low(conv_w).reshape(4, 9 * D, D)
    in_mats = low(proj_in).reshape(2, D, 3 * D)
    out_mats = low(proj_out).reshape(2, D, D)
    live_frames = jnp.arange(FRAMES) < one_count

    def residual(hidden, block):
        acts_one = low(swish(rms_norm(hidden, gains[4 * block])))
        inner_act = low_back(conv_apply(acts_one, kernels[2 * block])) + time_bias[block]
        acts_two = low(swish(rms_norm(inner_act, gains[4 * block + 1])))
        return hidden + low_back(conv_apply(acts_two, kernels[2 * block + 1]))

    def mixer(hidden, layer, temporal):
        normed = low(rms_norm(hidden, gains[2 + layer]))
        packed = low(low_back(jnp.matmul(normed, in_mats[layer], precision=HIGH)))
        if temporal:
            bias_mat = rel_bias[:, bucket_table()]
            valid = jnp.broadcast_to(live_frames[None, :], (SIDE * SIDE, FRAMES))
            mixture = jnp.transpose(attend(jnp.transpose(packed, (1, 0, 2)), bias_mat, valid), (1, 0, 2))
        else:
            valid = jnp.ones((FRAMES, SIDE * SIDE), bool)
            mixture = attend(packed, 0.0, valid)
        return hidden + low_back(jnp.matmul(mixture, out_mats[layer], precision=HIGH))
    hidden = residual(hidden, 0)
    hidden = mixer(hidden, 0, False)
    hidden = mixer(hidden, 1, True)
    hidden = residual(hidden, 1)
    normed = low(rms_norm(hidden, gains[6]))
    predicted = jnp.einsum('fpd,cd->fcp', normed, low(out_w), precision=HIGH)
    square = jnp.sum(live_frames.astype(jnp.float32)[:, None, None] * (predicted - one_noise) ** 2)
    return (square / pixel_total, square)

def adamw(weight, moment_one, moment_two, grad, clip_scale, step_rate):
    grad = grad * clip_scale
    moment_one = BETA_ONE * moment_one + (1.0 - BETA_ONE) * grad
    moment_two = BETA_TWO * moment_two + (1.0 - BETA_TWO) * grad * grad
    update = moment_one / (1.0 - BETA_ONE ** STEP) / (jnp.sqrt(moment_two / (1.0 - BETA_TWO ** STEP)) + ADAM_EPS)
    return (weight - step_rate * (update + DECAY * weight), moment_one, moment_two)

def reference(clean, noise, timesteps, frame_counts, conv_weight, conv_first, conv_second, proj_in, proj_in_first, proj_in_second, proj_out, proj_out_first, proj_out_second, time_weight, time_first, time_second, in_weight, in_first, in_second, out_weight, out_first, out_second, gains, gains_first, gains_second, rel_bias, rel_bias_first, rel_bias_second):
    pixels = SIDE * SIDE
    videos_clean = clean.reshape(-1, FRAMES, 3, pixels)
    videos_noise = noise.reshape(-1, FRAMES, 3, pixels)
    steps_all = timesteps.reshape(-1)
    counts_all = frame_counts.reshape(-1)
    pixel_total = jnp.sum(counts_all).astype(jnp.float32) * pixels
    weights = (conv_weight, proj_in, proj_out, time_weight, in_weight, out_weight, gains, rel_bias)

    def visit(carry, item):
        grads, loss_acc = carry
        one_clean, one_noise, one_step, one_count = item

        def scaled(params):
            return video_loss(params, one_clean, one_noise, one_step, one_count, pixel_total)
        primal, pullback, square = jax.vjp(scaled, weights, has_aux=True)
        grad_video, = pullback(jnp.ones_like(primal))
        return ((jax.tree.map(jnp.add, grads, grad_video), loss_acc + square), None)
    start = (jax.tree.map(jnp.zeros_like, weights), jnp.zeros((), jnp.float32))
    (grads, loss_sum), _ = lax.scan(visit, start, (videos_clean, videos_noise, steps_all, counts_all))
    grad_norm = jnp.sqrt(sum((jnp.sum(grad * grad) for grad in grads)))
    clip_scale = CLIP / jnp.maximum(grad_norm, CLIP)
    conv_new, conv_first_new, conv_second_new = adamw(conv_weight, conv_first, conv_second, grads[0], clip_scale, RATES[0])
    pin_new, pin_first_new, pin_second_new = adamw(proj_in, proj_in_first, proj_in_second, grads[1], clip_scale, RATES[1])
    pout_new, pout_first_new, pout_second_new = adamw(proj_out, proj_out_first, proj_out_second, grads[2], clip_scale, RATES[2])
    time_new, time_first_new, time_second_new = adamw(time_weight, time_first, time_second, grads[3], clip_scale, RATES[3])
    in_new, in_first_new, in_second_new = adamw(in_weight, in_first, in_second, grads[4], clip_scale, RATES[4])
    out_new, out_first_new, out_second_new = adamw(out_weight, out_first, out_second, grads[5], clip_scale, RATES[5])
    gains_new, gains_first_new, gains_second_new = adamw(gains, gains_first, gains_second, grads[6], clip_scale, RATES[6])
    bias_new, bias_first_new, bias_second_new = adamw(rel_bias, rel_bias_first, rel_bias_second, grads[7], clip_scale, RATES[7])
    return (loss_sum, pixel_total, grad_norm, conv_new, conv_first_new, conv_second_new, pin_new, pin_first_new, pin_second_new, pout_new, pout_first_new, pout_second_new, time_new, time_first_new, time_second_new, in_new, in_first_new, in_second_new, out_new, out_first_new, out_second_new, gains_new, gains_first_new, gains_second_new, bias_new, bias_first_new, bias_second_new)
```

```python
import math

import jax
import jax.numpy as jnp
from jax import lax
from jax.experimental import pallas as pl
from jax.experimental.pallas import tpu as pltpu
from jax.sharding import PartitionSpec as P

D = 256
HEADS = 4
FRAMES = 32
SIDE = 16
MICRO = 2
TSTEPS = 1000
STEP = 10


HIGH = lax.Precision.HIGHEST
EPS_NORM = 1e-06
CLIP = 0.05
BETA_ONE = 0.9
BETA_TWO = 0.999
ADAM_EPS = 1e-08
DECAY = 0.01
RATES = (0.02, 0.06, 0.18, 0.06, 0.6, 0.06, 1.0, 1.0)
NEG = -1000000000.0


def swish(values):
    return values * jax.nn.sigmoid(values)


def swish_grad(values):
    sigma_v = jax.nn.sigmoid(values)
    return sigma_v * (1.0 + values * (1.0 - sigma_v))


def norm_fwd(values, gain_vec):
    inverse = lax.rsqrt(jnp.mean(values * values, -1, keepdims=True) + EPS_NORM)
    return (values * inverse * gain_vec, inverse)


def norm_bwd(values, inverse, gain_vec, upstream):
    scaled = upstream * gain_vec
    dvalues = inverse * scaled - values * inverse**3 * jnp.mean(values * scaled, -1, keepdims=True)
    return (dvalues, jnp.sum(upstream * values * inverse, axis=(0, 1)))


def patches(acts):
    frames, pixels, width = acts.shape
    frame_grid = acts.reshape(frames, SIDE, SIDE, width)
    padded = jnp.pad(frame_grid, ((0, 0), (1, 1), (1, 1), (0, 0)))
    columns = [
        padded[:, offset // 3 : offset // 3 + SIDE, offset % 3 : offset % 3 + SIDE]
        for offset in range(9)
    ]
    return jnp.concatenate(columns, -1).reshape(frames * pixels, 9 * width)


def conv_fwd(acts, kernel):
    frames, pixels, width = acts.shape
    return jnp.dot(patches(acts), kernel, preferred_element_type=jnp.float32).reshape(
        frames, pixels, width
    )


def conv_bwd(acts, grad_low, kernel):
    frames, pixels, width = grad_low.shape
    flat_grad = grad_low.reshape(frames * pixels, width)
    dkernel = lax.dot_general(
        patches(acts), flat_grad, (((0,), (0,)), ((), ())), preferred_element_type=jnp.float32
    )
    tap_terms = lax.dot_general(
        flat_grad, kernel, (((1,), (1,)), ((), ())), preferred_element_type=jnp.float32
    )
    padded = jnp.pad(
        tap_terms.reshape(frames, SIDE, SIDE, 9, width), ((0, 0), (1, 1), (1, 1), (0, 0), (0, 0))
    )
    dacts = sum(
        (
            padded[
                :,
                2 - offset // 3 : 2 - offset // 3 + SIDE,
                2 - offset % 3 : 2 - offset % 3 + SIDE,
                offset,
            ]
            for offset in range(9)
        )
    )
    return (dacts.reshape(frames, pixels, width), dkernel)


def res_fwd(hidden, kern_one, kern_two, gain_one, gain_two, frame_bias):
    normed, inverse_one = norm_fwd(hidden, gain_one)
    acts_one = swish(normed).astype(jnp.bfloat16)
    inner_act = conv_fwd(acts_one, kern_one) + frame_bias
    second_norm, inverse_two = norm_fwd(inner_act, gain_two)
    acts_two = swish(second_norm).astype(jnp.bfloat16)
    saved = (normed, inverse_one, acts_one, inner_act, second_norm, inverse_two, acts_two)
    return (hidden + conv_fwd(acts_two, kern_two), saved)


def res_bwd(hidden, upstream, kern_one, kern_two, gain_one, gain_two, saved):
    normed, inverse_one, acts_one, inner_act, second_norm, inverse_two, acts_two = saved
    dacts_two, dkern_two = conv_bwd(acts_two, upstream.astype(jnp.bfloat16), kern_two)
    dinner, dgain_two = norm_bwd(
        inner_act, inverse_two, gain_two, dacts_two * swish_grad(second_norm)
    )
    dacts_one, dkern_one = conv_bwd(acts_one, dinner.astype(jnp.bfloat16), kern_one)
    dhidden, dgain_one = norm_bwd(hidden, inverse_one, gain_one, dacts_one * swish_grad(normed))
    return (upstream + dhidden, dkern_one, dkern_two, dgain_one, dgain_two, jnp.sum(dinner, 1))


def attend_probs(packed, bias_mat, valid):
    batch, length, _ = packed.shape
    split_heads = packed.reshape(batch, length, 3, HEADS, D // HEADS)
    scores = (
        jnp.einsum(
            "blhe,bmhe->bhlm",
            split_heads[:, :, 0],
            split_heads[:, :, 1],
            preferred_element_type=jnp.float32,
        )
        / math.sqrt(D // HEADS)
        + bias_mat
    )
    if valid is not None:
        scores = jnp.where(valid[:, None, None, :], scores, NEG)
    shifted = jnp.exp(scores - jnp.max(scores, -1, keepdims=True))
    return (shifted / jnp.sum(shifted, -1, keepdims=True), split_heads)


def attend_fwd(packed, bias_mat, valid):
    attn_probs, split_heads = attend_probs(packed, bias_mat, valid)
    mixture = jnp.einsum(
        "bhlm,bmhe->blhe",
        attn_probs.astype(jnp.bfloat16),
        split_heads[:, :, 2],
        preferred_element_type=jnp.float32,
    )
    return mixture.reshape(packed.shape[0], packed.shape[1], D).astype(jnp.bfloat16)


def attend_bwd(packed, dmixture, bias_mat, valid):
    batch, length, _ = packed.shape
    attn_probs, split_heads = attend_probs(packed, bias_mat, valid)
    grad_heads = dmixture.reshape(batch, length, HEADS, D // HEADS)
    dattn_probs = jnp.einsum(
        "blhe,bmhe->bhlm", grad_heads, split_heads[:, :, 2], preferred_element_type=jnp.float32
    )
    dvalues = jnp.einsum(
        "bhlm,blhe->bmhe",
        attn_probs.astype(jnp.bfloat16),
        grad_heads,
        preferred_element_type=jnp.float32,
    )
    dscores = attn_probs * (dattn_probs - jnp.sum(attn_probs * dattn_probs, -1, keepdims=True))
    dscore_low = dscores.astype(jnp.bfloat16)
    root_dim = math.sqrt(D // HEADS)
    dquery = (
        jnp.einsum(
            "bhlm,bmhe->blhe", dscore_low, split_heads[:, :, 1], preferred_element_type=jnp.float32
        )
        / root_dim
    )
    dkey_vals = (
        jnp.einsum(
            "bhlm,blhe->bmhe", dscore_low, split_heads[:, :, 0], preferred_element_type=jnp.float32
        )
        / root_dim
    )
    dpacked = (
        jnp.stack([dquery, dkey_vals, dvalues], 2)
        .reshape(batch, length, 3 * D)
        .astype(jnp.bfloat16)
    )
    return (dpacked, jnp.sum(dscores, 0))


def to_rows(spread, videos):
    slots, pix_dev, width = spread.shape
    return (
        spread.reshape(videos, slots // videos, pix_dev, width)
        .transpose(0, 2, 1, 3)
        .reshape(videos * pix_dev, slots // videos, width)
    )


def from_rows(rows, videos):
    count_rows, length, width = rows.shape
    pix_dev = count_rows // videos
    return (
        rows.reshape(videos, pix_dev, length, width)
        .transpose(0, 2, 1, 3)
        .reshape(videos * length, pix_dev, width)
    )


def mixer_fwd(hidden, gain_vec, w_in, w_out, context):
    normed, inverse = norm_fwd(hidden, gain_vec)
    normed_low = normed.astype(jnp.bfloat16)
    packed = jnp.dot(normed_low, w_in, preferred_element_type=jnp.float32).astype(jnp.bfloat16)
    if context is None:
        return (
            hidden
            + jnp.dot(attend_fwd(packed, 0.0, None), w_out, preferred_element_type=jnp.float32),
            (normed_low, inverse, packed, None),
        )
    videos, bias_mat, valid_rows, onehot = context
    spread = lax.all_to_all(packed, "frame", split_axis=1, concat_axis=0, tiled=True)
    mixture = from_rows(attend_fwd(to_rows(spread, videos), bias_mat, valid_rows), videos)
    gathered_back = lax.all_to_all(mixture, "frame", split_axis=0, concat_axis=1, tiled=True)
    return (
        hidden + jnp.dot(gathered_back, w_out, preferred_element_type=jnp.float32),
        (normed_low, inverse, packed, spread),
    )


def mixer_bwd(hidden, upstream, gain_vec, w_in, w_out, context, saved):
    normed_low, inverse, packed, kept_pixels = saved
    grad_low = upstream.astype(jnp.bfloat16)
    dtable_sum = None
    if context is None:
        inputs, grads_out, bias_mat, valid_rows = (packed, grad_low, 0.0, None)
    else:
        videos, bias_mat, valid_rows, onehot = context
        spread, grad_spread = (
            lax.all_to_all(packed, "frame", split_axis=1, concat_axis=0, tiled=True),
            lax.all_to_all(grad_low, "frame", split_axis=1, concat_axis=0, tiled=True),
        )
        inputs, grads_out = (to_rows(spread, videos), to_rows(grad_spread, videos))
    mixture = attend_fwd(inputs, bias_mat, valid_rows)
    dw_out = jnp.einsum("bld,ble->de", mixture, grads_out, preferred_element_type=jnp.float32)
    dmixture = jnp.einsum(
        "ble,de->bld", grads_out, w_out, preferred_element_type=jnp.float32
    ).astype(jnp.bfloat16)
    dpacked, dbias_sum = attend_bwd(inputs, dmixture, bias_mat, valid_rows)
    if context is not None:
        dpacked = lax.all_to_all(
            from_rows(dpacked, videos), "frame", split_axis=0, concat_axis=1, tiled=True
        )
        dtable_sum = jnp.einsum("hlm,lmk->hk", dbias_sum, onehot, precision=HIGH)
    dw_in = jnp.einsum("fpd,fpk->dk", normed_low, dpacked, preferred_element_type=jnp.float32)
    dnormed = jnp.einsum("fpk,dk->fpd", dpacked, w_in, preferred_element_type=jnp.float32)
    dhidden, dgain_vec = norm_bwd(hidden, inverse, gain_vec, dnormed)
    return (upstream + dhidden, dw_in, dw_out, dgain_vec, dtable_sum)


def fetch(conv_weight, proj_in, proj_out, time_weight):
    columns = (
        lax.all_gather(conv_weight.astype(jnp.bfloat16), "batch", axis=1, tiled=True),
        lax.all_gather(proj_in.astype(jnp.bfloat16), "batch", axis=1, tiled=True),
        lax.all_gather(proj_out.astype(jnp.bfloat16), "batch", axis=1, tiled=True),
        lax.all_gather(time_weight.astype(jnp.bfloat16), "batch", axis=1, tiled=True),
    )
    return (
        lax.all_gather(columns[0], "frame", axis=0, tiled=True),
        lax.all_gather(columns[1], "frame", axis=0, tiled=True),
        lax.all_gather(columns[2], "frame", axis=0, tiled=True),
        lax.all_gather(columns[3], "frame", axis=0, tiled=True),
    )


def reduce_rows(matrix_grads):
    row_parts = (
        lax.psum_scatter(matrix_grads[0], "frame", scatter_dimension=0, tiled=True),
        lax.psum_scatter(matrix_grads[1], "frame", scatter_dimension=0, tiled=True),
        lax.psum_scatter(matrix_grads[2], "frame", scatter_dimension=0, tiled=True),
        lax.psum_scatter(matrix_grads[3], "frame", scatter_dimension=0, tiled=True),
    )
    return (
        lax.psum_scatter(row_parts[0], "batch", scatter_dimension=1, tiled=True),
        lax.psum_scatter(row_parts[1], "batch", scatter_dimension=1, tiled=True),
        lax.psum_scatter(row_parts[2], "batch", scatter_dimension=1, tiled=True),
        lax.psum_scatter(row_parts[3], "batch", scatter_dimension=1, tiled=True),
    )


def adamw(weight, moment_one, moment_two, grad, clip_scale, step_rate):
    grad = grad * clip_scale
    moment_one = BETA_ONE * moment_one + (1.0 - BETA_ONE) * grad
    moment_two = BETA_TWO * moment_two + (1.0 - BETA_TWO) * grad * grad
    update = (
        moment_one
        / (1.0 - BETA_ONE**STEP)
        / (jnp.sqrt(moment_two / (1.0 - BETA_TWO**STEP)) + ADAM_EPS)
    )
    return (weight - step_rate * (update + DECAY * weight), moment_one, moment_two)


ROW_CONV = 576
ROW_GRAD = 704
ROW_ALL = 736
HALF = 352
PAIRS = 4
GAP = 272
NEVER = -1e30
MESH_ID = pl.DeviceIdType.MESH


def dot_nn(lhs, rhs):
    return jnp.dot(lhs, rhs, preferred_element_type=jnp.float32)


def dot_nt(lhs, rhs):
    return lax.dot_general(lhs, rhs, (((1,), (1,)), ((), ())), preferred_element_type=jnp.float32)


def dot_tn(lhs, rhs):
    return lax.dot_general(lhs, rhs, (((0,), (0,)), ((), ())), preferred_element_type=jnp.float32)


def low(values):
    return values.astype(jnp.bfloat16)


def rms(values, gain_row):
    inverse = lax.rsqrt(jnp.mean(values * values, -1, keepdims=True) + EPS_NORM)
    return values * inverse * gain_row, inverse


def rms_back(values, inverse, gain_row, upstream):
    scaled = upstream * gain_row
    unit = values * inverse
    mean = jnp.mean(unit * scaled, -1, keepdims=True)
    return inverse * (scaled - unit * mean), jnp.sum(upstream * unit, 0, keepdims=True)


def weave(block):
    first = block[:256].reshape(32, 1, 8, D)
    second = block[256:].reshape(32, 1, 8, D)
    return jnp.concatenate([first, second], 1).reshape(512, D)


def unweave(block):
    parts = block.reshape(32, 2, 8, D)
    return jnp.concatenate([parts[:, 0].reshape(256, D), parts[:, 1].reshape(256, D)], 0)


def tap_pieces(tap):
    start, stop = 256 * tap, 256 * tap + 256
    pieces = []
    while start < stop:
        block, offset = divmod(start, ROW_CONV)
        size = min(ROW_CONV - offset, stop - start)
        pieces.append((block // 2, block % 2, offset, size))
        start += size
    return pieces


def step_kernel(
    packed_ref,
    clip_ref,
    embed_ref,
    table_ref,
    gains_ref,
    win_ref,
    wout_ref,
    headpad_ref,
    scal_ref,
    grads_ref,
    vector_ref,
    squares_ref,
    wall,
    dslab,
    proj,
    outp,
    mine,
    hid_one,
    hid_two,
    inner_zero,
    dhid,
    pack_zero,
    mix_zero,
    spread_norm,
    pack_one,
    prob_one,
    mix_one,
    mix_back,
    dout_pix,
    dnorm_back,
    stage,
    bias_acc,
    shift_fwd,
    shift_one,
    shift_two,
    act_one,
    act_two,
    acc_out,
    red_sib,
    red_a,
    red_b,
    red_c,
    red_d,
    red_z,
    part_z,
    final,
    vec_acc,
    vec_recv,
    sq_acc,
    sq_recv,
    sem_sib,
    sem_z,
    sem_x,
    sem_y,
    sem_xf,
    sem_yf,
    sem_n,
    sem_m,
    sem_dy,
    sem_dn,
    sem_red,
    sem_fin,
    sem_vec,
    sem_sq,
):
    fr = lax.axis_index("frame")
    ba = lax.axis_index("batch")
    z, x = fr // 2, fr % 2
    y, c = ba // 2, ba % 2
    ox, oy, oc = 1 - x, 1 - y, 1 - c
    quarter = 2 * x + c
    sibling = (fr, 2 * y + oc)
    x_peer = (2 * z + ox, ba)
    y_peer = (fr, 2 * oy + c)
    xs_peer = (2 * z + ox, 2 * y + oc)
    z_ids = [(z + k) % 4 for k in (1, 2, 3)]
    z_peers = [(2 * k + x, ba) for k in z_ids]
    group = [(sibling, 2 * x + oc), (x_peer, 2 * ox + c), (xs_peer, 2 * ox + oc)]

    def remote(src, dst, sems, send_at, recv_at, device):
        return pltpu.make_async_remote_copy(
            src_ref=src,
            dst_ref=dst,
            send_sem=sems.at[(0,) + send_at],
            recv_sem=sems.at[(1,) + recv_at],
            device_id=device,
            device_id_type=MESH_ID,
        )

    barrier = pltpu.get_barrier_semaphore()
    everyone = [sibling, x_peer, y_peer, xs_peer] + z_peers
    for peer in everyone:
        pl.semaphore_signal(barrier, inc=1, device_id=peer, device_id_type=MESH_ID)
    pl.semaphore_wait(barrier, len(everyone))

    first = remote(packed_ref.at[oc], mine, sem_vec, (0,), (0,), sibling)
    first.start()
    zeros_row = jnp.zeros((3, 16, D), jnp.bfloat16)
    for frame in range(9):
        shift_one[:, GAP * frame : GAP * frame + 16, :] = zeros_row
        shift_two[:, GAP * frame : GAP * frame + 16, :] = zeros_row
    for frame in range(3):
        shift_fwd[:, GAP * frame : GAP * frame + 16, :] = zeros_row
    bias_acc[...] = jnp.zeros_like(bias_acc)
    vec_acc[...] = jnp.zeros_like(vec_acc)
    acc_out[...] = jnp.zeros_like(acc_out)
    first.wait()
    wall[y, fr, c] = packed_ref[c] + mine[...]

    own = wall.at[y, fr, c]
    sends = []

    def go(copy):
        copy.start()
        sends.append(copy)

    def arrive(dst, sems, at):
        remote(dst, dst, sems, at, at, sibling).wait_recv()

    def to_sibling(row_z, row_x, row_y):
        block = wall.at[row_y, 2 * row_z + row_x, c]
        at = (row_z, row_x, row_y)
        go(remote(block, block, sem_sib, at, at, sibling))

    lo, hi = pl.ds(0, 368), pl.ds(368, 368)
    for k, peer in enumerate(z_peers):
        go(remote(own, own, sem_z, (k,), (2 - k,), peer))
    go(remote(own, own, sem_x, (z,), (z,), x_peer))
    go(remote(own, own, sem_y, (z,), (z,), y_peer))
    to_sibling(z, x, y)
    for k, row_z in enumerate(z_ids):
        block = wall.at[y, 2 * row_z + x, c]
        arrive(block, sem_z, (k,))
        go(remote(block, block, sem_x, (row_z,), (row_z,), x_peer))
        go(remote(block, block, sem_y, (row_z,), (row_z,), y_peer))
        to_sibling(row_z, x, y)
    for row_z in [z] + z_ids:
        block = wall.at[y, 2 * row_z + ox, c]
        arrive(block, sem_x, (row_z,))
        part = wall.at[y, 2 * row_z + ox, c, lo]
        go(remote(part, part, sem_yf, (row_z,), (row_z,), y_peer))
        to_sibling(row_z, ox, y)
        block = wall.at[oy, 2 * row_z + x, c]
        arrive(block, sem_y, (row_z,))
        part = wall.at[oy, 2 * row_z + x, c, hi]
        go(remote(part, part, sem_xf, (row_z,), (row_z,), x_peer))
        to_sibling(row_z, x, oy)
    for row_z in [z] + z_ids:
        arrive(wall.at[oy, 2 * row_z + ox, c, lo], sem_yf, (row_z,))
        arrive(wall.at[oy, 2 * row_z + ox, c, hi], sem_xf, (row_z,))
        to_sibling(row_z, ox, oy)
    for row_z in range(4):
        for row_x in range(2):
            for row_y in range(2):
                arrive(
                    wall.at[row_y, 2 * row_z + row_x, oc], sem_sib, (row_z, row_x, row_y)
                )
    for copy in sends:
        copy.wait_send()

    for row_y in range(2):
        for row in range(8):
            for half in range(2):
                block = wall.at[row_y, row, half]
                rows = slice(64 * (row % 4) + 32 * half, 64 * (row % 4) + 32 * half + 32)
                for j in range(3):
                    cols = slice(384 * row_y + 128 * j, 384 * row_y + 128 * j + 128)
                    proj[row // 4, rows, cols] = block[ROW_CONV + 32 * j : ROW_CONV + 32 * j + 32]
                outp[row // 4, rows, 128 * row_y : 128 * row_y + 128] = block[672:704]

    def time_tile(layer):
        rows = []
        for row in range(4 * layer, 4 * layer + 4):
            for half in range(2):
                rows.append(
                    jnp.concatenate(
                        [wall[0, row, half, 704:736, :], wall[1, row, half, 704:736, :]], 1
                    )
                )
        return jnp.concatenate(rows, 0)

    def conv_tile(kernel, tap):
        rows = []
        for row, half, offset, size in tap_pieces(tap):
            block = (2 * kernel + row, half)
            rows.append(
                jnp.concatenate(
                    [
                        wall[(0,) + block + (slice(offset, offset + size),)],
                        wall[(1,) + block + (slice(offset, offset + size),)],
                    ],
                    1,
                )
            )
        return rows[0] if len(rows) == 1 else jnp.concatenate(rows, 0)

    embed = embed_ref[...]
    time_pre = [dot_nn(embed, time_tile(layer))[0:1] for layer in range(2)]
    time_bias = [pre * jax.nn.sigmoid(pre) for pre in time_pre]
    gain = [gains_ref[k : k + 1, :] for k in range(7)]
    column = lax.broadcasted_iota(jnp.int32, (1, D), 1)
    heads = [
        jnp.where(column // 64 == h, 1.0, 0.0).astype(jnp.bfloat16) for h in range(HEADS)
    ]
    pixel_x = lax.broadcasted_iota(jnp.int32, (256, 1), 0) % SIDE
    not_left = jnp.where(pixel_x != 0, 1.0, 0.0)
    not_right = jnp.where(pixel_x != SIDE - 1, 1.0, 0.0)

    def put_shifts(dst, bases, values):
        for k, base in enumerate(bases):
            frame = values[256 * k : 256 * k + 256]
            rows = pl.ds(base, 256)
            dst[0, rows, :] = low(pltpu.roll(frame, 1, 0) * not_left)
            dst[1, rows, :] = low(frame)
            dst[2, rows, :] = low(pltpu.roll(frame, 255, 0) * not_right)

    def aligned(value, multiple):
        return value if isinstance(value, int) else pl.multiple_of(value, multiple)

    def shifted(src, bases, dy, dx):
        return jnp.concatenate(
            [src[dx, pl.ds(aligned(base + 16 * (dy - 1), 16), 256), :] for base in bases], 0
        )

    def conv(src, bases, kernel):
        total = None
        for tap in range(9):
            part = dot_nn(shifted(src, bases, tap // 3, tap % 3), conv_tile(kernel, tap))
            total = part if total is None else total + part
        return total

    def conv_back(src, bases, kernel):
        total = None
        for tap in range(9):
            part = dot_nt(shifted(src, bases, 2 - tap // 3, 2 - tap % 3), conv_tile(kernel, tap))
            total = part if total is None else total + part
        return total

    def conv_grad(act, src, kernel, dst, first_row):
        for tap in range(9):
            grads = shifted(src, [16 + GAP * k for k in range(8)], 2 - tap // 3, 2 - tap % 3)
            total = low(dot_nn(act[...], grads))
            start = 0
            for row, half, offset, size in tap_pieces(tap):
                for row_y in range(2):
                    dst[row_y, first_row + row, half, offset : offset + size] = total[
                        start : start + size, 128 * row_y : 128 * row_y + 128
                    ]
                start += size

    def put_proj_grad(layer, din, dout, dst, first_row):
        for row in range(4):
            for half in range(2):
                rows = slice(64 * row + 32 * half, 64 * row + 32 * half + 32)
                for row_y in range(2):
                    for j in range(3):
                        cols = slice(384 * row_y + 128 * j, 384 * row_y + 128 * j + 128)
                        dst[
                            row_y,
                            first_row + row,
                            half,
                            ROW_CONV + 32 * j : ROW_CONV + 32 * j + 32,
                        ] = din[rows, cols]
                    dst[row_y, first_row + row, half, 672:704] = dout[
                        rows, 128 * row_y : 128 * row_y + 128
                    ]

    def softmax(scores):
        powers = jnp.exp(scores - jnp.max(scores, -1, keepdims=True))
        return low(powers * (1.0 / jnp.sum(powers, -1, keepdims=True)))

    def attend(query, key, value, bias):
        probs = []
        for h in range(HEADS):
            scores = dot_nt(query * heads[h], key) * 0.125
            if bias is not None:
                scores = scores + bias[h]
            probs.append(softmax(scores))
        values = jnp.concatenate([value * heads[h] for h in range(HEADS)], 0)
        return low(dot_nn(jnp.concatenate(probs, 1), values)), probs

    def attend_back(query, key, value, dmix, probs, add_bias):
        dmix_t, query_t = dmix.T, query.T
        dscores, dkey_t, dvalue_t = [], [], []
        for h in range(HEADS):
            prob_low = probs(h)
            prob = prob_low.astype(jnp.float32)
            dprob = dot_nt(dmix * heads[h], value)
            dscore = prob * (dprob - jnp.sum(prob * dprob, -1, keepdims=True))
            if add_bias is not None:
                add_bias(h, dscore)
            dscore_low = low(dscore)
            dscores.append(dscore_low)
            rows = slice(64 * h, 64 * h + 64)
            dvalue_t.append(dot_nn(dmix_t[rows], prob_low))
            dkey_t.append(dot_nn(query_t[rows], dscore_low))
        keys = jnp.concatenate([key * heads[h] for h in range(HEADS)], 0)
        dquery = low(dot_nn(jnp.concatenate(dscores, 1), keys) * 0.125)
        dkey = low(jnp.concatenate(dkey_t, 0) * 0.125).T
        dvalue = low(jnp.concatenate(dvalue_t, 0)).T
        return jnp.concatenate([dquery, dkey, dvalue], 1)

    def add_row(row, value):
        vec_acc[row : row + 1, :] += value

    def embed_input(rows):
        clip = clip_ref[rows, :]
        total = None
        for channel in range(3):
            part = clip[:, 3 + channel : 4 + channel] * win_ref[channel : channel + 1, :]
            total = part if total is None else total + part
        return total, clip

    fwd_bases = [16, 16 + GAP]

    def pair_rows(pair):
        return pl.ds(pl.multiple_of(pair * 512, 512), 512)

    def pair_bases(pair):
        return [
            pl.multiple_of(16 + GAP * (2 * pair), 16),
            pl.multiple_of(16 + GAP * (2 * pair + 1), 16),
        ]

    def send_pair(pair, dst, sems):
        for k, (peer, part) in enumerate(group):
            remote(
                stage.at[pl.ds(32 * pair + 8 * part, 8)],
                dst.at[:, 4 * quarter + pair],
                sems,
                (pair, k),
                (pair, k),
                peer,
            ).start()
        dst[:, 4 * quarter + pair] = stage[pl.ds(32 * pair + 8 * quarter, 8)]

    def wait_pairs(dst, sems):
        for pair in range(PAIRS):
            for k, (peer, part) in enumerate(group):
                copy = remote(
                    stage.at[pl.ds(32 * pair + 8 * part, 8)],
                    dst.at[:, 4 * part + pair],
                    sems,
                    (pair, k),
                    (pair, k),
                    peer,
                )
                copy.wait_send()
                copy.wait_recv()

    def block_tiles(src, block, part):
        return src.at[pl.ds(16 * block + 4 * part, 4)]

    def send_block(block, src, dst, sems):
        for k, (peer, part) in enumerate(group):
            remote(
                block_tiles(src, block, part),
                dst.at[:, quarter, block],
                sems,
                (block, k),
                (block, k),
                peer,
            ).start()
        dst[:, quarter, block] = block_tiles(src, block, quarter)[...]

    def wait_blocks(src, dst, sems):
        for block in range(8):
            for k, (peer, part) in enumerate(group):
                copy = remote(
                    block_tiles(src, block, part),
                    dst.at[:, part, block],
                    sems,
                    (block, k),
                    (block, k),
                    peer,
                )
                copy.wait_send()
                copy.wait_recv()

    def forward_pair(pair, carry):
        rows = pair_rows(pair)
        hidden, _ = embed_input(rows)
        normed, _ = rms(hidden, gain[0])
        put_shifts(shift_fwd, fwd_bases, normed * jax.nn.sigmoid(normed))
        inner = conv(shift_fwd, fwd_bases, 0) + time_bias[0]
        inner_zero[rows, :] = inner
        normed, _ = rms(inner, gain[1])
        put_shifts(shift_fwd, fwd_bases, normed * jax.nn.sigmoid(normed))
        hidden = hidden + conv(shift_fwd, fwd_bases, 1)
        hid_one[rows, :] = hidden
        normed, _ = rms(hidden, gain[2])
        packed = low(dot_nn(low(normed), proj[0]))
        pack_zero[rows, :] = packed
        mixed = []
        for k in range(2):
            part = packed[256 * k : 256 * k + 256]
            one, _ = attend(part[:, :D], part[:, D : 2 * D], part[:, 2 * D :], None)
            mixed.append(one)
        mixed = jnp.concatenate(mixed, 0)
        mix_zero[rows, :] = mixed
        hidden = hidden + dot_nn(mixed, outp[0])
        hid_two[rows, :] = hidden
        normed, _ = rms(hidden, gain[3])
        stage[pl.ds(32 * pair, 32)] = low(weave(normed)).reshape(32, 16, D)
        send_pair(pair, spread_norm, sem_n)
        return carry

    lax.fori_loop(0, PAIRS, forward_pair, 0)
    wait_pairs(spread_norm, sem_n)

    def temporal_block(block, carry):
        normed = spread_norm[block].reshape(256, D)
        packed = low(dot_nn(normed, proj[1]))
        pack_one[block] = packed
        mixed, probs = attend(
            packed[:, :D],
            packed[:, D : 2 * D],
            packed[:, 2 * D :],
            [table_ref[h] for h in range(HEADS)],
        )
        for h in range(HEADS):
            prob_one[block, h] = probs[h]
        mix_one[pl.ds(16 * block, 16)] = mixed.reshape(16, 16, D)
        send_block(block, mix_one, mix_back, sem_m)
        return carry

    lax.fori_loop(0, 8, temporal_block, 0)
    wait_blocks(mix_one, mix_back, sem_m)

    scale = scal_ref[0]

    def last_pair(pair, carry):
        rows = pair_rows(pair)
        bases = pair_bases(pair)
        lanes = pl.ds(pl.multiple_of(pair * 512, 512), 512)
        hidden = hid_two[rows, :] + unweave(dot_nn(mix_back[pair].reshape(512, D), outp[1]))
        normed, inverse = rms(hidden, gain[4])
        sig = jax.nn.sigmoid(normed)
        acts = normed * sig
        put_shifts(shift_fwd, fwd_bases, acts)
        act_one[:, lanes] = low(acts).T
        slope_one = sig * (1.0 + normed * (1.0 - sig))
        inner = conv(shift_fwd, fwd_bases, 2) + time_bias[1]
        normed_two, inverse_two = rms(inner, gain[5])
        sig_two = jax.nn.sigmoid(normed_two)
        acts_two = normed_two * sig_two
        put_shifts(shift_fwd, fwd_bases, acts_two)
        act_two[:, lanes] = low(acts_two).T
        slope_two = sig_two * (1.0 + normed_two * (1.0 - sig_two))
        last = hidden + conv(shift_fwd, fwd_bases, 3)
        normed, inverse_six = rms(last, gain[6])
        normed_low = low(normed)
        pred = dot_nt(normed_low, headpad_ref[...])
        clip = clip_ref[rows, :]
        valid = jnp.concatenate(
            [
                jnp.full((256, 128), scal_ref[1 + 2 * pair], jnp.float32),
                jnp.full((256, 128), scal_ref[2 + 2 * pair], jnp.float32),
            ],
            0,
        )
        lane = lax.broadcasted_iota(jnp.int32, (512, 128), 1)
        error = jnp.where(lane < 3, pred - clip, 0.0)
        weighted = error * valid
        vec_acc[7:8, 0:128] += jnp.sum(weighted * error, 0, keepdims=True)
        dpred = weighted * scale
        dpred_hi = low(dpred)
        dpred_lo = low(dpred - dpred_hi.astype(jnp.float32))
        acc_out[...] += dot_tn(dpred_hi, normed_low) + dot_tn(dpred_lo, normed_low)
        dnormed = None
        for channel in range(3):
            part = dpred[:, channel : channel + 1] * wout_ref[channel : channel + 1, :]
            dnormed = part if dnormed is None else dnormed + part
        dlast, dgain = rms_back(last, inverse_six, gain[6], dnormed)
        add_row(6, dgain)
        put_shifts(shift_two, bases, low(dlast).astype(jnp.float32))
        dnormed = conv_back(shift_two, bases, 3) * slope_two
        dinner, dgain = rms_back(inner, inverse_two, gain[5], dnormed)
        add_row(5, dgain)
        add_row(15, jnp.sum(dinner, 0, keepdims=True))
        put_shifts(shift_one, bases, low(dinner).astype(jnp.float32))
        dnormed = conv_back(shift_one, bases, 2) * slope_one
        dhidden, dgain = rms_back(hidden, inverse, gain[4], dnormed)
        add_row(4, dgain)
        dhidden = dhidden + dlast
        dhid[rows, :] = dhidden
        stage[pl.ds(32 * pair, 32)] = low(weave(dhidden)).reshape(32, 16, D)
        send_pair(pair, dout_pix, sem_dy)
        return carry

    lax.fori_loop(0, PAIRS, last_pair, 0)
    conv_grad(act_two, shift_two, 3, wall, 6)
    conv_grad(act_one, shift_one, 2, wall, 4)
    wait_pairs(dout_pix, sem_dy)

    def temporal_back(block, carry):
        dout = dout_pix[block].reshape(256, D)
        dmix = low(dot_nt(dout, outp[1]))
        packed = pack_one[block]

        def add_bias(h, dscore):
            bias_acc[h] += dscore

        dpacked = attend_back(
            packed[:, :D],
            packed[:, D : 2 * D],
            packed[:, 2 * D :],
            dmix,
            lambda h: prob_one[block, h],
            add_bias,
        )
        pack_one[block] = dpacked
        stage[pl.ds(16 * block, 16)] = low(dot_nt(dpacked, proj[1])).reshape(16, 16, D)
        send_block(block, stage, dnorm_back, sem_dn)
        return carry

    lax.fori_loop(0, 8, temporal_back, 0)
    flat = (2048, D)
    dout_one = low(dot_tn(mix_one[...].reshape(flat), dout_pix[...].reshape(flat)))
    din_one = low(dot_tn(spread_norm[...].reshape(flat), pack_one[...].reshape(2048, 3 * D)))
    put_proj_grad(1, din_one, dout_one, wall, 4)
    wait_blocks(stage, dnorm_back, sem_dn)

    def slab(k):
        return (wall, 2 * k) if k >= 2 else (dslab, 2 * k)

    top, low_half = pl.ds(0, HALF), pl.ds(HALF, HALF)

    def red_one(k):
        src, row = slab(k)
        return remote(
            src.at[:, pl.ds(row, 2), oc, pl.ds(0, ROW_GRAD)], red_sib.at[k], sem_red, (k, 0), (k, 0), sibling
        )

    def red_two(k):
        src, row = slab(k)
        return (
            remote(src.at[:, row + ox, c, top], red_a.at[k], sem_red, (k, 1), (k, 1), x_peer),
            remote(src.at[oy, pl.ds(row, 2), c, low_half], red_b.at[k], sem_red, (k, 2), (k, 2), y_peer),
        )

    def red_three(k):
        src, row = slab(k)
        return (
            remote(src.at[oy, row + x, c, top], red_c.at[k], sem_red, (k, 3), (k, 3), y_peer),
            remote(src.at[y, row + ox, c, low_half], red_d.at[k], sem_red, (k, 4), (k, 4), x_peer),
        )

    def both(left, right):
        return low(left.astype(jnp.float32) + right.astype(jnp.float32))

    def finish(copies):
        for copy in copies:
            copy.wait_send()
            copy.wait_recv()

    def add_one(k):
        src, row = slab(k)
        for row_y in range(2):
            for row_x in range(2):
                src[row_y, row + row_x, c, 0:ROW_GRAD] = both(
                    src[row_y, row + row_x, c, 0:ROW_GRAD], red_sib[k, row_y, row_x]
                )

    def add_two(k):
        src, row = slab(k)
        for part in range(2):
            src[part, row + x, c, 0:HALF] = both(src[part, row + x, c, 0:HALF], red_a[k, part])
            src[y, row + part, c, HALF:ROW_GRAD] = both(
                src[y, row + part, c, HALF:ROW_GRAD], red_b[k, part]
            )

    def add_three(k):
        src, row = slab(k)
        part_z[k, 0:HALF] = both(src[y, row + x, c, 0:HALF], red_c[k])
        part_z[k, HALF:ROW_GRAD] = both(src[y, row + x, c, HALF:ROW_GRAD], red_d[k])

    def start_all(copies):
        for copy in copies:
            copy.start()

    def spatial_back(pair, carry):
        rows = pair_rows(pair)
        bases = pair_bases(pair)
        lanes = pl.ds(pl.multiple_of(pair * 512, 512), 512)
        dnormed = unweave(dnorm_back[pair].reshape(512, D).astype(jnp.float32))
        hidden = hid_two[rows, :]
        _, inverse = rms(hidden, gain[3])
        dhidden, dgain = rms_back(hidden, inverse, gain[3], dnormed)
        add_row(3, dgain)
        dhidden = dhidden + dhid[rows, :]
        grad_low = low(dhidden)
        dout_pix[pl.ds(2 * pair, 2)] = grad_low.reshape(2, 16, 16, D)
        dmix = low(dot_nt(grad_low, outp[0]))
        packed = pack_zero[rows, :]
        dpacked = []
        for k in range(2):
            part = packed[256 * k : 256 * k + 256]
            query, key, value = part[:, :D], part[:, D : 2 * D], part[:, 2 * D :]

            def again(h):
                return softmax(dot_nt(query * heads[h], key) * 0.125)

            dpacked.append(
                attend_back(query, key, value, dmix[256 * k : 256 * k + 256], again, None)
            )
        dpacked = jnp.concatenate(dpacked, 0)
        pack_zero[rows, :] = dpacked
        hidden = hid_one[rows, :]
        normed, inverse = rms(hidden, gain[2])
        spread_norm[pl.ds(2 * pair, 2)] = low(normed).reshape(2, 16, 16, D)
        dnormed = dot_nt(dpacked, proj[0])
        dprev, dgain = rms_back(hidden, inverse, gain[2], dnormed)
        add_row(2, dgain)
        dhidden = dhidden + dprev
        dhid[rows, :] = dhidden
        put_shifts(shift_two, bases, low(dhidden).astype(jnp.float32))
        normed, _ = rms(inner_zero[rows, :], gain[1])
        act_two[:, lanes] = low(normed * jax.nn.sigmoid(normed)).T
        return carry

    start_all([red_one(3), red_one(2)])
    lax.fori_loop(0, PAIRS, spatial_back, 0)
    for k in (3, 2):
        finish([red_one(k)])
        add_one(k)
        start_all(red_two(k))
    din_zero = low(dot_tn(spread_norm[...].reshape(flat), pack_zero[...]))
    dout_zero = low(dot_tn(mix_zero[...], dout_pix[...].reshape(flat)))
    put_proj_grad(0, din_zero, dout_zero, dslab, 0)
    conv_grad(act_two, shift_two, 1, dslab, 2)
    start_all([red_one(1)])
    for k in (3, 2):
        finish(red_two(k))
        add_two(k)
        start_all(red_three(k))

    def first_back(pair, carry):
        rows = pair_rows(pair)
        bases = pair_bases(pair)
        lanes = pl.ds(pl.multiple_of(pair * 512, 512), 512)
        inner = inner_zero[rows, :]
        normed, inverse = rms(inner, gain[1])
        sig = jax.nn.sigmoid(normed)
        dnormed = conv_back(shift_two, bases, 1) * (sig * (1.0 + normed * (1.0 - sig)))
        dinner, dgain = rms_back(inner, inverse, gain[1], dnormed)
        add_row(1, dgain)
        add_row(14, jnp.sum(dinner, 0, keepdims=True))
        put_shifts(shift_one, bases, low(dinner).astype(jnp.float32))
        hidden, _ = embed_input(rows)
        normed, _ = rms(hidden, gain[0])
        act_one[:, lanes] = low(normed * jax.nn.sigmoid(normed)).T
        return carry

    lax.fori_loop(0, PAIRS, first_back, 0)
    conv_grad(act_one, shift_one, 0, dslab, 0)
    start_all([red_one(0)])
    for k in (3, 2):
        finish(red_three(k))
        add_three(k)
    finish([red_one(1)])
    add_one(1)
    start_all(red_two(1))

    def input_back(pair, carry):
        rows = pair_rows(pair)
        bases = pair_bases(pair)
        hidden, clip = embed_input(rows)
        normed, inverse = rms(hidden, gain[0])
        sig = jax.nn.sigmoid(normed)
        dnormed = conv_back(shift_one, bases, 0) * (sig * (1.0 + normed * (1.0 - sig)))
        dhidden, dgain = rms_back(hidden, inverse, gain[0], dnormed)
        add_row(0, dgain)
        dhidden = dhidden + dhid[rows, :]
        for channel in range(3):
            add_row(
                8 + channel,
                jnp.sum(clip[:, 3 + channel : 4 + channel] * dhidden, 0, keepdims=True),
            )
        return carry

    lax.fori_loop(0, PAIRS, input_back, 0)
    finish(red_two(1))
    add_two(1)
    start_all(red_three(1))
    finish([red_one(0)])
    add_one(0)
    start_all(red_two(0))

    vec_acc[11:14, :] = acc_out[0:3, :]
    place = 4 * (z // 2) + 2 * y + z % 2
    fold = lax.broadcasted_iota(jnp.int32, (256, 128), 0) // 8
    fold_lane = lax.broadcasted_iota(jnp.int32, (256, 128), 1)
    left = jnp.where(fold == fold_lane, 1.0, 0.0)
    table = None
    for h in range(HEADS):
        right = jnp.where(fold + 32 * h == fold_lane, 1.0, 0.0)
        wide = lax.dot_general(
            bias_acc[h], right, (((1,), (0,)), ((), ())), precision=HIGH, preferred_element_type=jnp.float32
        )
        part = lax.dot_general(
            left, wide, (((0,), (0,)), ((), ())), precision=HIGH, preferred_element_type=jnp.float32
        )
        table = part if table is None else table + part
    vec_acc[32:64, 0:128] = table[0:32]
    row_ids = lax.broadcasted_iota(jnp.int32, (16, D), 0)
    slots = jnp.zeros((16, D), jnp.float32)
    for layer in range(2):
        pre = time_pre[layer]
        sig = jax.nn.sigmoid(pre)
        dpre = vec_acc[14 + layer : 15 + layer, :] * (sig * (1.0 + pre * (1.0 - sig)))
        slots = jnp.where(row_ids == 2 * place + layer, dpre, slots)
    vec_acc[16:32, :] = slots

    def total_step(values, received, sems, index, peers):
        copies = [
            remote(values, received.at[index + r], sems, (1 + index + k,), (1 + index + r,), peer)
            for k, r, peer in peers
        ]
        start_all(copies)
        finish(copies)

    def total_pair(values, received, sems, index, peer):
        total_step(values, received, sems, index, [(0, 0, peer)])
        values[...] += received[index]

    def total_z(values, received, sems):
        peers = [(k, 2 - k, peer) for k, peer in enumerate(z_peers)]
        total_step(values, received, sems, 3, peers)
        return (values[...] + received[4]) + (received[3] + received[5])

    total_pair(vec_acc, vec_recv, sem_vec, 0, sibling)
    finish(red_three(1))
    add_three(1)
    finish(red_two(0))
    add_two(0)
    start_all(red_three(0))
    total_pair(vec_acc, vec_recv, sem_vec, 1, x_peer)
    total_pair(vec_acc, vec_recv, sem_vec, 2, y_peer)
    finish(red_three(0))
    add_three(0)
    z_copies = [
        remote(part_z.at[z_ids[k]], red_z.at[2 - k], sem_fin, (k,), (2 - k,), peer)
        for k, peer in enumerate(z_peers)
    ]
    start_all(z_copies)
    vector_ref[...] = total_z(vec_acc, vec_recv, sem_vec)
    finish(z_copies)
    total = part_z[z].astype(jnp.float32)
    for k in range(3):
        total = total + red_z[k].astype(jnp.float32)
    final[c] = total
    own_sums = remote(final.at[c], final.at[c], sem_fin, (3,), (3,), sibling)
    own_sums.start()
    square = jnp.sum(jnp.sum(total * total, 0, keepdims=True), 1, keepdims=True)
    sq_acc[...] = jnp.broadcast_to(square, (8, 128))
    grads_ref[c] = total
    total_pair(sq_acc, sq_recv, sem_sq, 0, sibling)
    total_pair(sq_acc, sq_recv, sem_sq, 1, x_peer)
    total_pair(sq_acc, sq_recv, sem_sq, 2, y_peer)
    squares_ref[...] = total_z(sq_acc, sq_recv, sem_sq)
    own_sums.wait_send()
    arrive(final.at[oc], sem_fin, (3,))
    grads_ref[oc] = final[oc]


def lane_place(block, c):
    wide = jnp.concatenate([block, block], -1)
    lane = lax.broadcasted_iota(jnp.int32, wide.shape, wide.ndim - 1)
    return jnp.where(lane // 64 == c, wide, jnp.zeros_like(wide))


def shards_pairs(
    clean,
    noise,
    timesteps,
    frame_counts,
    conv_weight,
    conv_first,
    conv_second,
    proj_in,
    proj_in_first,
    proj_in_second,
    proj_out,
    proj_out_first,
    proj_out_second,
    time_weight,
    time_first,
    time_second,
    in_weight,
    in_first,
    in_second,
    out_weight,
    out_first,
    out_second,
    gains,
    gains_first,
    gains_second,
    rel_bias,
    rel_bias_first,
    rel_bias_second,
):

    pixels = clean.shape[4]
    fr = lax.axis_index("frame")
    ba = lax.axis_index("batch")
    z, x = fr // 2, fr % 2
    y, c = ba // 2, ba % 2
    both = jnp.concatenate([clean[:, 0], noise[:, 0]], 2)
    moved = []
    for turn in range(2):
        pairs = []
        for sz in range(4):
            for sx in range(2):
                for sb in range(4):
                    micro = sx if turn == 0 else 1 - sx
                    dz, dx = 2 * micro + sb % 2, sz // 2
                    dst = (2 * dz + dx) * 4 + 2 * (sb // 2) + sz % 2
                    pairs.append(((2 * sz + sx) * 4 + sb, dst))
        piece = jnp.where((x == 0) == (turn == 0), both[0], both[1])
        moved.append(lax.ppermute(piece, ("frame", "batch"), pairs))
    frames = jnp.where(
        z < 2, jnp.concatenate(moved, 0), jnp.concatenate([moved[1], moved[0]], 0)
    )
    video = (z // 2) * 4 + 2 * y + z % 2
    all_levels = timesteps.reshape(-1).astype(jnp.float32)
    level = all_levels[video]
    count = frame_counts.reshape(-1)[video]
    pixel_total = jnp.sum(frame_counts).astype(jnp.float32) * pixels
    alpha_bar = jnp.cos(0.5 * math.pi * (level + 1.0) / (TSTEPS + 1.0)) ** 2
    noisy = jnp.sqrt(alpha_bar) * frames[:, :3] + jnp.sqrt(1.0 - alpha_bar) * frames[:, 3:]
    clip = jnp.concatenate([frames[:, 3:], noisy], 1).transpose(0, 2, 1).reshape(-1, 6)
    clip = jnp.pad(clip, ((0, 0), (0, 122)))
    frame_ids = 8 * (2 * x + c) + jnp.arange(8)
    live = (frame_ids < count).astype(jnp.float32)
    scal = jnp.concatenate([(2.0 / pixel_total)[None], live])
    half_width = D // 2
    frequency = jnp.exp(-math.log(10000.0) * jnp.arange(half_width, dtype=jnp.float32) / half_width)
    angles = all_levels[:, None] * frequency
    embedding = jnp.concatenate([jnp.sin(angles), jnp.cos(angles)], -1).astype(jnp.bfloat16)
    embed = jnp.broadcast_to(embedding[video][None], (16, D))
    offsets = jnp.arange(FRAMES)
    distance = offsets[None, :] - offsets[:, None]
    bucket = jnp.minimum(jnp.abs(distance), 15) + 16 * (distance > 0).astype(jnp.int32)
    onehot = (bucket[:, :, None] == jnp.arange(rel_bias.shape[1])[None, None, :]).astype(
        jnp.float32
    )
    bias_mat = jnp.einsum("hk,lmk->hlm", rel_bias, onehot, precision=HIGH)
    place = jnp.arange(256)
    usable = (place[:, None] % 8 == place[None, :] % 8) & (place[None, :] // 8 < count)
    table = jnp.where(usable, jnp.repeat(jnp.repeat(bias_mat, 8, 1), 8, 2), NEVER)
    narrow = jnp.concatenate(
        [
            low(conv_weight).reshape(2, 576, 64),
            low(proj_out).reshape(2, 32, 64),
            low(time_weight).reshape(2, 32, 64),
        ],
        1,
    )
    narrow = lane_place(narrow, c)
    wide = low(proj_in)
    wide = jnp.where(
        c == 0, jnp.pad(wide, ((0, 0), (0, 192))), jnp.pad(wide, ((0, 0), (192, 0)))
    )
    wide = wide.reshape(2, 32, 3, 128).transpose(0, 2, 1, 3).reshape(2, 96, 128)
    packed = jnp.concatenate([narrow[:, :576], wide, narrow[:, 576:]], 1)
    out_low = low(out_weight)
    headpad = jnp.pad(out_low, ((0, 125), (0, 0)))
    win = jnp.pad(in_weight, ((0, 5), (0, 0)))
    wout = jnp.pad(out_low.astype(jnp.float32), ((0, 5), (0, 0)))
    gain_rows = jnp.pad(gains, ((0, 1), (0, 0)))

    bf16, f32 = jnp.bfloat16, jnp.float32
    vmem = pl.BlockSpec(memory_space=pltpu.VMEM)
    smem = pl.BlockSpec(memory_space=pltpu.SMEM)
    scratch = [
        pltpu.VMEM((2, 8, 2, ROW_ALL, 128), bf16),
        pltpu.VMEM((2, 4, 2, ROW_GRAD, 128), bf16),
        pltpu.VMEM((2, D, 3 * D), bf16),
        pltpu.VMEM((2, D, D), bf16),
        pltpu.VMEM((ROW_ALL, 128), bf16),
        pltpu.VMEM((2048, D), f32),
        pltpu.VMEM((2048, D), f32),
        pltpu.VMEM((2048, D), f32),
        pltpu.VMEM((2048, D), f32),
        pltpu.VMEM((2048, 3 * D), bf16),
        pltpu.VMEM((2048, D), bf16),
        pltpu.VMEM((8, 16, 16, D), bf16),
        pltpu.VMEM((8, 256, 3 * D), bf16),
        pltpu.VMEM((8, HEADS, 256, 256), bf16),
        pltpu.VMEM((128, 16, D), bf16),
        pltpu.VMEM((PAIRS, 4, 8, 16, D), bf16),
        pltpu.VMEM((8, 16, 16, D), bf16),
        pltpu.VMEM((PAIRS, 4, 8, 16, D), bf16),
        pltpu.VMEM((128, 16, D), bf16),
        pltpu.VMEM((HEADS, 256, 256), f32),
        pltpu.VMEM((3, 2 * GAP + 16, D), bf16),
        pltpu.VMEM((3, 8 * GAP + 16, D), bf16),
        pltpu.VMEM((3, 8 * GAP + 16, D), bf16),
        pltpu.VMEM((D, 2048), bf16),
        pltpu.VMEM((D, 2048), bf16),
        pltpu.VMEM((128, D), f32),
        pltpu.VMEM((4, 2, 2, ROW_GRAD, 128), bf16),
        pltpu.VMEM((4, 2, HALF, 128), bf16),
        pltpu.VMEM((4, 2, HALF, 128), bf16),
        pltpu.VMEM((4, HALF, 128), bf16),
        pltpu.VMEM((4, HALF, 128), bf16),
        pltpu.VMEM((3, ROW_GRAD, 128), bf16),
        pltpu.VMEM((4, ROW_GRAD, 128), bf16),
        pltpu.VMEM((2, ROW_GRAD, 128), f32),
        pltpu.VMEM((64, D), f32),
        pltpu.VMEM((6, 64, D), f32),
        pltpu.VMEM((8, 128), f32),
        pltpu.VMEM((6, 8, 128), f32),
        pltpu.SemaphoreType.DMA((2, 4, 2, 2)),
        pltpu.SemaphoreType.DMA((2, 3)),
        pltpu.SemaphoreType.DMA((2, 4)),
        pltpu.SemaphoreType.DMA((2, 4)),
        pltpu.SemaphoreType.DMA((2, 4)),
        pltpu.SemaphoreType.DMA((2, 4)),
        pltpu.SemaphoreType.DMA((2, PAIRS, 3)),
        pltpu.SemaphoreType.DMA((2, 8, 3)),
        pltpu.SemaphoreType.DMA((2, PAIRS, 3)),
        pltpu.SemaphoreType.DMA((2, 8, 3)),
        pltpu.SemaphoreType.DMA((2, 4, 5)),
        pltpu.SemaphoreType.DMA((2, 4)),
        pltpu.SemaphoreType.DMA((2, 8)),
        pltpu.SemaphoreType.DMA((2, 8)),
    ]
    sums, vector, squares = pl.pallas_call(
        step_kernel,
        out_shape=(
            jax.ShapeDtypeStruct((2, ROW_GRAD, 128), f32),
            jax.ShapeDtypeStruct((64, D), f32),
            jax.ShapeDtypeStruct((8, 128), f32),
        ),
        in_specs=[vmem] * 8 + [smem],
        out_specs=(vmem, vmem, vmem),
        scratch_shapes=scratch,
        compiler_params=pltpu.CompilerParams(
            collective_id=0, has_side_effects=True, vmem_limit_bytes=64 * 2**20 - 2**16
        ),
        name="train_step",
    )(packed, clip, embed, table, gain_rows, win, wout, headpad, scal)

    conv_sum = lax.dynamic_slice_in_dim(sums[:, :576].reshape(1152, 128), 64 * c, 64, 1)
    pin_sum = sums[:, 576:672].reshape(2, 3, 32, 128).transpose(0, 2, 1, 3).reshape(64, 384)
    pin_sum = lax.dynamic_slice_in_dim(pin_sum, 192 * c, 192, 1)
    pout_sum = lax.dynamic_slice_in_dim(sums[:, 672:704].reshape(64, 128), 64 * c, 64, 1)
    dpre = vector[16:32].reshape(8, 2, D)
    dtime = jnp.einsum("vd,vje->jde", embedding.astype(f32), dpre, precision=HIGH)
    time_square = jnp.sum(dtime * dtime)
    time_sum = lax.dynamic_slice(dtime.reshape(2 * D, D), (64 * fr, 64 * ba), (64, 64))
    loss_sum = jnp.sum(vector[7, :3])
    sum_gains, sum_in, sum_out = vector[0:7], vector[8:11], vector[11:14]
    folded = vector[32:64, :128].reshape(FRAMES, HEADS, FRAMES)
    sum_table = jnp.einsum("lhm,lmk->hk", folded, onehot, precision=HIGH)
    square = (
        squares[0, 0]
        + time_square
        + sum((jnp.sum(grad * grad) for grad in (sum_in, sum_out, sum_gains, sum_table)))
    )
    grad_norm = jnp.sqrt(square)
    clip_scale = CLIP / jnp.maximum(grad_norm, CLIP)
    return (
        loss_sum,
        pixel_total,
        grad_norm,
        *adamw(conv_weight, conv_first, conv_second, conv_sum, clip_scale, RATES[0]),
        *adamw(proj_in, proj_in_first, proj_in_second, pin_sum, clip_scale, RATES[1]),
        *adamw(proj_out, proj_out_first, proj_out_second, pout_sum, clip_scale, RATES[2]),
        *adamw(time_weight, time_first, time_second, time_sum, clip_scale, RATES[3]),
        *adamw(in_weight, in_first, in_second, sum_in, clip_scale, RATES[4]),
        *adamw(out_weight, out_first, out_second, sum_out, clip_scale, RATES[5]),
        *adamw(gains, gains_first, gains_second, sum_gains, clip_scale, RATES[6]),
        *adamw(rel_bias, rel_bias_first, rel_bias_second, sum_table, clip_scale, RATES[7]),
    )


def shards(
    clean,
    noise,
    timesteps,
    frame_counts,
    conv_weight,
    conv_first,
    conv_second,
    proj_in,
    proj_in_first,
    proj_in_second,
    proj_out,
    proj_out_first,
    proj_out_second,
    time_weight,
    time_first,
    time_second,
    in_weight,
    in_first,
    in_second,
    out_weight,
    out_first,
    out_second,
    gains,
    gains_first,
    gains_second,
    rel_bias,
    rel_bias_first,
    rel_bias_second,
):
    fr_dev = clean.shape[2]
    pixels = clean.shape[4]
    videos = timesteps.shape[2]
    pix_dev = pixels // lax.axis_size("frame")
    group_idx = lax.axis_index("batch")
    frame_ids = lax.axis_index("frame") * fr_dev + jnp.arange(fr_dev)
    member = (frame_ids[:, None] // FRAMES == jnp.arange(videos)[None, :]).astype(jnp.float32)
    frame_place = frame_ids % FRAMES
    pixel_total = jnp.sum(frame_counts).astype(jnp.float32) * pixels
    offsets = jnp.arange(FRAMES)
    distance = offsets[None, :] - offsets[:, None]
    bucket = jnp.minimum(jnp.abs(distance), 15) + 16 * (distance > 0).astype(jnp.int32)
    onehot = (bucket[:, :, None] == jnp.arange(rel_bias.shape[1])[None, None, :]).astype(
        jnp.float32
    )
    bias_mat = jnp.einsum("hk,lmk->hlm", rel_bias, onehot, precision=HIGH)
    half_width = D // 2
    frequency = jnp.exp(-math.log(10000.0) * jnp.arange(half_width, dtype=jnp.float32) / half_width)
    out_low = out_weight.astype(jnp.bfloat16)
    matrix_acc = None
    vector_acc = None
    loss_local = jnp.zeros((), jnp.float32)
    for micro_idx in range(MICRO):
        gathered = fetch(conv_weight, proj_in, proj_out, time_weight)
        kernels = gathered[0].reshape(4, 9 * D, D)
        w_in = gathered[1].reshape(2, D, 3 * D)
        w_out = gathered[2].reshape(2, D, D)
        w_time = gathered[3].reshape(2, D, D)
        steps_grp = lax.dynamic_index_in_dim(timesteps[micro_idx], group_idx, 0, keepdims=False)
        count_grp = lax.dynamic_index_in_dim(frame_counts[micro_idx], group_idx, 0, keepdims=False)
        levels = steps_grp.astype(jnp.float32)
        embedding = jnp.concatenate(
            [jnp.sin(levels[:, None] * frequency), jnp.cos(levels[:, None] * frequency)], -1
        ).astype(jnp.bfloat16)
        time_pre = jnp.einsum("vd,jde->jve", embedding, w_time, preferred_element_type=jnp.float32)
        frame_bias = jnp.einsum("fv,jvd->jfd", member, swish(time_pre), precision=HIGH)[
            :, :, None, :
        ]
        frame_level = jnp.dot(member, levels, precision=HIGH)
        alpha_bar = jnp.cos(0.5 * math.pi * (frame_level + 1.0) / (TSTEPS + 1.0)) ** 2
        target = noise[micro_idx, 0]
        noisy_input = (
            jnp.sqrt(alpha_bar)[:, None, None] * clean[micro_idx, 0]
            + jnp.sqrt(1.0 - alpha_bar)[:, None, None] * target
        )
        frame_count = jnp.sum(member * count_grp.astype(jnp.float32)[None, :], 1)
        live_frames = (frame_place.astype(jnp.float32) < frame_count).astype(jnp.float32)
        valid_video = offsets[None, :] < count_grp[:, None]
        valid_rows = jnp.broadcast_to(valid_video[:, None, :], (videos, pix_dev, FRAMES)).reshape(
            videos * pix_dev, FRAMES
        )
        context = (videos, bias_mat, valid_rows, onehot)
        hidden_zero = jnp.einsum("fcp,cd->fpd", noisy_input, in_weight, precision=HIGH)
        hidden_one, saved_zero = res_fwd(
            hidden_zero, kernels[0], kernels[1], gains[0], gains[1], frame_bias[0]
        )
        hidden_two, saved_spatial = mixer_fwd(hidden_one, gains[2], w_in[0], w_out[0], None)
        hidden_three, saved_temporal = mixer_fwd(hidden_two, gains[3], w_in[1], w_out[1], context)
        hidden_four, saved_last = res_fwd(
            hidden_three, kernels[2], kernels[3], gains[4], gains[5], frame_bias[1]
        )
        normed, inverse = norm_fwd(hidden_four, gains[6])
        normed_low = normed.astype(jnp.bfloat16)
        predicted = jnp.einsum(
            "fpd,cd->fcp", normed_low, out_low, preferred_element_type=jnp.float32
        )
        pred_error = predicted - target
        weighted = live_frames[:, None, None] * pred_error
        loss_local = loss_local + jnp.sum(weighted * pred_error)
        dpred = 2.0 * weighted / pixel_total
        d_out = jnp.einsum("fcp,fpd->cd", dpred, normed_low.astype(jnp.float32), precision=HIGH)
        dnormed = jnp.einsum("fcp,cd->fpd", dpred, out_low.astype(jnp.float32), precision=HIGH)
        dhid_four, dgain_six = norm_bwd(hidden_four, inverse, gains[6], dnormed)
        dhid_three, dkern_two, dkern_three, dgain_four, dgain_five, dbias_one = res_bwd(
            hidden_three, dhid_four, kernels[2], kernels[3], gains[4], gains[5], saved_last
        )
        dhid_two, din_one, dout_one, dgain_three, dtable = mixer_bwd(
            hidden_two, dhid_three, gains[3], w_in[1], w_out[1], context, saved_temporal
        )
        dhid_one, din_zero, dout_zero, dgain_two, _ = mixer_bwd(
            hidden_one, dhid_two, gains[2], w_in[0], w_out[0], None, saved_spatial
        )
        dhid_zero, dkern_zero, dkern_one, dgain_zero, dgain_one, dbias_zero = res_bwd(
            hidden_zero, dhid_one, kernels[0], kernels[1], gains[0], gains[1], saved_zero
        )
        dtime_pre = jnp.einsum(
            "fv,jfd->jvd", member, jnp.stack([dbias_zero, dbias_one]), precision=HIGH
        ) * swish_grad(time_pre)
        dtime = jnp.einsum("vd,jve->jde", embedding.astype(jnp.float32), dtime_pre, precision=HIGH)
        d_in = jnp.einsum("fcp,fpd->cd", noisy_input, dhid_zero, precision=HIGH)
        matrix_grads = (
            jnp.stack([dkern_zero, dkern_one, dkern_two, dkern_three]).reshape(36 * D, D),
            jnp.stack([din_zero, din_one]).reshape(2 * D, 3 * D),
            jnp.stack([dout_zero, dout_one]).reshape(2 * D, D),
            dtime.reshape(2 * D, D),
        )
        vector_grads = (
            d_in,
            d_out,
            jnp.stack(
                [dgain_zero, dgain_one, dgain_two, dgain_three, dgain_four, dgain_five, dgain_six]
            ),
            dtable,
        )
        matrix_acc = (
            matrix_grads if matrix_acc is None else jax.tree.map(jnp.add, matrix_acc, matrix_grads)
        )
        vector_acc = (
            vector_grads if vector_acc is None else jax.tree.map(jnp.add, vector_acc, vector_grads)
        )
    matrix_acc = reduce_rows(matrix_acc)
    sum_in, sum_out, sum_gains, sum_table, loss_sum = lax.psum(
        (vector_acc[0], vector_acc[1], vector_acc[2], vector_acc[3], loss_local), ("frame", "batch")
    )
    local_square = sum((jnp.sum(grad * grad) for grad in matrix_acc))
    square = lax.psum(local_square, ("frame", "batch")) + sum(
        (jnp.sum(grad * grad) for grad in (sum_in, sum_out, sum_gains, sum_table))
    )
    grad_norm = jnp.sqrt(square)
    clip_scale = CLIP / jnp.maximum(grad_norm, CLIP)
    conv_new, conv_first_new, conv_second_new = adamw(
        conv_weight, conv_first, conv_second, matrix_acc[0], clip_scale, RATES[0]
    )
    pin_new, pin_first_new, pin_second_new = adamw(
        proj_in, proj_in_first, proj_in_second, matrix_acc[1], clip_scale, RATES[1]
    )
    pout_new, pout_first_new, pout_second_new = adamw(
        proj_out, proj_out_first, proj_out_second, matrix_acc[2], clip_scale, RATES[2]
    )
    time_new, time_first_new, time_second_new = adamw(
        time_weight, time_first, time_second, matrix_acc[3], clip_scale, RATES[3]
    )
    in_new, in_first_new, in_second_new = adamw(
        in_weight, in_first, in_second, sum_in, clip_scale, RATES[4]
    )
    out_new, out_first_new, out_second_new = adamw(
        out_weight, out_first, out_second, sum_out, clip_scale, RATES[5]
    )
    gains_new, gains_first_new, gains_second_new = adamw(
        gains, gains_first, gains_second, sum_gains, clip_scale, RATES[6]
    )
    bias_new, bias_first_new, bias_second_new = adamw(
        rel_bias, rel_bias_first, rel_bias_second, sum_table, clip_scale, RATES[7]
    )
    return (
        loss_sum,
        pixel_total,
        grad_norm,
        conv_new,
        conv_first_new,
        conv_second_new,
        pin_new,
        pin_first_new,
        pin_second_new,
        pout_new,
        pout_first_new,
        pout_second_new,
        time_new,
        time_first_new,
        time_second_new,
        in_new,
        in_first_new,
        in_second_new,
        out_new,
        out_first_new,
        out_second_new,
        gains_new,
        gains_first_new,
        gains_second_new,
        bias_new,
        bias_first_new,
        bias_second_new,
    )


def solution(mesh):
    in_specs = (
        P(None, "batch", "frame", None, None),
        P(None, "batch", "frame", None, None),
        P(),
        P(),
        P("frame", "batch"),
        P("frame", "batch"),
        P("frame", "batch"),
        P("frame", "batch"),
        P("frame", "batch"),
        P("frame", "batch"),
        P("frame", "batch"),
        P("frame", "batch"),
        P("frame", "batch"),
        P("frame", "batch"),
        P("frame", "batch"),
        P("frame", "batch"),
        P(),
        P(),
        P(),
        P(),
        P(),
        P(),
        P(),
        P(),
        P(),
        P(),
        P(),
        P(),
    )
    out_specs = (
        P(),
        P(),
        P(),
        P("frame", "batch"),
        P("frame", "batch"),
        P("frame", "batch"),
        P("frame", "batch"),
        P("frame", "batch"),
        P("frame", "batch"),
        P("frame", "batch"),
        P("frame", "batch"),
        P("frame", "batch"),
        P("frame", "batch"),
        P("frame", "batch"),
        P("frame", "batch"),
        P(),
        P(),
        P(),
        P(),
        P(),
        P(),
        P(),
        P(),
        P(),
        P(),
        P(),
        P(),
    )
    sizes = tuple(mesh.shape[name] for name in ("frame", "batch"))
    local = shards_pairs if sizes == (8, 4) else shards
    return jax.shard_map(local, mesh=mesh, in_specs=in_specs, out_specs=out_specs, check_vma=False)
```

```python
import math

import jax
import jax.numpy as jnp
from jax import lax
from jax.experimental import pallas as pl
from jax.experimental.pallas import tpu as pltpu
from jax.sharding import PartitionSpec as P

D = 256
HEADS = 4
FRAMES = 32
SIDE = 16
MICRO = 2
TSTEPS = 1000
STEP = 10


HIGH = lax.Precision.HIGHEST
EPS_NORM = 1e-06
CLIP = 0.05
BETA_ONE = 0.9
BETA_TWO = 0.999
ADAM_EPS = 1e-08
DECAY = 0.01
RATES = (0.02, 0.06, 0.18, 0.06, 0.6, 0.06, 1.0, 1.0)
NEG = -1000000000.0


def swish(values):
    return values * jax.nn.sigmoid(values)


def swish_grad(values):
    sigma_v = jax.nn.sigmoid(values)
    return sigma_v * (1.0 + values * (1.0 - sigma_v))


def norm_fwd(values, gain_vec):
    inverse = lax.rsqrt(jnp.mean(values * values, -1, keepdims=True) + EPS_NORM)
    return (values * inverse * gain_vec, inverse)


def norm_bwd(values, inverse, gain_vec, upstream):
    scaled = upstream * gain_vec
    dvalues = inverse * scaled - values * inverse**3 * jnp.mean(values * scaled, -1, keepdims=True)
    return (dvalues, jnp.sum(upstream * values * inverse, axis=(0, 1)))


def patches(acts):
    frames, pixels, width = acts.shape
    frame_grid = acts.reshape(frames, SIDE, SIDE, width)
    padded = jnp.pad(frame_grid, ((0, 0), (1, 1), (1, 1), (0, 0)))
    columns = [
        padded[:, offset // 3 : offset // 3 + SIDE, offset % 3 : offset % 3 + SIDE]
        for offset in range(9)
    ]
    return jnp.concatenate(columns, -1).reshape(frames * pixels, 9 * width)


def conv_fwd(acts, kernel):
    frames, pixels, width = acts.shape
    return jnp.dot(patches(acts), kernel, preferred_element_type=jnp.float32).reshape(
        frames, pixels, width
    )


def conv_bwd(acts, grad_low, kernel):
    frames, pixels, width = grad_low.shape
    flat_grad = grad_low.reshape(frames * pixels, width)
    dkernel = lax.dot_general(
        patches(acts), flat_grad, (((0,), (0,)), ((), ())), preferred_element_type=jnp.float32
    )
    tap_terms = lax.dot_general(
        flat_grad, kernel, (((1,), (1,)), ((), ())), preferred_element_type=jnp.float32
    )
    padded = jnp.pad(
        tap_terms.reshape(frames, SIDE, SIDE, 9, width), ((0, 0), (1, 1), (1, 1), (0, 0), (0, 0))
    )
    dacts = sum(
        (
            padded[
                :,
                2 - offset // 3 : 2 - offset // 3 + SIDE,
                2 - offset % 3 : 2 - offset % 3 + SIDE,
                offset,
            ]
            for offset in range(9)
        )
    )
    return (dacts.reshape(frames, pixels, width), dkernel)


def res_fwd(hidden, kern_one, kern_two, gain_one, gain_two, frame_bias):
    normed, inverse_one = norm_fwd(hidden, gain_one)
    acts_one = swish(normed).astype(jnp.bfloat16)
    inner_act = conv_fwd(acts_one, kern_one) + frame_bias
    second_norm, inverse_two = norm_fwd(inner_act, gain_two)
    acts_two = swish(second_norm).astype(jnp.bfloat16)
    saved = (normed, inverse_one, acts_one, inner_act, second_norm, inverse_two, acts_two)
    return (hidden + conv_fwd(acts_two, kern_two), saved)


def res_bwd(hidden, upstream, kern_one, kern_two, gain_one, gain_two, saved):
    normed, inverse_one, acts_one, inner_act, second_norm, inverse_two, acts_two = saved
    dacts_two, dkern_two = conv_bwd(acts_two, upstream.astype(jnp.bfloat16), kern_two)
    dinner, dgain_two = norm_bwd(
        inner_act, inverse_two, gain_two, dacts_two * swish_grad(second_norm)
    )
    dacts_one, dkern_one = conv_bwd(acts_one, dinner.astype(jnp.bfloat16), kern_one)
    dhidden, dgain_one = norm_bwd(hidden, inverse_one, gain_one, dacts_one * swish_grad(normed))
    return (upstream + dhidden, dkern_one, dkern_two, dgain_one, dgain_two, jnp.sum(dinner, 1))


def attend_probs(packed, bias_mat, valid):
    batch, length, _ = packed.shape
    split_heads = packed.reshape(batch, length, 3, HEADS, D // HEADS)
    scores = (
        jnp.einsum(
            "blhe,bmhe->bhlm",
            split_heads[:, :, 0],
            split_heads[:, :, 1],
            preferred_element_type=jnp.float32,
        )
        / math.sqrt(D // HEADS)
        + bias_mat
    )
    if valid is not None:
        scores = jnp.where(valid[:, None, None, :], scores, NEG)
    shifted = jnp.exp(scores - jnp.max(scores, -1, keepdims=True))
    return (shifted / jnp.sum(shifted, -1, keepdims=True), split_heads)


def attend_fwd(packed, bias_mat, valid):
    attn_probs, split_heads = attend_probs(packed, bias_mat, valid)
    mixture = jnp.einsum(
        "bhlm,bmhe->blhe",
        attn_probs.astype(jnp.bfloat16),
        split_heads[:, :, 2],
        preferred_element_type=jnp.float32,
    )
    return mixture.reshape(packed.shape[0], packed.shape[1], D).astype(jnp.bfloat16)


def attend_bwd(packed, dmixture, bias_mat, valid):
    batch, length, _ = packed.shape
    attn_probs, split_heads = attend_probs(packed, bias_mat, valid)
    grad_heads = dmixture.reshape(batch, length, HEADS, D // HEADS)
    dattn_probs = jnp.einsum(
        "blhe,bmhe->bhlm", grad_heads, split_heads[:, :, 2], preferred_element_type=jnp.float32
    )
    dvalues = jnp.einsum(
        "bhlm,blhe->bmhe",
        attn_probs.astype(jnp.bfloat16),
        grad_heads,
        preferred_element_type=jnp.float32,
    )
    dscores = attn_probs * (dattn_probs - jnp.sum(attn_probs * dattn_probs, -1, keepdims=True))
    dscore_low = dscores.astype(jnp.bfloat16)
    root_dim = math.sqrt(D // HEADS)
    dquery = (
        jnp.einsum(
            "bhlm,bmhe->blhe", dscore_low, split_heads[:, :, 1], preferred_element_type=jnp.float32
        )
        / root_dim
    )
    dkey_vals = (
        jnp.einsum(
            "bhlm,blhe->bmhe", dscore_low, split_heads[:, :, 0], preferred_element_type=jnp.float32
        )
        / root_dim
    )
    dpacked = (
        jnp.stack([dquery, dkey_vals, dvalues], 2)
        .reshape(batch, length, 3 * D)
        .astype(jnp.bfloat16)
    )
    return (dpacked, jnp.sum(dscores, 0))


def to_rows(spread, videos):
    slots, pix_dev, width = spread.shape
    return (
        spread.reshape(videos, slots // videos, pix_dev, width)
        .transpose(0, 2, 1, 3)
        .reshape(videos * pix_dev, slots // videos, width)
    )


def from_rows(rows, videos):
    count_rows, length, width = rows.shape
    pix_dev = count_rows // videos
    return (
        rows.reshape(videos, pix_dev, length, width)
        .transpose(0, 2, 1, 3)
        .reshape(videos * length, pix_dev, width)
    )


def mixer_fwd(hidden, gain_vec, w_in, w_out, context):
    normed, inverse = norm_fwd(hidden, gain_vec)
    normed_low = normed.astype(jnp.bfloat16)
    packed = jnp.dot(normed_low, w_in, preferred_element_type=jnp.float32).astype(jnp.bfloat16)
    if context is None:
        return (
            hidden
            + jnp.dot(attend_fwd(packed, 0.0, None), w_out, preferred_element_type=jnp.float32),
            (normed_low, inverse, packed, None),
        )
    videos, bias_mat, valid_rows, onehot = context
    spread = lax.all_to_all(packed, "frame", split_axis=1, concat_axis=0, tiled=True)
    mixture = from_rows(attend_fwd(to_rows(spread, videos), bias_mat, valid_rows), videos)
    gathered_back = lax.all_to_all(mixture, "frame", split_axis=0, concat_axis=1, tiled=True)
    return (
        hidden + jnp.dot(gathered_back, w_out, preferred_element_type=jnp.float32),
        (normed_low, inverse, packed, spread),
    )


def mixer_bwd(hidden, upstream, gain_vec, w_in, w_out, context, saved):
    normed_low, inverse, packed, kept_pixels = saved
    grad_low = upstream.astype(jnp.bfloat16)
    dtable_sum = None
    if context is None:
        inputs, grads_out, bias_mat, valid_rows = (packed, grad_low, 0.0, None)
    else:
        videos, bias_mat, valid_rows, onehot = context
        spread, grad_spread = (
            lax.all_to_all(packed, "frame", split_axis=1, concat_axis=0, tiled=True),
            lax.all_to_all(grad_low, "frame", split_axis=1, concat_axis=0, tiled=True),
        )
        inputs, grads_out = (to_rows(spread, videos), to_rows(grad_spread, videos))
    mixture = attend_fwd(inputs, bias_mat, valid_rows)
    dw_out = jnp.einsum("bld,ble->de", mixture, grads_out, preferred_element_type=jnp.float32)
    dmixture = jnp.einsum(
        "ble,de->bld", grads_out, w_out, preferred_element_type=jnp.float32
    ).astype(jnp.bfloat16)
    dpacked, dbias_sum = attend_bwd(inputs, dmixture, bias_mat, valid_rows)
    if context is not None:
        dpacked = lax.all_to_all(
            from_rows(dpacked, videos), "frame", split_axis=0, concat_axis=1, tiled=True
        )
        dtable_sum = jnp.einsum("hlm,lmk->hk", dbias_sum, onehot, precision=HIGH)
    dw_in = jnp.einsum("fpd,fpk->dk", normed_low, dpacked, preferred_element_type=jnp.float32)
    dnormed = jnp.einsum("fpk,dk->fpd", dpacked, w_in, preferred_element_type=jnp.float32)
    dhidden, dgain_vec = norm_bwd(hidden, inverse, gain_vec, dnormed)
    return (upstream + dhidden, dw_in, dw_out, dgain_vec, dtable_sum)


def fetch(conv_weight, proj_in, proj_out, time_weight):
    columns = (
        lax.all_gather(conv_weight.astype(jnp.bfloat16), "batch", axis=1, tiled=True),
        lax.all_gather(proj_in.astype(jnp.bfloat16), "batch", axis=1, tiled=True),
        lax.all_gather(proj_out.astype(jnp.bfloat16), "batch", axis=1, tiled=True),
        lax.all_gather(time_weight.astype(jnp.bfloat16), "batch", axis=1, tiled=True),
    )
    return (
        lax.all_gather(columns[0], "frame", axis=0, tiled=True),
        lax.all_gather(columns[1], "frame", axis=0, tiled=True),
        lax.all_gather(columns[2], "frame", axis=0, tiled=True),
        lax.all_gather(columns[3], "frame", axis=0, tiled=True),
    )


def reduce_rows(matrix_grads):
    row_parts = (
        lax.psum_scatter(matrix_grads[0], "frame", scatter_dimension=0, tiled=True),
        lax.psum_scatter(matrix_grads[1], "frame", scatter_dimension=0, tiled=True),
        lax.psum_scatter(matrix_grads[2], "frame", scatter_dimension=0, tiled=True),
        lax.psum_scatter(matrix_grads[3], "frame", scatter_dimension=0, tiled=True),
    )
    return (
        lax.psum_scatter(row_parts[0], "batch", scatter_dimension=1, tiled=True),
        lax.psum_scatter(row_parts[1], "batch", scatter_dimension=1, tiled=True),
        lax.psum_scatter(row_parts[2], "batch", scatter_dimension=1, tiled=True),
        lax.psum_scatter(row_parts[3], "batch", scatter_dimension=1, tiled=True),
    )


def adamw(weight, moment_one, moment_two, grad, clip_scale, step_rate):
    grad = grad * clip_scale
    moment_one = BETA_ONE * moment_one + (1.0 - BETA_ONE) * grad
    moment_two = BETA_TWO * moment_two + (1.0 - BETA_TWO) * grad * grad
    update = (
        moment_one
        / (1.0 - BETA_ONE**STEP)
        / (jnp.sqrt(moment_two / (1.0 - BETA_TWO**STEP)) + ADAM_EPS)
    )
    return (weight - step_rate * (update + DECAY * weight), moment_one, moment_two)


ROW_CONV = 576
ROW_GRAD = 704
ROW_ALL = 736
HALF = 352
PAIRS = 4
GAP = 272
NEVER = -1e30
MESH_ID = pl.DeviceIdType.MESH


def dot_nn(lhs, rhs):
    return jnp.dot(lhs, rhs, preferred_element_type=jnp.float32)


def dot_nt(lhs, rhs):
    return lax.dot_general(lhs, rhs, (((1,), (1,)), ((), ())), preferred_element_type=jnp.float32)


def dot_tn(lhs, rhs):
    return lax.dot_general(lhs, rhs, (((0,), (0,)), ((), ())), preferred_element_type=jnp.float32)


def low(values):
    return values.astype(jnp.bfloat16)


def rms(values, gain_row):
    inverse = lax.rsqrt(jnp.mean(values * values, -1, keepdims=True) + EPS_NORM)
    return values * inverse * gain_row, inverse


def rms_back(values, inverse, gain_row, upstream):
    scaled = upstream * gain_row
    unit = values * inverse
    mean = jnp.mean(unit * scaled, -1, keepdims=True)
    return inverse * (scaled - unit * mean), jnp.sum(upstream * unit, 0, keepdims=True)


def weave(block):
    first = block[:256].reshape(32, 1, 8, D)
    second = block[256:].reshape(32, 1, 8, D)
    return jnp.concatenate([first, second], 1).reshape(512, D)


def unweave(block):
    parts = block.reshape(32, 2, 8, D)
    return jnp.concatenate([parts[:, 0].reshape(256, D), parts[:, 1].reshape(256, D)], 0)


def tap_pieces(tap):
    start, stop = 256 * tap, 256 * tap + 256
    pieces = []
    while start < stop:
        block, offset = divmod(start, ROW_CONV)
        size = min(ROW_CONV - offset, stop - start)
        pieces.append((block // 2, block % 2, offset, size))
        start += size
    return pieces


def step_kernel(
    clean_ref,
    noise_ref,
    count_ref,
    video_ref,
    conv_ref,
    pin_ref,
    pout_ref,
    time_ref,
    win_ref,
    wout_ref,
    gains_ref,
    rel_ref,
    grads_ref,
    vector_ref,
    squares_ref,
    dtime_ref,
    wall,
    dslab,
    proj,
    outp,
    mine,
    ready,
    frames_in,
    eight,
    clip_ref,
    table_ref,
    head_pad,
    hid_one,
    hid_two,
    inner_zero,
    dhid,
    pack_zero,
    mix_zero,
    spread_norm,
    pack_one,
    prob_one,
    mix_one,
    mix_back,
    dout_pix,
    dnorm_back,
    stage,
    bias_acc,
    shift_fwd,
    shift_one,
    shift_two,
    act_one,
    act_two,
    acc_out,
    red_sib,
    red_a,
    red_b,
    red_c,
    red_d,
    red_z,
    part_z,
    final,
    vec_acc,
    vec_recv,
    sq_acc,
    sq_recv,
    sem_sib,
    sem_zu,
    sem_zd,
    sem_x,
    sem_y,
    sem_xf,
    sem_yf,
    sem_n,
    sem_m,
    sem_dy,
    sem_dn,
    sem_red,
    sem_fin,
    sem_vec,
    sem_sq,
    sem_in,
):
    fr = lax.axis_index("frame")
    ba = lax.axis_index("batch")
    z, x = fr // 2, fr % 2
    y, c = ba // 2, ba % 2
    ox, oy, oc = 1 - x, 1 - y, 1 - c
    quarter = 2 * x + c
    sibling = (fr, 2 * y + oc)
    x_peer = (2 * z + ox, ba)
    y_peer = (fr, 2 * oy + c)
    xs_peer = (2 * z + ox, 2 * y + oc)
    z_ids = [(z + k) % 4 for k in (1, 2, 3)]
    z_peers = [(2 * k + x, ba) for k in z_ids]
    up_peer = (2 * jnp.minimum(z + 1, 3) + x, ba)
    down_peer = (2 * jnp.maximum(z - 1, 0) + x, ba)
    plane = [(2 * z + px, 2 * py + pc) for px, py, pc in (
        (x, y, oc), (x, oy, c), (x, oy, oc), (ox, y, c), (ox, y, oc), (ox, oy, c), (ox, oy, oc)
    )]
    group = [(sibling, 2 * x + oc), (x_peer, 2 * ox + c), (xs_peer, 2 * ox + oc)]

    def remote(src, dst, sems, send_at, recv_at, device):
        return pltpu.make_async_remote_copy(
            src_ref=src,
            dst_ref=dst,
            send_sem=sems.at[(0,) + send_at],
            recv_sem=sems.at[(1,) + recv_at],
            device_id=device,
            device_id_type=MESH_ID,
        )

    video = 4 * (z // 2) + 2 * y + z % 2
    in_dst = [(4 * (x if t == 0 else ox) + 2 * c + z // 2, 2 * y + z % 2) for t in range(2)]
    in_src = [(2 * quarter + (z // 2 if t == 0 else 1 - z // 2), 2 * y + z % 2) for t in range(2)]
    moves = [(dst[0] != fr) | (dst[1] != ba) for dst in in_dst]

    barrier = pltpu.get_barrier_semaphore()
    everyone = plane + z_peers
    for peer in everyone:
        pl.semaphore_signal(barrier, inc=1, device_id=peer, device_id_type=MESH_ID)
    for turn in range(2):

        @pl.when(moves[turn])
        def _(turn=turn):
            pl.semaphore_signal(barrier, inc=1, device_id=in_src[turn], device_id_type=MESH_ID)

    def spots(rows, columns, shift):
        row = lax.broadcasted_iota(jnp.int32, (rows, columns), 0)
        column = lax.broadcasted_iota(jnp.int32, (rows, columns), 1)
        return low(jnp.where(row + shift == column, 1.0, 0.0))

    narrow = spots(64, 128, 64 * c)
    conv_own = low(dot_tn(low(conv_ref[...]), narrow))
    pin_own = low(dot_nn(low(pin_ref[...]), spots(192, 384, 192 * c)))
    pout_own = low(dot_nn(low(pout_ref[...]), narrow))
    time_own = low(dot_nn(low(time_ref[...]), narrow))
    for half in range(2):
        rows = slice(32 * half, 32 * half + 32)
        ready[half, 0:ROW_CONV] = conv_own[ROW_CONV * half : ROW_CONV * half + ROW_CONV]
        for j in range(3):
            ready[half, ROW_CONV + 32 * j : ROW_CONV + 32 * j + 32] = pin_own[
                rows, 128 * j : 128 * j + 128
            ]
        ready[half, 672:704] = pout_own[rows]
        ready[half, 704:736] = time_own[rows]

    pl.semaphore_wait(
        barrier, len(everyone) + moves[0].astype(jnp.int32) + moves[1].astype(jnp.int32)
    )
    first = remote(ready.at[oc], mine, sem_vec, (11,), (11,), sibling)
    first.start()

    def input_copies(turn):
        micro = x if turn == 0 else ox
        return [
            remote(
                src.at[micro, 0],
                frames_in.at[x, k],
                sem_in,
                (turn, k),
                (turn, k),
                in_dst[turn],
            )
            for k, src in enumerate((clean_ref, noise_ref))
        ]

    for turn in range(2):

        @pl.when(moves[turn])
        def _(turn=turn):
            for copy in input_copies(turn):
                copy.start()

        @pl.when(jnp.logical_not(moves[turn]))
        def _(turn=turn):
            for k, src in enumerate((clean_ref, noise_ref)):
                frames_in[x, k] = src[x if turn == 0 else ox, 0]

    own = wall.at[y, fr, c]
    parts = [pl.ds(0, 368), pl.ds(368, 368)]

    def arrive(dst, sems, at):
        remote(dst, dst, sems, at, at, sibling).wait_recv()

    def push(block, sems, at, device):
        remote(block, block, sems, at, at, device).start()

    def to_sibling(row_z, row_x, row_y):
        at = (row_z, row_x, row_y)
        push(wall.at[row_y, 2 * row_z + row_x, c], sem_sib, at, sibling)

    def turn_row(turn):
        return jnp.where(turn <= z, z - turn, turn)

    def gather_one(turn):
        row_z = turn_row(turn)
        for k, part in enumerate(parts):
            block = wall.at[y, 2 * row_z + x, c, part]
            at = (row_z, k)
            if turn > 0:

                @pl.when(turn <= z)
                def _():
                    arrive(block, sem_zu, at)

                @pl.when(turn > z)
                def _():
                    arrive(block, sem_zd, at)

            @pl.when((turn <= z) & (z < 3))
            def _():
                push(block, sem_zu, at, up_peer)

            @pl.when(((turn > z) | (turn == 0)) & (z > 0))
            def _():
                push(block, sem_zd, at, down_peer)

            push(block, sem_x, at, x_peer)
            push(block, sem_y, at, y_peer)
        to_sibling(row_z, x, y)

    def gather_two(turn):
        row_z = turn_row(turn)
        from_x = [wall.at[y, 2 * row_z + ox, c, part] for part in parts]
        from_y = [wall.at[oy, 2 * row_z + x, c, part] for part in parts]
        arrive(from_x[0], sem_x, (row_z, 0))
        push(from_x[0], sem_yf, (row_z,), y_peer)
        arrive(from_y[0], sem_y, (row_z, 0))
        arrive(from_y[1], sem_y, (row_z, 1))
        push(from_y[1], sem_xf, (row_z,), x_peer)
        to_sibling(row_z, x, oy)
        arrive(from_x[1], sem_x, (row_z, 1))
        to_sibling(row_z, ox, y)

    def gather_three(row_z):
        arrive(wall.at[oy, 2 * row_z + ox, c, parts[0]], sem_yf, (row_z,))
        arrive(wall.at[oy, 2 * row_z + ox, c, parts[1]], sem_xf, (row_z,))
        to_sibling(row_z, ox, oy)

    def gather_four(row_z):
        for row_x in range(2):
            for row_y in range(2):
                arrive(wall.at[row_y, 2 * row_z + row_x, oc], sem_sib, (row_z, row_x, row_y))

    def gather_sent():
        part = wall.at[y, fr, c, parts[0]]

        def sent(block, sems, at):
            remote(block, block, sems, at, at, sibling).wait_send()

        for row_z in range(4):
            for k in range(2):
                sent(part, sem_x, (row_z, k))
                sent(part, sem_y, (row_z, k))

                @pl.when((row_z <= z) & (z < 3))
                def _():
                    sent(part, sem_zu, (row_z, k))

                @pl.when((row_z >= z) & (z > 0))
                def _():
                    sent(part, sem_zd, (row_z, k))

            sent(part, sem_xf, (row_z,))
            sent(part, sem_yf, (row_z,))
            for row_x in range(2):
                for row_y in range(2):
                    sent(own, sem_sib, (row_z, row_x, row_y))

    zeros_row = jnp.zeros((3, 16, D), jnp.bfloat16)
    for frame in range(9):
        shift_one[:, GAP * frame : GAP * frame + 16, :] = zeros_row
        shift_two[:, GAP * frame : GAP * frame + 16, :] = zeros_row
    for frame in range(3):
        shift_fwd[:, GAP * frame : GAP * frame + 16, :] = zeros_row
    bias_acc[...] = jnp.zeros_like(bias_acc)
    vec_acc[...] = jnp.zeros_like(vec_acc)
    acc_out[...] = jnp.zeros_like(acc_out)
    eight[...] = jnp.zeros_like(eight)
    head_pad[...] = jnp.zeros_like(head_pad)
    head_pad[0:3, :] = wout_ref[...]
    first.wait()
    wall[y, fr, c] = ready[c] + mine[...]

    gather_one(0)
    count = count_ref[video]

    def table_rows(part, carry):
        rows = pl.ds(pl.multiple_of(32 * part, 32), 32)
        row = lax.broadcasted_iota(jnp.int32, (32, 256), 0) + 32 * part
        column = lax.broadcasted_iota(jnp.int32, (32, 256), 1)
        away = column // 8 - row // 8
        bucket = jnp.minimum(jnp.abs(away), 15) + jnp.where(away > 0, 16, 0)
        usable = (row % 8 == column % 8) & (column // 8 < count)
        bucket = jnp.where(usable, bucket, -1)
        biases = [jnp.full((32, 256), NEVER, jnp.float32) for _ in range(HEADS)]
        for k in range(32):
            here = bucket == k
            biases = [jnp.where(here, rel_ref[h, k], biases[h]) for h in range(HEADS)]
        for h in range(HEADS):
            table_ref[h, rows, :] = biases[h]
        return carry

    lax.fori_loop(0, 8, table_rows, 0)

    for turn in range(2):

        @pl.when(moves[turn])
        def _(turn=turn):
            for copy in input_copies(turn):
                copy.wait_send()
                copy.wait_recv()

    video_row = video_ref[pl.ds(video, 1), :]
    keep, add = video_row[:, 256:257], video_row[:, 257:258]
    place = spots(8, 128, 0).astype(jnp.float32)
    for frame in range(8):
        noise_rows = frames_in[frame // 4, 1, frame % 4]
        eight[frame, 0:3] = noise_rows
        eight[frame, 3:6] = keep * frames_in[frame // 4, 0, frame % 4] + add * noise_rows
        clip_ref[256 * frame : 256 * frame + 256, :] = lax.dot_general(
            eight[frame],
            place,
            (((0,), (0,)), ((), ())),
            precision=HIGH,
            preferred_element_type=jnp.float32,
        )

    gather_one(1)
    gather_two(0)
    gather_one(2)
    gather_two(1)
    gather_one(3)
    gather_two(2)
    gather_two(3)
    gather_three(0)
    gather_four(0)

    def unpack(rows_of):
        for row_y in range(2):
            for row in rows_of:
                for half in range(2):
                    block = wall.at[row_y, row, half]
                    rows = slice(64 * (row % 4) + 32 * half, 64 * (row % 4) + 32 * half + 32)
                    for j in range(3):
                        cols = slice(384 * row_y + 128 * j, 384 * row_y + 128 * j + 128)
                        proj[row // 4, rows, cols] = block[
                            ROW_CONV + 32 * j : ROW_CONV + 32 * j + 32
                        ]
                    outp[row // 4, rows, 128 * row_y : 128 * row_y + 128] = block[672:704]

    def time_tile(layer):
        rows = []
        for row in range(4 * layer, 4 * layer + 4):
            for half in range(2):
                rows.append(
                    jnp.concatenate(
                        [wall[0, row, half, 704:736, :], wall[1, row, half, 704:736, :]], 1
                    )
                )
        return jnp.concatenate(rows, 0)

    def conv_tile(kernel, tap):
        rows = []
        for row, half, offset, size in tap_pieces(tap):
            block = (2 * kernel + row, half)
            rows.append(
                jnp.concatenate(
                    [
                        wall[(0,) + block + (slice(offset, offset + size),)],
                        wall[(1,) + block + (slice(offset, offset + size),)],
                    ],
                    1,
                )
            )
        return rows[0] if len(rows) == 1 else jnp.concatenate(rows, 0)

    embed = low(jnp.broadcast_to(video_row[:, 0:D], (16, D)))

    def time_project(layer):
        pre = dot_nn(embed, time_tile(layer))[0:1]
        return pre, pre * jax.nn.sigmoid(pre)

    gain = [gains_ref[k : k + 1, :] for k in range(7)]
    column = lax.broadcasted_iota(jnp.int32, (1, D), 1)
    heads = [
        jnp.where(column // 64 == h, 1.0, 0.0).astype(jnp.bfloat16) for h in range(HEADS)
    ]
    pixel_x = lax.broadcasted_iota(jnp.int32, (256, 1), 0) % SIDE
    not_left = jnp.where(pixel_x != 0, 1.0, 0.0)
    not_right = jnp.where(pixel_x != SIDE - 1, 1.0, 0.0)

    def put_shifts(dst, bases, values):
        for k, base in enumerate(bases):
            frame = values[256 * k : 256 * k + 256]
            rows = pl.ds(base, 256)
            dst[0, rows, :] = low(pltpu.roll(frame, 1, 0) * not_left)
            dst[1, rows, :] = low(frame)
            dst[2, rows, :] = low(pltpu.roll(frame, 255, 0) * not_right)

    def aligned(value, multiple):
        return value if isinstance(value, int) else pl.multiple_of(value, multiple)

    def shifted(src, bases, dy, dx):
        return jnp.concatenate(
            [src[dx, pl.ds(aligned(base + 16 * (dy - 1), 16), 256), :] for base in bases], 0
        )

    def conv(src, bases, kernel):
        total = None
        for tap in range(9):
            part = dot_nn(shifted(src, bases, tap // 3, tap % 3), conv_tile(kernel, tap))
            total = part if total is None else total + part
        return total

    def conv_back(src, bases, kernel):
        total = None
        for tap in range(9):
            part = dot_nt(shifted(src, bases, 2 - tap // 3, 2 - tap % 3), conv_tile(kernel, tap))
            total = part if total is None else total + part
        return total

    def conv_grad(act, src, kernel, dst, first_row):
        for tap in range(9):
            grads = shifted(src, [16 + GAP * k for k in range(8)], 2 - tap // 3, 2 - tap % 3)
            total = low(dot_nn(act[...], grads))
            start = 0
            for row, half, offset, size in tap_pieces(tap):
                for row_y in range(2):
                    dst[row_y, first_row + row, half, offset : offset + size] = total[
                        start : start + size, 128 * row_y : 128 * row_y + 128
                    ]
                start += size

    def put_proj_grad(layer, din, dout, dst, first_row):
        for row in range(4):
            for half in range(2):
                rows = slice(64 * row + 32 * half, 64 * row + 32 * half + 32)
                for row_y in range(2):
                    for j in range(3):
                        cols = slice(384 * row_y + 128 * j, 384 * row_y + 128 * j + 128)
                        dst[
                            row_y,
                            first_row + row,
                            half,
                            ROW_CONV + 32 * j : ROW_CONV + 32 * j + 32,
                        ] = din[rows, cols]
                    dst[row_y, first_row + row, half, 672:704] = dout[
                        rows, 128 * row_y : 128 * row_y + 128
                    ]

    def softmax(scores):
        powers = jnp.exp(scores - jnp.max(scores, -1, keepdims=True))
        return low(powers * (1.0 / jnp.sum(powers, -1, keepdims=True)))

    def attend(query, key, value, bias):
        probs = []
        for h in range(HEADS):
            scores = dot_nt(query * heads[h], key) * 0.125
            if bias is not None:
                scores = scores + bias[h]
            probs.append(softmax(scores))
        values = jnp.concatenate([value * heads[h] for h in range(HEADS)], 0)
        return low(dot_nn(jnp.concatenate(probs, 1), values)), probs

    def attend_back(query, key, value, dmix, probs, add_bias):
        dmix_t, query_t = dmix.T, query.T
        dscores, dkey_t, dvalue_t = [], [], []
        for h in range(HEADS):
            prob_low = probs(h)
            prob = prob_low.astype(jnp.float32)
            dprob = dot_nt(dmix * heads[h], value)
            dscore = prob * (dprob - jnp.sum(prob * dprob, -1, keepdims=True))
            if add_bias is not None:
                add_bias(h, dscore)
            dscore_low = low(dscore)
            dscores.append(dscore_low)
            rows = slice(64 * h, 64 * h + 64)
            dvalue_t.append(dot_nn(dmix_t[rows], prob_low))
            dkey_t.append(dot_nn(query_t[rows], dscore_low))
        keys = jnp.concatenate([key * heads[h] for h in range(HEADS)], 0)
        dquery = low(dot_nn(jnp.concatenate(dscores, 1), keys) * 0.125)
        dkey = low(jnp.concatenate(dkey_t, 0) * 0.125).T
        dvalue = low(jnp.concatenate(dvalue_t, 0)).T
        return jnp.concatenate([dquery, dkey, dvalue], 1)

    def add_row(row, value):
        vec_acc[row : row + 1, :] += value

    def embed_input(rows):
        clip = clip_ref[rows, :]
        total = None
        for channel in range(3):
            part = clip[:, 3 + channel : 4 + channel] * win_ref[channel : channel + 1, :]
            total = part if total is None else total + part
        return total, clip

    fwd_bases = [16, 16 + GAP]

    def pair_rows(pair):
        return pl.ds(pl.multiple_of(pair * 512, 512), 512)

    def pair_bases(pair):
        return [
            pl.multiple_of(16 + GAP * (2 * pair), 16),
            pl.multiple_of(16 + GAP * (2 * pair + 1), 16),
        ]

    def send_pair(pair, dst, sems):
        for k, (peer, part) in enumerate(group):
            remote(
                stage.at[pl.ds(32 * pair + 8 * part, 8)],
                dst.at[:, 4 * quarter + pair],
                sems,
                (pair, k),
                (pair, k),
                peer,
            ).start()
        dst[:, 4 * quarter + pair] = stage[pl.ds(32 * pair + 8 * quarter, 8)]

    def wait_pairs(dst, sems):
        for pair in range(PAIRS):
            for k, (peer, part) in enumerate(group):
                copy = remote(
                    stage.at[pl.ds(32 * pair + 8 * part, 8)],
                    dst.at[:, 4 * part + pair],
                    sems,
                    (pair, k),
                    (pair, k),
                    peer,
                )
                copy.wait_send()
                copy.wait_recv()

    def block_tiles(src, block, part):
        return src.at[pl.ds(16 * block + 4 * part, 4)]

    def send_block(block, src, dst, sems):
        for k, (peer, part) in enumerate(group):
            remote(
                block_tiles(src, block, part),
                dst.at[:, quarter, block],
                sems,
                (block, k),
                (block, k),
                peer,
            ).start()
        dst[:, quarter, block] = block_tiles(src, block, quarter)[...]

    def wait_blocks(src, dst, sems):
        for block in range(8):
            for k, (peer, part) in enumerate(group):
                copy = remote(
                    block_tiles(src, block, part),
                    dst.at[:, part, block],
                    sems,
                    (block, k),
                    (block, k),
                    peer,
                )
                copy.wait_send()
                copy.wait_recv()

    def at_pair(pair, when, work):
        @pl.when(pair == when)
        def _():
            work()

    def first_conv(pair, carry):
        rows = pair_rows(pair)
        hidden, _ = embed_input(rows)
        normed, _ = rms(hidden, gain[0])
        put_shifts(shift_fwd, fwd_bases, normed * jax.nn.sigmoid(normed))
        inner_zero[rows, :] = conv(shift_fwd, fwd_bases, 0)
        at_pair(pair, 0, lambda: gather_three(1))
        at_pair(pair, 2, lambda: gather_three(2))
        at_pair(pair, 3, lambda: gather_three(3))
        return carry

    lax.fori_loop(0, PAIRS, first_conv, 0)
    gather_four(1)
    unpack(range(4))
    pre_zero, bias_zero = time_project(0)

    def forward_pair(pair, carry):
        rows = pair_rows(pair)
        hidden, _ = embed_input(rows)
        inner = inner_zero[rows, :] + bias_zero
        inner_zero[rows, :] = inner
        normed, _ = rms(inner, gain[1])
        put_shifts(shift_fwd, fwd_bases, normed * jax.nn.sigmoid(normed))
        hidden = hidden + conv(shift_fwd, fwd_bases, 1)
        hid_one[rows, :] = hidden
        normed, _ = rms(hidden, gain[2])
        packed = low(dot_nn(low(normed), proj[0]))
        pack_zero[rows, :] = packed
        mixed = []
        for k in range(2):
            part = packed[256 * k : 256 * k + 256]
            one, _ = attend(part[:, :D], part[:, D : 2 * D], part[:, 2 * D :], None)
            mixed.append(one)
        mixed = jnp.concatenate(mixed, 0)
        mix_zero[rows, :] = mixed
        hidden = hidden + dot_nn(mixed, outp[0])
        hid_two[rows, :] = hidden
        normed, _ = rms(hidden, gain[3])
        stage[pl.ds(32 * pair, 32)] = low(weave(normed)).reshape(32, 16, D)
        send_pair(pair, spread_norm, sem_n)
        return carry

    lax.fori_loop(0, PAIRS, forward_pair, 0)
    gather_four(2)
    gather_four(3)
    gather_sent()
    unpack(range(4, 8))
    pre_one, bias_one = time_project(1)
    wait_pairs(spread_norm, sem_n)

    def temporal_block(block, carry):
        normed = spread_norm[block].reshape(256, D)
        packed = low(dot_nn(normed, proj[1]))
        pack_one[block] = packed
        mixed, probs = attend(
            packed[:, :D],
            packed[:, D : 2 * D],
            packed[:, 2 * D :],
            [table_ref[h] for h in range(HEADS)],
        )
        for h in range(HEADS):
            prob_one[block, h] = probs[h]
        mix_one[pl.ds(16 * block, 16)] = mixed.reshape(16, 16, D)
        send_block(block, mix_one, mix_back, sem_m)
        return carry

    lax.fori_loop(0, 8, temporal_block, 0)
    wait_blocks(mix_one, mix_back, sem_m)

    frames_all = count_ref[0]
    for k in range(1, 8):
        frames_all = frames_all + count_ref[k]
    pixel_total = jnp.full((1, 1), frames_all, jnp.int32).astype(jnp.float32) * 256.0
    scale = 2.0 / pixel_total
    wout_low = low(wout_ref[...]).astype(jnp.float32)

    def last_pair(pair, carry):
        rows = pair_rows(pair)
        bases = pair_bases(pair)
        lanes = pl.ds(pl.multiple_of(pair * 512, 512), 512)
        hidden = hid_two[rows, :] + unweave(dot_nn(mix_back[pair].reshape(512, D), outp[1]))
        normed, inverse = rms(hidden, gain[4])
        sig = jax.nn.sigmoid(normed)
        acts = normed * sig
        put_shifts(shift_fwd, fwd_bases, acts)
        act_one[:, lanes] = low(acts).T
        slope_one = sig * (1.0 + normed * (1.0 - sig))
        inner = conv(shift_fwd, fwd_bases, 2) + bias_one
        normed_two, inverse_two = rms(inner, gain[5])
        sig_two = jax.nn.sigmoid(normed_two)
        acts_two = normed_two * sig_two
        put_shifts(shift_fwd, fwd_bases, acts_two)
        act_two[:, lanes] = low(acts_two).T
        slope_two = sig_two * (1.0 + normed_two * (1.0 - sig_two))
        last = hidden + conv(shift_fwd, fwd_bases, 3)
        normed, inverse_six = rms(last, gain[6])
        normed_low = low(normed)
        pred = dot_nt(normed_low, low(head_pad[...]))
        clip = clip_ref[rows, :]
        frame_id = lax.broadcasted_iota(jnp.int32, (512, 128), 0) // 256 + (8 * quarter + 2 * pair)
        valid = jnp.where(frame_id < count, 1.0, 0.0)
        lane = lax.broadcasted_iota(jnp.int32, (512, 128), 1)
        error = jnp.where(lane < 3, pred - clip, 0.0)
        weighted = error * valid
        vec_acc[7:8, 0:128] += jnp.sum(weighted * error, 0, keepdims=True)
        dpred = weighted * scale
        dpred_hi = low(dpred)
        dpred_lo = low(dpred - dpred_hi.astype(jnp.float32))
        acc_out[...] += dot_tn(dpred_hi, normed_low) + dot_tn(dpred_lo, normed_low)
        dnormed = None
        for channel in range(3):
            part = dpred[:, channel : channel + 1] * wout_low[channel : channel + 1, :]
            dnormed = part if dnormed is None else dnormed + part
        dlast, dgain = rms_back(last, inverse_six, gain[6], dnormed)
        add_row(6, dgain)
        put_shifts(shift_two, bases, low(dlast).astype(jnp.float32))
        dnormed = conv_back(shift_two, bases, 3) * slope_two
        dinner, dgain = rms_back(inner, inverse_two, gain[5], dnormed)
        add_row(5, dgain)
        add_row(15, jnp.sum(dinner, 0, keepdims=True))
        put_shifts(shift_one, bases, low(dinner).astype(jnp.float32))
        dnormed = conv_back(shift_one, bases, 2) * slope_one
        dhidden, dgain = rms_back(hidden, inverse, gain[4], dnormed)
        add_row(4, dgain)
        dhidden = dhidden + dlast
        dhid[rows, :] = dhidden
        stage[pl.ds(32 * pair, 32)] = low(weave(dhidden)).reshape(32, 16, D)
        send_pair(pair, dout_pix, sem_dy)
        return carry

    lax.fori_loop(0, PAIRS, last_pair, 0)
    conv_grad(act_two, shift_two, 3, wall, 6)
    conv_grad(act_one, shift_one, 2, wall, 4)
    wait_pairs(dout_pix, sem_dy)

    def temporal_back(block, carry):
        dout = dout_pix[block].reshape(256, D)
        dmix = low(dot_nt(dout, outp[1]))
        packed = pack_one[block]

        def add_bias(h, dscore):
            bias_acc[h] += dscore

        dpacked = attend_back(
            packed[:, :D],
            packed[:, D : 2 * D],
            packed[:, 2 * D :],
            dmix,
            lambda h: prob_one[block, h],
            add_bias,
        )
        pack_one[block] = dpacked
        stage[pl.ds(16 * block, 16)] = low(dot_nt(dpacked, proj[1])).reshape(16, 16, D)
        send_block(block, stage, dnorm_back, sem_dn)
        return carry

    lax.fori_loop(0, 8, temporal_back, 0)
    flat = (2048, D)
    dout_one = low(dot_tn(mix_one[...].reshape(flat), dout_pix[...].reshape(flat)))
    din_one = low(dot_tn(spread_norm[...].reshape(flat), pack_one[...].reshape(2048, 3 * D)))
    put_proj_grad(1, din_one, dout_one, wall, 4)
    wait_blocks(stage, dnorm_back, sem_dn)

    def slab(k):
        return (wall, 2 * k) if k >= 2 else (dslab, 2 * k)

    top, low_half = pl.ds(0, HALF), pl.ds(HALF, HALF)

    def red_one(k):
        src, row = slab(k)
        return remote(
            src.at[:, pl.ds(row, 2), oc, pl.ds(0, ROW_GRAD)], red_sib.at[k], sem_red, (k, 0), (k, 0), sibling
        )

    def red_two(k):
        src, row = slab(k)
        return (
            remote(src.at[:, row + ox, c, top], red_a.at[k], sem_red, (k, 1), (k, 1), x_peer),
            remote(src.at[oy, pl.ds(row, 2), c, low_half], red_b.at[k], sem_red, (k, 2), (k, 2), y_peer),
        )

    def red_three(k):
        src, row = slab(k)
        return (
            remote(src.at[oy, row + x, c, top], red_c.at[k], sem_red, (k, 3), (k, 3), y_peer),
            remote(src.at[y, row + ox, c, low_half], red_d.at[k], sem_red, (k, 4), (k, 4), x_peer),
        )

    def both(left, right):
        return low(left.astype(jnp.float32) + right.astype(jnp.float32))

    def finish(copies):
        for copy in copies:
            copy.wait_send()
            copy.wait_recv()

    def add_one(k):
        src, row = slab(k)
        for row_y in range(2):
            for row_x in range(2):
                src[row_y, row + row_x, c, 0:ROW_GRAD] = both(
                    src[row_y, row + row_x, c, 0:ROW_GRAD], red_sib[k, row_y, row_x]
                )

    def add_two(k):
        src, row = slab(k)
        for part in range(2):
            src[part, row + x, c, 0:HALF] = both(src[part, row + x, c, 0:HALF], red_a[k, part])
            src[y, row + part, c, HALF:ROW_GRAD] = both(
                src[y, row + part, c, HALF:ROW_GRAD], red_b[k, part]
            )

    def add_three(k):
        src, row = slab(k)
        part_z[k, 0:HALF] = both(src[y, row + x, c, 0:HALF], red_c[k])
        part_z[k, HALF:ROW_GRAD] = both(src[y, row + x, c, HALF:ROW_GRAD], red_d[k])

    def z_copy(k):
        slot = (z + 3 - k) % 4
        return remote(part_z.at[k], red_z.at[slot], sem_fin, (k,), (slot,), (2 * k + x, ba))

    def send_z(k):
        @pl.when(z != k)
        def _():
            z_copy(k).start()

    def start_all(copies):
        for copy in copies:
            copy.start()

    def spatial_back(pair, carry):
        rows = pair_rows(pair)
        bases = pair_bases(pair)
        lanes = pl.ds(pl.multiple_of(pair * 512, 512), 512)
        dnormed = unweave(dnorm_back[pair].reshape(512, D).astype(jnp.float32))
        hidden = hid_two[rows, :]
        _, inverse = rms(hidden, gain[3])
        dhidden, dgain = rms_back(hidden, inverse, gain[3], dnormed)
        add_row(3, dgain)
        dhidden = dhidden + dhid[rows, :]
        grad_low = low(dhidden)
        dout_pix[pl.ds(2 * pair, 2)] = grad_low.reshape(2, 16, 16, D)
        dmix = low(dot_nt(grad_low, outp[0]))
        packed = pack_zero[rows, :]
        dpacked = []
        for k in range(2):
            part = packed[256 * k : 256 * k + 256]
            query, key, value = part[:, :D], part[:, D : 2 * D], part[:, 2 * D :]

            def again(h):
                return softmax(dot_nt(query * heads[h], key) * 0.125)

            dpacked.append(
                attend_back(query, key, value, dmix[256 * k : 256 * k + 256], again, None)
            )
        dpacked = jnp.concatenate(dpacked, 0)
        pack_zero[rows, :] = dpacked
        hidden = hid_one[rows, :]
        normed, inverse = rms(hidden, gain[2])
        spread_norm[pl.ds(2 * pair, 2)] = low(normed).reshape(2, 16, 16, D)
        dnormed = dot_nt(dpacked, proj[0])
        dprev, dgain = rms_back(hidden, inverse, gain[2], dnormed)
        add_row(2, dgain)
        dhidden = dhidden + dprev
        dhid[rows, :] = dhidden
        put_shifts(shift_two, bases, low(dhidden).astype(jnp.float32))
        normed, _ = rms(inner_zero[rows, :], gain[1])
        act_two[:, lanes] = low(normed * jax.nn.sigmoid(normed)).T
        at_pair(pair, 1, lambda: one_to_two(3))
        at_pair(pair, 2, lambda: one_to_two(2))
        at_pair(pair, 3, lambda: two_to_three(3))
        return carry

    def one_to_two(k):
        finish([red_one(k)])
        add_one(k)
        start_all(red_two(k))

    def two_to_three(k):
        finish(red_two(k))
        add_two(k)
        start_all(red_three(k))

    def three_to_z(k):
        finish(red_three(k))
        add_three(k)
        send_z(k)

    start_all([red_one(3), red_one(2)])
    lax.fori_loop(0, PAIRS, spatial_back, 0)
    two_to_three(2)
    din_zero = low(dot_tn(spread_norm[...].reshape(flat), pack_zero[...]))
    dout_zero = low(dot_tn(mix_zero[...], dout_pix[...].reshape(flat)))
    put_proj_grad(0, din_zero, dout_zero, dslab, 0)
    conv_grad(act_two, shift_two, 1, dslab, 2)
    start_all([red_one(1)])

    def first_back(pair, carry):
        rows = pair_rows(pair)
        bases = pair_bases(pair)
        lanes = pl.ds(pl.multiple_of(pair * 512, 512), 512)
        inner = inner_zero[rows, :]
        normed, inverse = rms(inner, gain[1])
        sig = jax.nn.sigmoid(normed)
        dnormed = conv_back(shift_two, bases, 1) * (sig * (1.0 + normed * (1.0 - sig)))
        dinner, dgain = rms_back(inner, inverse, gain[1], dnormed)
        add_row(1, dgain)
        add_row(14, jnp.sum(dinner, 0, keepdims=True))
        put_shifts(shift_one, bases, low(dinner).astype(jnp.float32))
        hidden, _ = embed_input(rows)
        normed, _ = rms(hidden, gain[0])
        act_one[:, lanes] = low(normed * jax.nn.sigmoid(normed)).T
        at_pair(pair, 0, lambda: three_to_z(3))
        at_pair(pair, 1, lambda: one_to_two(1))
        at_pair(pair, 2, lambda: three_to_z(2))
        return carry

    lax.fori_loop(0, PAIRS, first_back, 0)
    conv_grad(act_one, shift_one, 0, dslab, 0)
    start_all([red_one(0)])
    two_to_three(1)

    def input_back(pair, carry):
        rows = pair_rows(pair)
        bases = pair_bases(pair)
        hidden, clip = embed_input(rows)
        normed, inverse = rms(hidden, gain[0])
        sig = jax.nn.sigmoid(normed)
        dnormed = conv_back(shift_one, bases, 0) * (sig * (1.0 + normed * (1.0 - sig)))
        dhidden, dgain = rms_back(hidden, inverse, gain[0], dnormed)
        add_row(0, dgain)
        dhidden = dhidden + dhid[rows, :]
        for channel in range(3):
            add_row(
                8 + channel,
                jnp.sum(clip[:, 3 + channel : 4 + channel] * dhidden, 0, keepdims=True),
            )
        at_pair(pair, 0, lambda: one_to_two(0))
        at_pair(pair, 1, lambda: three_to_z(1))
        at_pair(pair, 3, lambda: two_to_three(0))
        return carry

    lax.fori_loop(0, PAIRS, input_back, 0)
    vec_acc[11:14, :] = acc_out[0:3, :]
    fold = lax.broadcasted_iota(jnp.int32, (256, 128), 0) // 8
    fold_lane = lax.broadcasted_iota(jnp.int32, (256, 128), 1)
    left = jnp.where(fold == fold_lane, 1.0, 0.0)
    table = None
    for h in range(HEADS):
        right = jnp.where(fold + 32 * h == fold_lane, 1.0, 0.0)
        wide = lax.dot_general(
            bias_acc[h], right, (((1,), (0,)), ((), ())), precision=HIGH, preferred_element_type=jnp.float32
        )
        part = lax.dot_general(
            left, wide, (((0,), (0,)), ((), ())), precision=HIGH, preferred_element_type=jnp.float32
        )
        table = part if table is None else table + part
    away = fold_lane[0:32] % 32 - lax.broadcasted_iota(jnp.int32, (32, 128), 0)
    bucket = jnp.minimum(jnp.abs(away), 15) + jnp.where(away > 0, 16, 0)
    bucket_rows = lax.broadcasted_iota(jnp.int32, (32, 128), 0)
    by_bucket = jnp.zeros((32, 128), jnp.float32)
    for k in range(32):
        one = jnp.sum(jnp.where(bucket == k, table[0:32], 0.0), 0, keepdims=True)
        by_bucket = jnp.where(bucket_rows == k, one, by_bucket)
    head_row = lax.broadcasted_iota(jnp.int32, (8, 128), 0)
    head_lane = lax.broadcasted_iota(jnp.int32, (8, 128), 1)
    pick = jnp.where(head_lane // 32 == head_row, 1.0, 0.0)
    table_sum = lax.dot_general(
        pick, by_bucket, (((1,), (1,)), ((), ())), precision=HIGH, preferred_element_type=jnp.float32
    )
    vec_acc[32:40, 0:32] = table_sum
    row_ids = lax.broadcasted_iota(jnp.int32, (16, D), 0)
    slots = jnp.zeros((16, D), jnp.float32)
    for layer in range(2):
        pre = (pre_zero, pre_one)[layer]
        sig = jax.nn.sigmoid(pre)
        dpre = vec_acc[14 + layer : 15 + layer, :] * (sig * (1.0 + pre * (1.0 - sig)))
        slots = jnp.where(row_ids == 8 * layer + video, dpre, slots)
    vec_acc[16:32, :] = slots

    spot = 4 * x + 2 * y + c

    def plane_copies(values, received, sems):
        return [
            remote(values, received.at[spot], sems, (k,), (spot,), peer)
            for k, peer in enumerate(plane)
        ]

    def plane_total(values, received, sems):
        for px, py, pc in (
            (x, y, oc), (x, oy, c), (x, oy, oc), (ox, y, c), (ox, y, oc), (ox, oy, c), (ox, oy, oc)
        ):
            slot = 4 * px + 2 * py + pc
            remote(values, received.at[slot], sems, (0,), (slot,), sibling).wait_recv()
        for copy in plane_copies(values, received, sems):
            copy.wait_send()
        received[spot] = values[...]
        total = received[0]
        for k in range(1, 8):
            total = total + received[k]
        values[...] = total

    def z_total_copies(values, received, sems):
        return [
            remote(values, received.at[8 + 2 - k], sems, (8 + k,), (8 + 2 - k,), peer)
            for k, peer in enumerate(z_peers)
        ]

    def z_total(values, received, sems):
        finish(z_total_copies(values, received, sems))
        return (values[...] + received[9]) + (received[8] + received[10])

    start_all(plane_copies(vec_acc, vec_recv, sem_vec))
    three_to_z(0)
    plane_total(vec_acc, vec_recv, sem_vec)
    start_all(z_total_copies(vec_acc, vec_recv, sem_vec))
    vector = z_total(vec_acc, vec_recv, sem_vec)
    vector_ref[...] = vector
    small = jnp.sum(vector[0:7] * vector[0:7]) + jnp.sum(vector[8:14] * vector[8:14])
    small = small + jnp.sum(vector[32:36, 0:32] * vector[32:36, 0:32])
    for layer in range(2):
        dtime = lax.dot_general(
            video_ref[:, 0:D],
            vector[16 + 8 * layer : 24 + 8 * layer],
            (((0,), (0,)), ((), ())),
            precision=HIGH,
            preferred_element_type=jnp.float32,
        )
        dtime_ref[layer] = dtime
        small = small + jnp.sum(dtime * dtime)
    total = part_z[z].astype(jnp.float32)
    for slot in range(3):
        arrive(red_z.at[slot], sem_fin, (slot,))
        total = total + red_z[slot].astype(jnp.float32)
    final[c] = total
    own_sums = remote(final.at[c], final.at[c], sem_fin, (4,), (4,), sibling)
    own_sums.start()
    square = jnp.sum(jnp.sum(total * total, 0, keepdims=True), 1, keepdims=True)
    sq_acc[...] = jnp.broadcast_to(square, (8, 128))
    start_all(plane_copies(sq_acc, sq_recv, sem_sq))
    grads_ref[c] = total
    plane_total(sq_acc, sq_recv, sem_sq)
    start_all(z_total_copies(sq_acc, sq_recv, sem_sq))
    own_sums.wait_send()
    arrive(final.at[oc], sem_fin, (4,))
    grads_ref[oc] = final[oc]
    for k in range(4):

        @pl.when(z != k)
        def _():
            z_copy(k).wait_send()

    squares_ref[...] = z_total(sq_acc, sq_recv, sem_sq) + small


def dot_exact(lhs, rhs, dims):
    return lax.dot_general(
        lhs, rhs, (dims, ((), ())), precision=HIGH, preferred_element_type=jnp.float32
    )


def update_kernel(*refs):
    sums_ref, vector_ref, squares_ref, dtime_ref, count_ref = refs[:5]
    state, outs = refs[5:29], refs[29:]
    fr = lax.axis_index("frame")
    ba = lax.axis_index("batch")
    c = ba % 2

    def spots(rows, columns, shift):
        row = lax.broadcasted_iota(jnp.int32, (rows, columns), 0)
        column = lax.broadcasted_iota(jnp.int32, (rows, columns), 1)
        return jnp.where(row + shift == column, 1.0, 0.0)

    norm = jnp.sqrt(squares_ref[0:1, 0:1])
    clip_scale = CLIP / jnp.maximum(norm, CLIP)
    frames_all = count_ref[0]
    for k in range(1, 8):
        frames_all = frames_all + count_ref[k]
    outs[0][...] = jnp.sum(vector_ref[7:8, :], 1, keepdims=True)
    outs[1][...] = jnp.full((1, 1), frames_all, jnp.int32).astype(jnp.float32) * 256.0
    outs[2][...] = norm
    pick = spots(64, 128, 64 * c)
    conv_rows = jnp.concatenate([sums_ref[0, 0:ROW_CONV], sums_ref[1, 0:ROW_CONV]], 0)
    pin, pout = [], []
    for half in range(2):
        rows = None
        for j in range(3):
            part = dot_exact(
                sums_ref[half, ROW_CONV + 32 * j : ROW_CONV + 32 * j + 32],
                spots(192, 128, 192 * c - 128 * j),
                ((1,), (1,)),
            )
            rows = part if rows is None else rows + part
        pin.append(rows)
        pout.append(dot_exact(sums_ref[half, 672:704], pick, ((1,), (1,))))
    time_rows = dtime_ref[fr // 4, pl.ds(pl.multiple_of(64 * (fr % 4), 64), 64), :]
    grads = [
        dot_exact(pick, conv_rows, ((1,), (1,))),
        jnp.concatenate(pin, 0),
        jnp.concatenate(pout, 0),
        dot_exact(time_rows, spots(64, 256, 64 * ba), ((1,), (1,))),
        vector_ref[8:11, :],
        vector_ref[11:14, :],
        vector_ref[0:7, :],
        vector_ref[32:36, 0:32],
    ]
    for k, grad in enumerate(grads):
        weight, first, second = (ref[...] for ref in state[3 * k : 3 * k + 3])
        news = adamw(weight, first, second, grad, clip_scale, RATES[k])
        for ref, value in zip(outs[3 + 3 * k : 6 + 3 * k], news):
            ref[...] = value


def shards_pairs(
    clean,
    noise,
    timesteps,
    frame_counts,
    conv_weight,
    conv_first,
    conv_second,
    proj_in,
    proj_in_first,
    proj_in_second,
    proj_out,
    proj_out_first,
    proj_out_second,
    time_weight,
    time_first,
    time_second,
    in_weight,
    in_first,
    in_second,
    out_weight,
    out_first,
    out_second,
    gains,
    gains_first,
    gains_second,
    rel_bias,
    rel_bias_first,
    rel_bias_second,
):

    levels = timesteps.reshape(-1, 1).astype(jnp.float32)
    counts = frame_counts.reshape(-1)
    half_width = D // 2
    lane = lax.broadcasted_iota(jnp.int32, (8, 384), 1)
    frequency = jnp.exp(-math.log(10000.0) * (lane % half_width).astype(jnp.float32) / half_width)
    angles = jnp.where(
        lane < D, levels * frequency, 0.5 * math.pi * (levels + 1.0) / (TSTEPS + 1.0)
    )
    sines, cosines = jnp.sin(angles), jnp.cos(angles)
    embedding = jnp.where(lane < half_width, sines, cosines).astype(jnp.bfloat16)
    alpha_bar = cosines**2
    video_rows = jnp.where(
        lane < D,
        embedding.astype(jnp.float32),
        jnp.where(lane == D, jnp.sqrt(alpha_bar), jnp.sqrt(1.0 - alpha_bar)),
    )

    bf16, f32 = jnp.bfloat16, jnp.float32
    vmem = pl.BlockSpec(memory_space=pltpu.VMEM)
    smem = pl.BlockSpec(memory_space=pltpu.SMEM)
    scratch = [
        pltpu.VMEM((2, 8, 2, ROW_ALL, 128), bf16),
        pltpu.VMEM((2, 4, 2, ROW_GRAD, 128), bf16),
        pltpu.VMEM((2, D, 3 * D), bf16),
        pltpu.VMEM((2, D, D), bf16),
        pltpu.VMEM((ROW_ALL, 128), bf16),
        pltpu.VMEM((2, ROW_ALL, 128), bf16),
        pltpu.VMEM((2, 2, 4, 3, 256), f32),
        pltpu.VMEM((8, 8, 256), f32),
        pltpu.VMEM((2048, 128), f32),
        pltpu.VMEM((HEADS, 256, 256), f32),
        pltpu.VMEM((128, D), f32),
        pltpu.VMEM((2048, D), f32),
        pltpu.VMEM((2048, D), f32),
        pltpu.VMEM((2048, D), f32),
        pltpu.VMEM((2048, D), f32),
        pltpu.VMEM((2048, 3 * D), bf16),
        pltpu.VMEM((2048, D), bf16),
        pltpu.VMEM((8, 16, 16, D), bf16),
        pltpu.VMEM((8, 256, 3 * D), bf16),
        pltpu.VMEM((8, HEADS, 256, 256), bf16),
        pltpu.VMEM((128, 16, D), bf16),
        pltpu.VMEM((PAIRS, 4, 8, 16, D), bf16),
        pltpu.VMEM((8, 16, 16, D), bf16),
        pltpu.VMEM((PAIRS, 4, 8, 16, D), bf16),
        pltpu.VMEM((128, 16, D), bf16),
        pltpu.VMEM((HEADS, 256, 256), f32),
        pltpu.VMEM((3, 2 * GAP + 16, D), bf16),
        pltpu.VMEM((3, 8 * GAP + 16, D), bf16),
        pltpu.VMEM((3, 8 * GAP + 16, D), bf16),
        pltpu.VMEM((D, 2048), bf16),
        pltpu.VMEM((D, 2048), bf16),
        pltpu.VMEM((128, D), f32),
        pltpu.VMEM((4, 2, 2, ROW_GRAD, 128), bf16),
        pltpu.VMEM((4, 2, HALF, 128), bf16),
        pltpu.VMEM((4, 2, HALF, 128), bf16),
        pltpu.VMEM((4, HALF, 128), bf16),
        pltpu.VMEM((4, HALF, 128), bf16),
        pltpu.VMEM((3, ROW_GRAD, 128), bf16),
        pltpu.VMEM((4, ROW_GRAD, 128), bf16),
        pltpu.VMEM((2, ROW_GRAD, 128), f32),
        pltpu.VMEM((40, D), f32),
        pltpu.VMEM((11, 40, D), f32),
        pltpu.VMEM((8, 128), f32),
        pltpu.VMEM((11, 8, 128), f32),
        pltpu.SemaphoreType.DMA((2, 4, 2, 2)),
        pltpu.SemaphoreType.DMA((2, 4, 2)),
        pltpu.SemaphoreType.DMA((2, 4, 2)),
        pltpu.SemaphoreType.DMA((2, 4, 2)),
        pltpu.SemaphoreType.DMA((2, 4, 2)),
        pltpu.SemaphoreType.DMA((2, 4)),
        pltpu.SemaphoreType.DMA((2, 4)),
        pltpu.SemaphoreType.DMA((2, PAIRS, 3)),
        pltpu.SemaphoreType.DMA((2, 8, 3)),
        pltpu.SemaphoreType.DMA((2, PAIRS, 3)),
        pltpu.SemaphoreType.DMA((2, 8, 3)),
        pltpu.SemaphoreType.DMA((2, 4, 5)),
        pltpu.SemaphoreType.DMA((2, 5)),
        pltpu.SemaphoreType.DMA((2, 12)),
        pltpu.SemaphoreType.DMA((2, 12)),
        pltpu.SemaphoreType.DMA((2, 2, 2)),
    ]
    sums, vector, squares, dtime = pl.pallas_call(
        step_kernel,
        out_shape=(
            jax.ShapeDtypeStruct((2, ROW_GRAD, 128), f32),
            jax.ShapeDtypeStruct((40, D), f32),
            jax.ShapeDtypeStruct((8, 128), f32),
            jax.ShapeDtypeStruct((2, D, D), f32),
        ),
        in_specs=[vmem, vmem, smem] + [vmem] * 8 + [smem],
        out_specs=(vmem,) * 4,
        scratch_shapes=scratch,
        compiler_params=pltpu.CompilerParams(
            collective_id=0, has_side_effects=True, vmem_limit_bytes=64 * 2**20 - 2**16
        ),
        name="train_step",
    )(
        clean,
        noise,
        counts,
        video_rows,
        conv_weight.T,
        proj_in,
        proj_out,
        time_weight,
        in_weight,
        out_weight,
        gains,
        rel_bias,
    )
    state = (
        conv_weight.T,
        conv_first.T,
        conv_second.T,
        proj_in,
        proj_in_first,
        proj_in_second,
        proj_out,
        proj_out_first,
        proj_out_second,
        time_weight,
        time_first,
        time_second,
        in_weight,
        in_first,
        in_second,
        out_weight,
        out_first,
        out_second,
        gains,
        gains_first,
        gains_second,
        rel_bias,
        rel_bias_first,
        rel_bias_second,
    )
    scalar = jax.ShapeDtypeStruct((1, 1), f32)
    results = pl.pallas_call(
        update_kernel,
        out_shape=[scalar] * 3 + [jax.ShapeDtypeStruct(value.shape, f32) for value in state],
        in_specs=[vmem] * 4 + [smem] + [vmem] * 24,
        out_specs=[vmem] * 27,
        compiler_params=pltpu.CompilerParams(vmem_limit_bytes=64 * 2**20 - 2**16),
        name="update",
    )(sums, vector, squares, dtime, counts, *state)
    return (
        *(value.reshape(()) for value in results[:3]),
        *(value.T for value in results[3:6]),
        *results[6:],
    )


def shards(
    clean,
    noise,
    timesteps,
    frame_counts,
    conv_weight,
    conv_first,
    conv_second,
    proj_in,
    proj_in_first,
    proj_in_second,
    proj_out,
    proj_out_first,
    proj_out_second,
    time_weight,
    time_first,
    time_second,
    in_weight,
    in_first,
    in_second,
    out_weight,
    out_first,
    out_second,
    gains,
    gains_first,
    gains_second,
    rel_bias,
    rel_bias_first,
    rel_bias_second,
):
    fr_dev = clean.shape[2]
    pixels = clean.shape[4]
    videos = timesteps.shape[2]
    pix_dev = pixels // lax.axis_size("frame")
    group_idx = lax.axis_index("batch")
    frame_ids = lax.axis_index("frame") * fr_dev + jnp.arange(fr_dev)
    member = (frame_ids[:, None] // FRAMES == jnp.arange(videos)[None, :]).astype(jnp.float32)
    frame_place = frame_ids % FRAMES
    pixel_total = jnp.sum(frame_counts).astype(jnp.float32) * pixels
    offsets = jnp.arange(FRAMES)
    distance = offsets[None, :] - offsets[:, None]
    bucket = jnp.minimum(jnp.abs(distance), 15) + 16 * (distance > 0).astype(jnp.int32)
    onehot = (bucket[:, :, None] == jnp.arange(rel_bias.shape[1])[None, None, :]).astype(
        jnp.float32
    )
    bias_mat = jnp.einsum("hk,lmk->hlm", rel_bias, onehot, precision=HIGH)
    half_width = D // 2
    frequency = jnp.exp(-math.log(10000.0) * jnp.arange(half_width, dtype=jnp.float32) / half_width)
    out_low = out_weight.astype(jnp.bfloat16)
    matrix_acc = None
    vector_acc = None
    loss_local = jnp.zeros((), jnp.float32)
    for micro_idx in range(MICRO):
        gathered = fetch(conv_weight, proj_in, proj_out, time_weight)
        kernels = gathered[0].reshape(4, 9 * D, D)
        w_in = gathered[1].reshape(2, D, 3 * D)
        w_out = gathered[2].reshape(2, D, D)
        w_time = gathered[3].reshape(2, D, D)
        steps_grp = lax.dynamic_index_in_dim(timesteps[micro_idx], group_idx, 0, keepdims=False)
        count_grp = lax.dynamic_index_in_dim(frame_counts[micro_idx], group_idx, 0, keepdims=False)
        levels = steps_grp.astype(jnp.float32)
        embedding = jnp.concatenate(
            [jnp.sin(levels[:, None] * frequency), jnp.cos(levels[:, None] * frequency)], -1
        ).astype(jnp.bfloat16)
        time_pre = jnp.einsum("vd,jde->jve", embedding, w_time, preferred_element_type=jnp.float32)
        frame_bias = jnp.einsum("fv,jvd->jfd", member, swish(time_pre), precision=HIGH)[
            :, :, None, :
        ]
        frame_level = jnp.dot(member, levels, precision=HIGH)
        alpha_bar = jnp.cos(0.5 * math.pi * (frame_level + 1.0) / (TSTEPS + 1.0)) ** 2
        target = noise[micro_idx, 0]
        noisy_input = (
            jnp.sqrt(alpha_bar)[:, None, None] * clean[micro_idx, 0]
            + jnp.sqrt(1.0 - alpha_bar)[:, None, None] * target
        )
        frame_count = jnp.sum(member * count_grp.astype(jnp.float32)[None, :], 1)
        live_frames = (frame_place.astype(jnp.float32) < frame_count).astype(jnp.float32)
        valid_video = offsets[None, :] < count_grp[:, None]
        valid_rows = jnp.broadcast_to(valid_video[:, None, :], (videos, pix_dev, FRAMES)).reshape(
            videos * pix_dev, FRAMES
        )
        context = (videos, bias_mat, valid_rows, onehot)
        hidden_zero = jnp.einsum("fcp,cd->fpd", noisy_input, in_weight, precision=HIGH)
        hidden_one, saved_zero = res_fwd(
            hidden_zero, kernels[0], kernels[1], gains[0], gains[1], frame_bias[0]
        )
        hidden_two, saved_spatial = mixer_fwd(hidden_one, gains[2], w_in[0], w_out[0], None)
        hidden_three, saved_temporal = mixer_fwd(hidden_two, gains[3], w_in[1], w_out[1], context)
        hidden_four, saved_last = res_fwd(
            hidden_three, kernels[2], kernels[3], gains[4], gains[5], frame_bias[1]
        )
        normed, inverse = norm_fwd(hidden_four, gains[6])
        normed_low = normed.astype(jnp.bfloat16)
        predicted = jnp.einsum(
            "fpd,cd->fcp", normed_low, out_low, preferred_element_type=jnp.float32
        )
        pred_error = predicted - target
        weighted = live_frames[:, None, None] * pred_error
        loss_local = loss_local + jnp.sum(weighted * pred_error)
        dpred = 2.0 * weighted / pixel_total
        d_out = jnp.einsum("fcp,fpd->cd", dpred, normed_low.astype(jnp.float32), precision=HIGH)
        dnormed = jnp.einsum("fcp,cd->fpd", dpred, out_low.astype(jnp.float32), precision=HIGH)
        dhid_four, dgain_six = norm_bwd(hidden_four, inverse, gains[6], dnormed)
        dhid_three, dkern_two, dkern_three, dgain_four, dgain_five, dbias_one = res_bwd(
            hidden_three, dhid_four, kernels[2], kernels[3], gains[4], gains[5], saved_last
        )
        dhid_two, din_one, dout_one, dgain_three, dtable = mixer_bwd(
            hidden_two, dhid_three, gains[3], w_in[1], w_out[1], context, saved_temporal
        )
        dhid_one, din_zero, dout_zero, dgain_two, _ = mixer_bwd(
            hidden_one, dhid_two, gains[2], w_in[0], w_out[0], None, saved_spatial
        )
        dhid_zero, dkern_zero, dkern_one, dgain_zero, dgain_one, dbias_zero = res_bwd(
            hidden_zero, dhid_one, kernels[0], kernels[1], gains[0], gains[1], saved_zero
        )
        dtime_pre = jnp.einsum(
            "fv,jfd->jvd", member, jnp.stack([dbias_zero, dbias_one]), precision=HIGH
        ) * swish_grad(time_pre)
        dtime = jnp.einsum("vd,jve->jde", embedding.astype(jnp.float32), dtime_pre, precision=HIGH)
        d_in = jnp.einsum("fcp,fpd->cd", noisy_input, dhid_zero, precision=HIGH)
        matrix_grads = (
            jnp.stack([dkern_zero, dkern_one, dkern_two, dkern_three]).reshape(36 * D, D),
            jnp.stack([din_zero, din_one]).reshape(2 * D, 3 * D),
            jnp.stack([dout_zero, dout_one]).reshape(2 * D, D),
            dtime.reshape(2 * D, D),
        )
        vector_grads = (
            d_in,
            d_out,
            jnp.stack(
                [dgain_zero, dgain_one, dgain_two, dgain_three, dgain_four, dgain_five, dgain_six]
            ),
            dtable,
        )
        matrix_acc = (
            matrix_grads if matrix_acc is None else jax.tree.map(jnp.add, matrix_acc, matrix_grads)
        )
        vector_acc = (
            vector_grads if vector_acc is None else jax.tree.map(jnp.add, vector_acc, vector_grads)
        )
    matrix_acc = reduce_rows(matrix_acc)
    sum_in, sum_out, sum_gains, sum_table, loss_sum = lax.psum(
        (vector_acc[0], vector_acc[1], vector_acc[2], vector_acc[3], loss_local), ("frame", "batch")
    )
    local_square = sum((jnp.sum(grad * grad) for grad in matrix_acc))
    square = lax.psum(local_square, ("frame", "batch")) + sum(
        (jnp.sum(grad * grad) for grad in (sum_in, sum_out, sum_gains, sum_table))
    )
    grad_norm = jnp.sqrt(square)
    clip_scale = CLIP / jnp.maximum(grad_norm, CLIP)
    conv_new, conv_first_new, conv_second_new = adamw(
        conv_weight, conv_first, conv_second, matrix_acc[0], clip_scale, RATES[0]
    )
    pin_new, pin_first_new, pin_second_new = adamw(
        proj_in, proj_in_first, proj_in_second, matrix_acc[1], clip_scale, RATES[1]
    )
    pout_new, pout_first_new, pout_second_new = adamw(
        proj_out, proj_out_first, proj_out_second, matrix_acc[2], clip_scale, RATES[2]
    )
    time_new, time_first_new, time_second_new = adamw(
        time_weight, time_first, time_second, matrix_acc[3], clip_scale, RATES[3]
    )
    in_new, in_first_new, in_second_new = adamw(
        in_weight, in_first, in_second, sum_in, clip_scale, RATES[4]
    )
    out_new, out_first_new, out_second_new = adamw(
        out_weight, out_first, out_second, sum_out, clip_scale, RATES[5]
    )
    gains_new, gains_first_new, gains_second_new = adamw(
        gains, gains_first, gains_second, sum_gains, clip_scale, RATES[6]
    )
    bias_new, bias_first_new, bias_second_new = adamw(
        rel_bias, rel_bias_first, rel_bias_second, sum_table, clip_scale, RATES[7]
    )
    return (
        loss_sum,
        pixel_total,
        grad_norm,
        conv_new,
        conv_first_new,
        conv_second_new,
        pin_new,
        pin_first_new,
        pin_second_new,
        pout_new,
        pout_first_new,
        pout_second_new,
        time_new,
        time_first_new,
        time_second_new,
        in_new,
        in_first_new,
        in_second_new,
        out_new,
        out_first_new,
        out_second_new,
        gains_new,
        gains_first_new,
        gains_second_new,
        bias_new,
        bias_first_new,
        bias_second_new,
    )


def solution(mesh):
    in_specs = (
        P(None, "batch", "frame", None, None),
        P(None, "batch", "frame", None, None),
        P(),
        P(),
        P("frame", "batch"),
        P("frame", "batch"),
        P("frame", "batch"),
        P("frame", "batch"),
        P("frame", "batch"),
        P("frame", "batch"),
        P("frame", "batch"),
        P("frame", "batch"),
        P("frame", "batch"),
        P("frame", "batch"),
        P("frame", "batch"),
        P("frame", "batch"),
        P(),
        P(),
        P(),
        P(),
        P(),
        P(),
        P(),
        P(),
        P(),
        P(),
        P(),
        P(),
    )
    out_specs = (
        P(),
        P(),
        P(),
        P("frame", "batch"),
        P("frame", "batch"),
        P("frame", "batch"),
        P("frame", "batch"),
        P("frame", "batch"),
        P("frame", "batch"),
        P("frame", "batch"),
        P("frame", "batch"),
        P("frame", "batch"),
        P("frame", "batch"),
        P("frame", "batch"),
        P("frame", "batch"),
        P(),
        P(),
        P(),
        P(),
        P(),
        P(),
        P(),
        P(),
        P(),
        P(),
        P(),
        P(),
    )
    sizes = tuple(mesh.shape[name] for name in ("frame", "batch"))
    local = shards_pairs if sizes == (8, 4) else shards
    return jax.shard_map(local, mesh=mesh, in_specs=in_specs, out_specs=out_specs, check_vma=False)
```

```python
import math

import jax
import jax.numpy as jnp
from jax import lax
from jax.experimental import pallas as pl
from jax.experimental.pallas import tpu as pltpu
from jax.sharding import PartitionSpec as P

D = 256
HEADS = 4
FRAMES = 32
SIDE = 16
MICRO = 2
TSTEPS = 1000
STEP = 10


HIGH = lax.Precision.HIGHEST
EPS_NORM = 1e-06
CLIP = 0.05
BETA_ONE = 0.9
BETA_TWO = 0.999
ADAM_EPS = 1e-08
DECAY = 0.01
RATES = (0.02, 0.06, 0.18, 0.06, 0.6, 0.06, 1.0, 1.0)
NEG = -1000000000.0


def swish(values):
    return values * jax.nn.sigmoid(values)


def swish_grad(values):
    sigma_v = jax.nn.sigmoid(values)
    return sigma_v * (1.0 + values * (1.0 - sigma_v))


def norm_fwd(values, gain_vec):
    inverse = lax.rsqrt(jnp.mean(values * values, -1, keepdims=True) + EPS_NORM)
    return (values * inverse * gain_vec, inverse)


def norm_bwd(values, inverse, gain_vec, upstream):
    scaled = upstream * gain_vec
    dvalues = inverse * scaled - values * inverse**3 * jnp.mean(values * scaled, -1, keepdims=True)
    return (dvalues, jnp.sum(upstream * values * inverse, axis=(0, 1)))


def patches(acts):
    frames, pixels, width = acts.shape
    frame_grid = acts.reshape(frames, SIDE, SIDE, width)
    padded = jnp.pad(frame_grid, ((0, 0), (1, 1), (1, 1), (0, 0)))
    columns = [
        padded[:, offset // 3 : offset // 3 + SIDE, offset % 3 : offset % 3 + SIDE]
        for offset in range(9)
    ]
    return jnp.concatenate(columns, -1).reshape(frames * pixels, 9 * width)


def conv_fwd(acts, kernel):
    frames, pixels, width = acts.shape
    return jnp.dot(patches(acts), kernel, preferred_element_type=jnp.float32).reshape(
        frames, pixels, width
    )


def conv_bwd(acts, grad_low, kernel):
    frames, pixels, width = grad_low.shape
    flat_grad = grad_low.reshape(frames * pixels, width)
    dkernel = lax.dot_general(
        patches(acts), flat_grad, (((0,), (0,)), ((), ())), preferred_element_type=jnp.float32
    )
    tap_terms = lax.dot_general(
        flat_grad, kernel, (((1,), (1,)), ((), ())), preferred_element_type=jnp.float32
    )
    padded = jnp.pad(
        tap_terms.reshape(frames, SIDE, SIDE, 9, width), ((0, 0), (1, 1), (1, 1), (0, 0), (0, 0))
    )
    dacts = sum(
        (
            padded[
                :,
                2 - offset // 3 : 2 - offset // 3 + SIDE,
                2 - offset % 3 : 2 - offset % 3 + SIDE,
                offset,
            ]
            for offset in range(9)
        )
    )
    return (dacts.reshape(frames, pixels, width), dkernel)


def res_fwd(hidden, kern_one, kern_two, gain_one, gain_two, frame_bias):
    normed, inverse_one = norm_fwd(hidden, gain_one)
    acts_one = swish(normed).astype(jnp.bfloat16)
    inner_act = conv_fwd(acts_one, kern_one) + frame_bias
    second_norm, inverse_two = norm_fwd(inner_act, gain_two)
    acts_two = swish(second_norm).astype(jnp.bfloat16)
    saved = (normed, inverse_one, acts_one, inner_act, second_norm, inverse_two, acts_two)
    return (hidden + conv_fwd(acts_two, kern_two), saved)


def res_bwd(hidden, upstream, kern_one, kern_two, gain_one, gain_two, saved):
    normed, inverse_one, acts_one, inner_act, second_norm, inverse_two, acts_two = saved
    dacts_two, dkern_two = conv_bwd(acts_two, upstream.astype(jnp.bfloat16), kern_two)
    dinner, dgain_two = norm_bwd(
        inner_act, inverse_two, gain_two, dacts_two * swish_grad(second_norm)
    )
    dacts_one, dkern_one = conv_bwd(acts_one, dinner.astype(jnp.bfloat16), kern_one)
    dhidden, dgain_one = norm_bwd(hidden, inverse_one, gain_one, dacts_one * swish_grad(normed))
    return (upstream + dhidden, dkern_one, dkern_two, dgain_one, dgain_two, jnp.sum(dinner, 1))


def attend_probs(packed, bias_mat, valid):
    batch, length, _ = packed.shape
    split_heads = packed.reshape(batch, length, 3, HEADS, D // HEADS)
    scores = (
        jnp.einsum(
            "blhe,bmhe->bhlm",
            split_heads[:, :, 0],
            split_heads[:, :, 1],
            preferred_element_type=jnp.float32,
        )
        / math.sqrt(D // HEADS)
        + bias_mat
    )
    if valid is not None:
        scores = jnp.where(valid[:, None, None, :], scores, NEG)
    shifted = jnp.exp(scores - jnp.max(scores, -1, keepdims=True))
    return (shifted / jnp.sum(shifted, -1, keepdims=True), split_heads)


def attend_fwd(packed, bias_mat, valid):
    attn_probs, split_heads = attend_probs(packed, bias_mat, valid)
    mixture = jnp.einsum(
        "bhlm,bmhe->blhe",
        attn_probs.astype(jnp.bfloat16),
        split_heads[:, :, 2],
        preferred_element_type=jnp.float32,
    )
    return mixture.reshape(packed.shape[0], packed.shape[1], D).astype(jnp.bfloat16)


def attend_bwd(packed, dmixture, bias_mat, valid):
    batch, length, _ = packed.shape
    attn_probs, split_heads = attend_probs(packed, bias_mat, valid)
    grad_heads = dmixture.reshape(batch, length, HEADS, D // HEADS)
    dattn_probs = jnp.einsum(
        "blhe,bmhe->bhlm", grad_heads, split_heads[:, :, 2], preferred_element_type=jnp.float32
    )
    dvalues = jnp.einsum(
        "bhlm,blhe->bmhe",
        attn_probs.astype(jnp.bfloat16),
        grad_heads,
        preferred_element_type=jnp.float32,
    )
    dscores = attn_probs * (dattn_probs - jnp.sum(attn_probs * dattn_probs, -1, keepdims=True))
    dscore_low = dscores.astype(jnp.bfloat16)
    root_dim = math.sqrt(D // HEADS)
    dquery = (
        jnp.einsum(
            "bhlm,bmhe->blhe", dscore_low, split_heads[:, :, 1], preferred_element_type=jnp.float32
        )
        / root_dim
    )
    dkey_vals = (
        jnp.einsum(
            "bhlm,blhe->bmhe", dscore_low, split_heads[:, :, 0], preferred_element_type=jnp.float32
        )
        / root_dim
    )
    dpacked = (
        jnp.stack([dquery, dkey_vals, dvalues], 2)
        .reshape(batch, length, 3 * D)
        .astype(jnp.bfloat16)
    )
    return (dpacked, jnp.sum(dscores, 0))


def to_rows(spread, videos):
    slots, pix_dev, width = spread.shape
    return (
        spread.reshape(videos, slots // videos, pix_dev, width)
        .transpose(0, 2, 1, 3)
        .reshape(videos * pix_dev, slots // videos, width)
    )


def from_rows(rows, videos):
    count_rows, length, width = rows.shape
    pix_dev = count_rows // videos
    return (
        rows.reshape(videos, pix_dev, length, width)
        .transpose(0, 2, 1, 3)
        .reshape(videos * length, pix_dev, width)
    )


def mixer_fwd(hidden, gain_vec, w_in, w_out, context):
    normed, inverse = norm_fwd(hidden, gain_vec)
    normed_low = normed.astype(jnp.bfloat16)
    packed = jnp.dot(normed_low, w_in, preferred_element_type=jnp.float32).astype(jnp.bfloat16)
    if context is None:
        return (
            hidden
            + jnp.dot(attend_fwd(packed, 0.0, None), w_out, preferred_element_type=jnp.float32),
            (normed_low, inverse, packed, None),
        )
    videos, bias_mat, valid_rows, onehot = context
    spread = lax.all_to_all(packed, "frame", split_axis=1, concat_axis=0, tiled=True)
    mixture = from_rows(attend_fwd(to_rows(spread, videos), bias_mat, valid_rows), videos)
    gathered_back = lax.all_to_all(mixture, "frame", split_axis=0, concat_axis=1, tiled=True)
    return (
        hidden + jnp.dot(gathered_back, w_out, preferred_element_type=jnp.float32),
        (normed_low, inverse, packed, spread),
    )


def mixer_bwd(hidden, upstream, gain_vec, w_in, w_out, context, saved):
    normed_low, inverse, packed, kept_pixels = saved
    grad_low = upstream.astype(jnp.bfloat16)
    dtable_sum = None
    if context is None:
        inputs, grads_out, bias_mat, valid_rows = (packed, grad_low, 0.0, None)
    else:
        videos, bias_mat, valid_rows, onehot = context
        spread, grad_spread = (
            lax.all_to_all(packed, "frame", split_axis=1, concat_axis=0, tiled=True),
            lax.all_to_all(grad_low, "frame", split_axis=1, concat_axis=0, tiled=True),
        )
        inputs, grads_out = (to_rows(spread, videos), to_rows(grad_spread, videos))
    mixture = attend_fwd(inputs, bias_mat, valid_rows)
    dw_out = jnp.einsum("bld,ble->de", mixture, grads_out, preferred_element_type=jnp.float32)
    dmixture = jnp.einsum(
        "ble,de->bld", grads_out, w_out, preferred_element_type=jnp.float32
    ).astype(jnp.bfloat16)
    dpacked, dbias_sum = attend_bwd(inputs, dmixture, bias_mat, valid_rows)
    if context is not None:
        dpacked = lax.all_to_all(
            from_rows(dpacked, videos), "frame", split_axis=0, concat_axis=1, tiled=True
        )
        dtable_sum = jnp.einsum("hlm,lmk->hk", dbias_sum, onehot, precision=HIGH)
    dw_in = jnp.einsum("fpd,fpk->dk", normed_low, dpacked, preferred_element_type=jnp.float32)
    dnormed = jnp.einsum("fpk,dk->fpd", dpacked, w_in, preferred_element_type=jnp.float32)
    dhidden, dgain_vec = norm_bwd(hidden, inverse, gain_vec, dnormed)
    return (upstream + dhidden, dw_in, dw_out, dgain_vec, dtable_sum)


def fetch(conv_weight, proj_in, proj_out, time_weight):
    columns = (
        lax.all_gather(conv_weight.astype(jnp.bfloat16), "batch", axis=1, tiled=True),
        lax.all_gather(proj_in.astype(jnp.bfloat16), "batch", axis=1, tiled=True),
        lax.all_gather(proj_out.astype(jnp.bfloat16), "batch", axis=1, tiled=True),
        lax.all_gather(time_weight.astype(jnp.bfloat16), "batch", axis=1, tiled=True),
    )
    return (
        lax.all_gather(columns[0], "frame", axis=0, tiled=True),
        lax.all_gather(columns[1], "frame", axis=0, tiled=True),
        lax.all_gather(columns[2], "frame", axis=0, tiled=True),
        lax.all_gather(columns[3], "frame", axis=0, tiled=True),
    )


def reduce_rows(matrix_grads):
    row_parts = (
        lax.psum_scatter(matrix_grads[0], "frame", scatter_dimension=0, tiled=True),
        lax.psum_scatter(matrix_grads[1], "frame", scatter_dimension=0, tiled=True),
        lax.psum_scatter(matrix_grads[2], "frame", scatter_dimension=0, tiled=True),
        lax.psum_scatter(matrix_grads[3], "frame", scatter_dimension=0, tiled=True),
    )
    return (
        lax.psum_scatter(row_parts[0], "batch", scatter_dimension=1, tiled=True),
        lax.psum_scatter(row_parts[1], "batch", scatter_dimension=1, tiled=True),
        lax.psum_scatter(row_parts[2], "batch", scatter_dimension=1, tiled=True),
        lax.psum_scatter(row_parts[3], "batch", scatter_dimension=1, tiled=True),
    )


def adamw(weight, moment_one, moment_two, grad, clip_scale, step_rate):
    grad = grad * clip_scale
    moment_one = BETA_ONE * moment_one + (1.0 - BETA_ONE) * grad
    moment_two = BETA_TWO * moment_two + (1.0 - BETA_TWO) * grad * grad
    update = (
        moment_one
        / (1.0 - BETA_ONE**STEP)
        / (jnp.sqrt(moment_two / (1.0 - BETA_TWO**STEP)) + ADAM_EPS)
    )
    return (weight - step_rate * (update + DECAY * weight), moment_one, moment_two)


ROW_CONV = 576
ROW_GRAD = 704
ROW_ALL = 736
HALF = 352
PAIRS = 4
STEPS = 4
ROWS = 512
BLOCKS = 2
GAP = 272
NEVER = -1e30
MESH_ID = pl.DeviceIdType.MESH


def dot_nn(lhs, rhs):
    return jnp.dot(lhs, rhs, preferred_element_type=jnp.float32)


def dot_nt(lhs, rhs):
    return lax.dot_general(lhs, rhs, (((1,), (1,)), ((), ())), preferred_element_type=jnp.float32)


def dot_tn(lhs, rhs):
    return lax.dot_general(lhs, rhs, (((0,), (0,)), ((), ())), preferred_element_type=jnp.float32)


def low(values):
    return values.astype(jnp.bfloat16)


def rms(values, gain_row):
    inverse = lax.rsqrt(jnp.mean(values * values, -1, keepdims=True) + EPS_NORM)
    return values * inverse * gain_row, inverse


def rms_back(values, inverse, gain_row, upstream):
    scaled = upstream * gain_row
    unit = values * inverse
    mean = jnp.mean(unit * scaled, -1, keepdims=True)
    return inverse * (scaled - unit * mean), jnp.sum(upstream * unit, 0, keepdims=True)


def weave(block):
    first = block[:256].reshape(32, 1, 8, D)
    second = block[256:].reshape(32, 1, 8, D)
    return jnp.concatenate([first, second], 1).reshape(512, D)


def unweave(block):
    parts = block.reshape(32, 2, 8, D)
    return jnp.concatenate([parts[:, 0].reshape(256, D), parts[:, 1].reshape(256, D)], 0)


def tap_pieces(tap):
    start, stop = 256 * tap, 256 * tap + 256
    pieces = []
    while start < stop:
        block, offset = divmod(start, ROW_CONV)
        size = min(ROW_CONV - offset, stop - start)
        pieces.append((block // 2, block % 2, offset, size))
        start += size
    return pieces


def frames_total(count_ref):
    total = 0
    for micro in range(2):
        for group in range(4):
            total = total + count_ref[micro, group, 0]
    return total


def step_kernel(
    clean_ref,
    noise_ref,
    count_ref,
    steps_ref,
    conv_ref,
    pin_ref,
    pout_ref,
    time_ref,
    win_ref,
    wout_ref,
    gains_ref,
    rel_ref,
    grads_ref,
    vector_ref,
    squares_ref,
    dtime_ref,
    prob_far,
    wall,
    dslab,
    proj,
    outp,
    mine,
    ready,
    frames_in,
    eight,
    clip_ref,
    video_ref,
    table_ref,
    head_pad,
    hid_one,
    hid_two,
    inner_zero,
    dhid,
    pack_zero,
    mix_zero,
    spread_norm,
    pack_one,
    prob_one,
    mix_one,
    mix_back,
    dout_pix,
    stage,
    shift_fwd,
    shift_one,
    shift_two,
    act_one,
    act_two,
    acc_out,
    red_sib,
    red_a,
    red_b,
    red_c,
    red_d,
    red_z,
    part_z,
    final,
    final_recv,
    vec_acc,
    vec_recv,
    sq_acc,
    sq_recv,
    sem_sib,
    sem_zu,
    sem_zd,
    sem_x,
    sem_y,
    sem_xf,
    sem_yf,
    sem_n,
    sem_m,
    sem_dy,
    sem_dn,
    sem_red,
    sem_fin,
    sem_vec,
    sem_sq,
    sem_in,
    sem_prob,
):
    fr = lax.axis_index("frame")
    ba = lax.axis_index("batch")
    z, x = fr // 2, fr % 2
    y, c = ba // 2, ba % 2
    ox, oy, oc = 1 - x, 1 - y, 1 - c
    quarter = 2 * x + c
    sibling = (fr, 2 * y + oc)
    x_peer = (2 * z + ox, ba)
    y_peer = (fr, 2 * oy + c)
    xs_peer = (2 * z + ox, 2 * y + oc)
    z_ids = [(z + k) % 4 for k in (1, 2, 3)]
    z_peers = [(2 * k + x, ba) for k in z_ids]
    up_peer = (2 * jnp.minimum(z + 1, 3) + x, ba)
    down_peer = (2 * jnp.maximum(z - 1, 0) + x, ba)
    plane = [(2 * z + px, 2 * py + pc) for px, py, pc in (
        (x, y, oc), (x, oy, c), (x, oy, oc), (ox, y, c), (ox, y, oc), (ox, oy, c), (ox, oy, oc)
    )]
    group = [(sibling, 2 * x + oc), (x_peer, 2 * ox + c), (xs_peer, 2 * ox + oc)]

    def remote(src, dst, sems, send_at, recv_at, device):
        return pltpu.make_async_remote_copy(
            src_ref=src,
            dst_ref=dst,
            send_sem=sems.at[(0,) + send_at],
            recv_sem=sems.at[(1,) + recv_at],
            device_id=device,
            device_id_type=MESH_ID,
        )

    video = 4 * (z // 2) + 2 * y + z % 2
    in_dst = [(4 * (x if t == 0 else ox) + 2 * c + z // 2, 2 * y + z % 2) for t in range(2)]
    in_src = [(2 * quarter + (z // 2 if t == 0 else 1 - z // 2), 2 * y + z % 2) for t in range(2)]
    moves = [(dst[0] != fr) | (dst[1] != ba) for dst in in_dst]

    barrier = pltpu.get_barrier_semaphore()
    everyone = plane + z_peers
    for peer in everyone:
        pl.semaphore_signal(barrier, inc=1, device_id=peer, device_id_type=MESH_ID)
    for turn in range(2):

        @pl.when(moves[turn])
        def _(turn=turn):
            pl.semaphore_signal(barrier, inc=1, device_id=in_src[turn], device_id_type=MESH_ID)

    def spots(rows, columns, shift):
        row = lax.broadcasted_iota(jnp.int32, (rows, columns), 0)
        column = lax.broadcasted_iota(jnp.int32, (rows, columns), 1)
        return low(jnp.where(row + shift == column, 1.0, 0.0))

    narrow = spots(64, 128, 64 * c)
    conv_own = low(dot_tn(low(conv_ref[...]), narrow))
    pin_own = low(dot_nn(low(pin_ref[...]), spots(192, 384, 192 * c)))
    pout_own = low(dot_nn(low(pout_ref[...]), narrow))
    time_own = low(dot_nn(low(time_ref[...]), narrow))
    for half in range(2):
        rows = slice(32 * half, 32 * half + 32)
        ready[half, 0:ROW_CONV] = conv_own[ROW_CONV * half : ROW_CONV * half + ROW_CONV]
        for j in range(3):
            ready[half, ROW_CONV + 32 * j : ROW_CONV + 32 * j + 32] = pin_own[
                rows, 128 * j : 128 * j + 128
            ]
        ready[half, 672:704] = pout_own[rows]
        ready[half, 704:736] = time_own[rows]

    pl.semaphore_wait(
        barrier, len(everyone) + moves[0].astype(jnp.int32) + moves[1].astype(jnp.int32)
    )
    first = remote(ready.at[oc], mine, sem_vec, (11,), (11,), sibling)
    first.start()

    def input_copies(turn):
        micro = x if turn == 0 else ox
        return [
            remote(
                src.at[micro, 0],
                frames_in.at[x, k],
                sem_in,
                (turn, k),
                (turn, k),
                in_dst[turn],
            )
            for k, src in enumerate((clean_ref, noise_ref))
        ]

    for turn in range(2):

        @pl.when(moves[turn])
        def _(turn=turn):
            for copy in input_copies(turn):
                copy.start()

        @pl.when(jnp.logical_not(moves[turn]))
        def _(turn=turn):
            for k, src in enumerate((clean_ref, noise_ref)):
                frames_in[x, k] = src[x if turn == 0 else ox, 0]

    def arrive(dst, sems, at):
        remote(dst, dst, sems, at, at, sibling).wait_recv()

    def push(block, sems, at, device):
        remote(block, block, sems, at, at, device).start()

    parts = [pl.ds(0, 368), pl.ds(368, 368)]

    def to_sibling(row_z, row_x, row_y):
        at = (row_z, row_x, row_y)
        push(wall.at[row_y, 2 * row_z + row_x, c], sem_sib, at, sibling)

    def turn_row(turn):
        return jnp.where(turn <= z, z - turn, turn)

    def gather_one(turn):
        row_z = turn_row(turn)
        for k, part in enumerate(parts):
            block = wall.at[y, 2 * row_z + x, c, part]
            at = (row_z, k)
            if turn > 0:

                @pl.when(turn <= z)
                def _():
                    arrive(block, sem_zu, at)

                @pl.when(turn > z)
                def _():
                    arrive(block, sem_zd, at)

            @pl.when((turn <= z) & (z < 3))
            def _():
                push(block, sem_zu, at, up_peer)

            @pl.when(((turn > z) | (turn == 0)) & (z > 0))
            def _():
                push(block, sem_zd, at, down_peer)

            push(block, sem_x, at, x_peer)
            push(block, sem_y, at, y_peer)
        to_sibling(row_z, x, y)

    def gather_two(turn):
        row_z = turn_row(turn)
        from_x = [wall.at[y, 2 * row_z + ox, c, part] for part in parts]
        from_y = [wall.at[oy, 2 * row_z + x, c, part] for part in parts]
        arrive(from_x[0], sem_x, (row_z, 0))
        push(from_x[0], sem_yf, (row_z,), y_peer)
        arrive(from_y[0], sem_y, (row_z, 0))
        arrive(from_y[1], sem_y, (row_z, 1))
        push(from_y[1], sem_xf, (row_z,), x_peer)
        to_sibling(row_z, x, oy)
        arrive(from_x[1], sem_x, (row_z, 1))
        to_sibling(row_z, ox, y)

    def gather_three(row_z):
        arrive(wall.at[oy, 2 * row_z + ox, c, parts[0]], sem_yf, (row_z,))
        arrive(wall.at[oy, 2 * row_z + ox, c, parts[1]], sem_xf, (row_z,))
        to_sibling(row_z, ox, oy)

    def gather_four(row_z):
        for row_x in range(2):
            for row_y in range(2):
                arrive(wall.at[row_y, 2 * row_z + row_x, oc], sem_sib, (row_z, row_x, row_y))

    def gather_sent():
        part = wall.at[y, fr, c, parts[0]]

        def sent(block, sems, at):
            remote(block, block, sems, at, at, sibling).wait_send()

        for row_z in range(4):
            for k in range(2):
                sent(part, sem_x, (row_z, k))
                sent(part, sem_y, (row_z, k))

                @pl.when((row_z <= z) & (z < 3))
                def _():
                    sent(part, sem_zu, (row_z, k))

                @pl.when((row_z >= z) & (z > 0))
                def _():
                    sent(part, sem_zd, (row_z, k))

            sent(part, sem_xf, (row_z,))
            sent(part, sem_yf, (row_z,))
            for row_x in range(2):
                for row_y in range(2):
                    sent(wall.at[y, fr, c], sem_sib, (row_z, row_x, row_y))

    zeros_row = jnp.zeros((3, 16, D), jnp.bfloat16)
    for frame in range(9):
        shift_one[:, GAP * frame : GAP * frame + 16, :] = zeros_row
        shift_two[:, GAP * frame : GAP * frame + 16, :] = zeros_row
    for frame in range(ROWS // 256 + 1):
        shift_fwd[:, GAP * frame : GAP * frame + 16, :] = zeros_row
    vec_acc[...] = jnp.zeros_like(vec_acc)
    acc_out[...] = jnp.zeros_like(acc_out)
    eight[...] = jnp.zeros_like(eight)
    head_pad[...] = jnp.zeros_like(head_pad)
    head_pad[0:3, :] = wout_ref[...]
    first.wait()
    wall[y, fr, c] = ready[c] + mine[...]

    gather_one(0)

    count = count_ref[z // 2, 2 * y + z % 2, 0]

    def table_rows(part, carry):
        rows = pl.ds(pl.multiple_of(32 * part, 32), 32)
        row = lax.broadcasted_iota(jnp.int32, (32, 256), 0) + 32 * part
        column = lax.broadcasted_iota(jnp.int32, (32, 256), 1)
        away = column // 8 - row // 8
        bucket = jnp.minimum(jnp.abs(away), 15) + jnp.where(away > 0, 16, 0)
        usable = (row % 8 == column % 8) & (column // 8 < count)
        bucket = jnp.where(usable, bucket, -1)
        biases = [jnp.full((32, 256), NEVER, jnp.float32) for _ in range(HEADS)]
        for k in range(32):
            here = bucket == k
            biases = [jnp.where(here, rel_ref[h, k], biases[h]) for h in range(HEADS)]
        for h in range(HEADS):
            table_ref[h, rows, :] = biases[h]
        return carry

    gather_one(1)
    gather_two(0)
    lax.fori_loop(0, 4, table_rows, 0)
    gather_one(2)
    gather_two(1)
    lax.fori_loop(4, 8, table_rows, 0)
    gather_one(3)
    gather_two(2)

    for turn in range(2):

        @pl.when(moves[turn])
        def _(turn=turn):
            for copy in input_copies(turn):
                copy.wait_send()
                copy.wait_recv()

    row = lax.broadcasted_iota(jnp.int32, (8, 384), 0)
    lane = lax.broadcasted_iota(jnp.int32, (8, 384), 1)
    levels = jnp.zeros((8, 384), jnp.int32)
    for k in range(8):
        levels = jnp.where(row == k, steps_ref[k // 4, k % 4, 0], levels)
    levels = levels.astype(jnp.float32)
    half_width = D // 2
    frequency = jnp.exp(-math.log(10000.0) * (lane % half_width).astype(jnp.float32) / half_width)
    angles = jnp.where(
        lane < D, levels * frequency, 0.5 * math.pi * (levels + 1.0) / (TSTEPS + 1.0)
    )
    cosines = jnp.cos(angles)
    embedding = low(jnp.where(lane < half_width, jnp.sin(angles), cosines)).astype(jnp.float32)
    alpha_bar = cosines * cosines
    alphas = jnp.where(lane == D, jnp.sqrt(alpha_bar), jnp.sqrt(1.0 - alpha_bar))
    video_ref[...] = jnp.where(lane < D, embedding, alphas)
    video_row = video_ref[pl.ds(video, 1), :]
    keep, add = video_row[:, 256:257], video_row[:, 257:258]
    place = spots(8, 128, 0).astype(jnp.float32)
    for frame in range(8):
        for channel in range(3):
            here = (channel, slice(frame % 4, frame % 4 + 1))
            noise_row = frames_in[(frame // 4, 1) + here]
            eight[frame, channel : channel + 1] = noise_row
            eight[frame, 3 + channel : 4 + channel] = (
                keep * frames_in[(frame // 4, 0) + here] + add * noise_row
            )
        clip_ref[256 * frame : 256 * frame + 256, :] = lax.dot_general(
            eight[frame],
            place,
            (((0,), (0,)), ((), ())),
            precision=HIGH,
            preferred_element_type=jnp.float32,
        )

    gather_two(3)
    gather_three(0)
    gather_four(0)

    def unpack(rows_of):
        for row_y in range(2):
            for row in rows_of:
                for half in range(2):
                    block = wall.at[row_y, row, half]
                    rows = slice(64 * (row % 4) + 32 * half, 64 * (row % 4) + 32 * half + 32)
                    for j in range(3):
                        cols = slice(384 * row_y + 128 * j, 384 * row_y + 128 * j + 128)
                        proj[row // 4, rows, cols] = block[
                            ROW_CONV + 32 * j : ROW_CONV + 32 * j + 32
                        ]
                    outp[row // 4, rows, 128 * row_y : 128 * row_y + 128] = block[672:704]

    def time_tile(layer):
        rows = []
        for row in range(4 * layer, 4 * layer + 4):
            for half in range(2):
                rows.append(
                    jnp.concatenate(
                        [wall[0, row, half, 704:736, :], wall[1, row, half, 704:736, :]], 1
                    )
                )
        return jnp.concatenate(rows, 0)

    def conv_tile(kernel, tap):
        rows = []
        for row, half, offset, size in tap_pieces(tap):
            block = (2 * kernel + row, half)
            rows.append(
                jnp.concatenate(
                    [
                        wall[(0,) + block + (slice(offset, offset + size),)],
                        wall[(1,) + block + (slice(offset, offset + size),)],
                    ],
                    1,
                )
            )
        return rows[0] if len(rows) == 1 else jnp.concatenate(rows, 0)

    embed = low(jnp.broadcast_to(video_row[:, 0:D], (16, D)))

    def time_project(layer):
        pre = dot_nn(embed, time_tile(layer))[0:1]
        return pre, pre * jax.nn.sigmoid(pre)

    gain = [gains_ref[k : k + 1, :] for k in range(7)]
    column = lax.broadcasted_iota(jnp.int32, (1, D), 1)
    heads = [
        jnp.where(column // 64 == h, 1.0, 0.0).astype(jnp.bfloat16) for h in range(HEADS)
    ]
    pixel_x = lax.broadcasted_iota(jnp.int32, (256, 1), 0) % SIDE
    not_left = jnp.where(pixel_x != 0, 1.0, 0.0)
    not_right = jnp.where(pixel_x != SIDE - 1, 1.0, 0.0)

    def put_shifts(dst, bases, values):
        for k, base in enumerate(bases):
            frame = values[256 * k : 256 * k + 256]
            rows = pl.ds(base, 256)
            dst[0, rows, :] = low(pltpu.roll(frame, 1, 0) * not_left)
            dst[1, rows, :] = low(frame)
            dst[2, rows, :] = low(pltpu.roll(frame, 255, 0) * not_right)

    def aligned(value, multiple):
        return value if isinstance(value, int) else pl.multiple_of(value, multiple)

    def shifted(src, bases, dy, dx):
        return jnp.concatenate(
            [src[dx, pl.ds(aligned(base + 16 * (dy - 1), 16), 256), :] for base in bases], 0
        )

    def conv(src, bases, kernel):
        totals = []
        for base in bases:
            total = None
            for tap in range(9):
                part = dot_nn(shifted(src, [base], tap // 3, tap % 3), conv_tile(kernel, tap))
                total = part if total is None else total + part
            totals.append(total)
        return jnp.concatenate(totals, 0)

    def conv_back(src, bases, kernel):
        totals = []
        for base in bases:
            total = None
            for tap in range(9):
                here = shifted(src, [base], 2 - tap // 3, 2 - tap % 3)
                part = dot_nt(here, conv_tile(kernel, tap))
                total = part if total is None else total + part
            totals.append(total)
        return jnp.concatenate(totals, 0)

    def conv_grad(act, src, kernel, dst, first_row):
        for tap in range(9):
            grads = shifted(src, [16 + GAP * k for k in range(8)], 2 - tap // 3, 2 - tap % 3)
            total = low(dot_nn(act[...], grads))
            start = 0
            for row, half, offset, size in tap_pieces(tap):
                for row_y in range(2):
                    dst[row_y, first_row + row, half, offset : offset + size] = total[
                        start : start + size, 128 * row_y : 128 * row_y + 128
                    ]
                start += size

    def put_proj_grad(layer, din, dout, dst, first_row):
        for row in range(4):
            for half in range(2):
                rows = slice(64 * row + 32 * half, 64 * row + 32 * half + 32)
                for row_y in range(2):
                    for j in range(3):
                        cols = slice(384 * row_y + 128 * j, 384 * row_y + 128 * j + 128)
                        dst[
                            row_y,
                            first_row + row,
                            half,
                            ROW_CONV + 32 * j : ROW_CONV + 32 * j + 32,
                        ] = din[rows, cols]
                    dst[row_y, first_row + row, half, 672:704] = dout[
                        rows, 128 * row_y : 128 * row_y + 128
                    ]

    def softmax(scores):
        powers = jnp.exp(scores - jnp.max(scores, -1, keepdims=True))
        return low(powers * (1.0 / jnp.sum(powers, -1, keepdims=True)))

    def attend(query, key, value, bias):
        probs = []
        for h in range(HEADS):
            scores = dot_nt(query * heads[h], key) * 0.125
            if bias is not None:
                scores = scores + bias[h]
            probs.append(softmax(scores))
        values = jnp.concatenate([value * heads[h] for h in range(HEADS)], 0)
        return low(dot_nn(jnp.concatenate(probs, 1), values)), probs

    def attend_back(query, key, value, dmix, probs, add_bias):
        dmix_t, query_t = dmix.T, query.T
        dscores, dkey_t, dvalue_t = [], [], []
        for h in range(HEADS):
            prob_low = probs(h)
            prob = prob_low.astype(jnp.float32)
            dprob = dot_nt(dmix * heads[h], value)
            dscore = prob * (dprob - jnp.sum(prob * dprob, -1, keepdims=True))
            if add_bias is not None:
                add_bias(h, dscore)
            dscore_low = low(dscore)
            dscores.append(dscore_low)
            rows = slice(64 * h, 64 * h + 64)
            dvalue_t.append(dot_nn(dmix_t[rows], prob_low))
            dkey_t.append(dot_nn(query_t[rows], dscore_low))
        keys = jnp.concatenate([key * heads[h] for h in range(HEADS)], 0)
        dquery = low(dot_nn(jnp.concatenate(dscores, 1), keys) * 0.125)
        dkey = low(jnp.concatenate(dkey_t, 0) * 0.125).T
        dvalue = low(jnp.concatenate(dvalue_t, 0)).T
        return jnp.concatenate([dquery, dkey, dvalue], 1)

    def add_row(row, value):
        vec_acc[row : row + 1, :] += value

    def embed_input(rows):
        clip = clip_ref[rows, :]
        total = None
        for channel in range(3):
            part = clip[:, 3 + channel : 4 + channel] * win_ref[channel : channel + 1, :]
            total = part if total is None else total + part
        return total, clip

    fwd_bases = [16 + GAP * k for k in range(ROWS // 256)]

    frames = range(ROWS // 256)

    def step_rows(step):
        return pl.ds(pl.multiple_of(step * ROWS, ROWS), ROWS)

    def step_bases(step):
        return [pl.multiple_of(16 + GAP * (len(frames) * step + k), 16) for k in frames]

    def put_stage(step, values):
        for k in range(len(frames) // 2):
            pair = len(frames) // 2 * step + k
            woven = low(weave(values[512 * k : 512 * k + 512]))
            stage[pl.ds(32 * pair, 32)] = woven.reshape(32, 16, D)

    def from_pairs(step, src):
        pairs = len(frames) // 2
        return src[pl.ds(pairs * step, pairs)].reshape(ROWS, D)

    def unweave_all(values):
        return jnp.concatenate(
            [unweave(values[512 * k : 512 * k + 512]) for k in range(len(frames) // 2)], 0
        )

    def send_pair(pair, dst, sems):
        for k, (peer, part) in enumerate(group):
            remote(
                stage.at[pl.ds(32 * pair + 8 * part, 8)],
                dst.at[:, 4 * quarter + pair],
                sems,
                (pair, k),
                (pair, k),
                peer,
            ).start()
        dst[:, 4 * quarter + pair] = stage[pl.ds(32 * pair + 8 * quarter, 8)]

    def wait_pairs(dst, sems):
        for pair in range(PAIRS):
            for k, (peer, part) in enumerate(group):
                copy = remote(
                    stage.at[pl.ds(32 * pair + 8 * part, 8)],
                    dst.at[:, 4 * part + pair],
                    sems,
                    (pair, k),
                    (pair, k),
                    peer,
                )
                copy.wait_send()
                copy.wait_recv()

    def block_tiles(src, block, part):
        return src.at[pl.ds(16 * block + 4 * part, 4)]

    def send_block(block, src, dst, sems):
        for k, (peer, part) in enumerate(group):
            remote(
                block_tiles(src, block, part),
                dst.at[:, quarter, block],
                sems,
                (block, k),
                (block, k),
                peer,
            ).start()
        dst[:, quarter, block] = block_tiles(src, block, quarter)[...]

    def wait_blocks(src, dst, sems):
        for block in range(8):
            for k, (peer, part) in enumerate(group):
                copy = remote(
                    block_tiles(src, block, part),
                    dst.at[:, part, block],
                    sems,
                    (block, k),
                    (block, k),
                    peer,
                )
                copy.wait_send()
                copy.wait_recv()

    def at_step(step, when, work):
        @pl.when(step == when)
        def _():
            work()

    def prob_away(step):
        some = pl.ds(len(frames) * step, len(frames))
        return pltpu.make_async_copy(prob_one.at[some], prob_far.at[some], sem_prob.at[0, step])

    def prob_home(step):
        some = pl.ds(len(frames) * step, len(frames))
        return pltpu.make_async_copy(prob_far.at[some], prob_one.at[some], sem_prob.at[1, step])

    def first_conv(step, carry):
        rows = step_rows(step)
        hidden, _ = embed_input(rows)
        normed, _ = rms(hidden, gain[0])
        put_shifts(shift_fwd, fwd_bases, normed * jax.nn.sigmoid(normed))
        inner_zero[rows, :] = conv(shift_fwd, fwd_bases, 0)
        at_step(step, 0, lambda: gather_three(1))
        at_step(step, 2, lambda: gather_three(2))
        at_step(step, 3, lambda: gather_three(3))
        return carry

    lax.fori_loop(0, STEPS, first_conv, 0)
    gather_four(1)
    unpack(range(4))
    pre_zero, bias_zero = time_project(0)

    def forward_step(step, carry):
        rows = step_rows(step)
        hidden, _ = embed_input(rows)
        inner = inner_zero[rows, :] + bias_zero
        inner_zero[rows, :] = inner
        normed, _ = rms(inner, gain[1])
        put_shifts(shift_fwd, fwd_bases, normed * jax.nn.sigmoid(normed))
        hidden = hidden + conv(shift_fwd, fwd_bases, 1)
        hid_one[rows, :] = hidden
        normed, _ = rms(hidden, gain[2])
        packed = low(dot_nn(low(normed), proj[0]))
        pack_zero[rows, :] = packed
        mixed = []
        for k in frames:
            part = packed[256 * k : 256 * k + 256]
            one, probs = attend(part[:, :D], part[:, D : 2 * D], part[:, 2 * D :], None)
            for h in range(HEADS):
                prob_one[len(frames) * step + k, h] = probs[h]
            mixed.append(one)
        prob_away(step).start()
        mixed = jnp.concatenate(mixed, 0)
        mix_zero[rows, :] = mixed
        hidden = hidden + dot_nn(mixed, outp[0])
        hid_two[rows, :] = hidden
        normed, _ = rms(hidden, gain[3])
        put_stage(step, normed)
        for k in range(len(frames) // 2):
            send_pair(len(frames) // 2 * step + k, spread_norm, sem_n)
        return carry

    lax.fori_loop(0, STEPS, forward_step, 0)
    gather_four(2)
    gather_four(3)
    gather_sent()
    unpack(range(4, 8))
    pre_one, bias_one = time_project(1)
    wait_pairs(spread_norm, sem_n)
    for step in range(STEPS):
        prob_away(step).wait()

    def temporal_blocks(turn, carry):
        blocks = [BLOCKS * turn + k for k in range(BLOCKS)]
        tables = [table_ref[h] for h in range(HEADS)]
        packs = [
            low(dot_nn(spread_norm[block].reshape(256, D), proj[1])) for block in blocks
        ]
        results = [
            attend(packed[:, :D], packed[:, D : 2 * D], packed[:, 2 * D :], tables)
            for packed in packs
        ]
        for block, packed, (mixed, probs) in zip(blocks, packs, results):
            pack_one[block] = packed
            for h in range(HEADS):
                prob_one[block, h] = probs[h]
            mix_one[pl.ds(16 * block, 16)] = mixed.reshape(16, 16, D)
        for block in blocks:
            send_block(block, mix_one, mix_back, sem_m)
        return carry

    lax.fori_loop(0, 8 // BLOCKS, temporal_blocks, 0)
    wait_blocks(mix_one, mix_back, sem_m)

    pixel_total = jnp.full((1, 1), frames_total(count_ref), jnp.int32).astype(jnp.float32) * 256.0
    scale = 2.0 / pixel_total
    wout_low = low(wout_ref[...]).astype(jnp.float32)

    def last_step(step, carry):
        rows = step_rows(step)
        bases = step_bases(step)
        lanes = step_rows(step)
        hidden = hid_two[rows, :] + unweave_all(dot_nn(from_pairs(step, mix_back), outp[1]))
        normed, inverse = rms(hidden, gain[4])
        sig = jax.nn.sigmoid(normed)
        acts = normed * sig
        put_shifts(shift_fwd, fwd_bases, acts)
        act_one[:, lanes] = low(acts).T
        slope_one = sig * (1.0 + normed * (1.0 - sig))
        inner = conv(shift_fwd, fwd_bases, 2) + bias_one
        normed_two, inverse_two = rms(inner, gain[5])
        sig_two = jax.nn.sigmoid(normed_two)
        acts_two = normed_two * sig_two
        put_shifts(shift_fwd, fwd_bases, acts_two)
        act_two[:, lanes] = low(acts_two).T
        slope_two = sig_two * (1.0 + normed_two * (1.0 - sig_two))
        last = hidden + conv(shift_fwd, fwd_bases, 3)
        normed, inverse_six = rms(last, gain[6])
        normed_low = low(normed)
        pred = dot_nt(normed_low, low(head_pad[...]))
        clip = clip_ref[rows, :]
        frame_id = lax.broadcasted_iota(jnp.int32, (ROWS, 128), 0) // 256
        frame_id = frame_id + (8 * quarter + len(frames) * step)
        valid = jnp.where(frame_id < count, 1.0, 0.0)
        lane = lax.broadcasted_iota(jnp.int32, (ROWS, 128), 1)
        error = jnp.where(lane < 3, pred - clip, 0.0)
        weighted = error * valid
        vec_acc[7:8, 0:128] += jnp.sum(weighted * error, 0, keepdims=True)
        dpred = weighted * scale
        dpred_hi = low(dpred)
        dpred_lo = low(dpred - dpred_hi.astype(jnp.float32))
        acc_out[...] += dot_tn(dpred_hi, normed_low) + dot_tn(dpred_lo, normed_low)
        dnormed = None
        for channel in range(3):
            part = dpred[:, channel : channel + 1] * wout_low[channel : channel + 1, :]
            dnormed = part if dnormed is None else dnormed + part
        dlast, dgain = rms_back(last, inverse_six, gain[6], dnormed)
        add_row(6, dgain)
        put_shifts(shift_two, bases, low(dlast).astype(jnp.float32))
        dnormed = conv_back(shift_two, bases, 3) * slope_two
        dinner, dgain = rms_back(inner, inverse_two, gain[5], dnormed)
        add_row(5, dgain)
        add_row(15, jnp.sum(dinner, 0, keepdims=True))
        put_shifts(shift_one, bases, low(dinner).astype(jnp.float32))
        dnormed = conv_back(shift_one, bases, 2) * slope_one
        dhidden, dgain = rms_back(hidden, inverse, gain[4], dnormed)
        add_row(4, dgain)
        dhidden = dhidden + dlast
        dhid[rows, :] = dhidden
        put_stage(step, dhidden)
        for k in range(len(frames) // 2):
            send_pair(len(frames) // 2 * step + k, dout_pix, sem_dy)
        return carry

    lax.fori_loop(0, STEPS, last_step, 0)
    conv_grad(act_two, shift_two, 3, wall, 6)
    conv_grad(act_one, shift_one, 2, wall, 4)
    wait_pairs(dout_pix, sem_dy)

    bias_acc = table_ref
    bias_acc[...] = jnp.zeros_like(bias_acc)

    def temporal_back(turn, carry):
        blocks = [BLOCKS * turn + k for k in range(BLOCKS)]
        sums = [[] for _ in range(HEADS)]
        results = []
        for block in blocks:
            dmix = low(dot_nt(dout_pix[block].reshape(256, D), outp[1]))
            packed = pack_one[block]
            results.append(
                attend_back(
                    packed[:, :D],
                    packed[:, D : 2 * D],
                    packed[:, 2 * D :],
                    dmix,
                    lambda h, block=block: prob_one[block, h],
                    lambda h, dscore: sums[h].append(dscore),
                )
            )
        for h in range(HEADS):
            bias_acc[h] += sum(sums[h][1:], sums[h][0])
        dnorms = [low(dot_nt(dpacked, proj[1])) for dpacked in results]
        for block, dpacked, dnorm in zip(blocks, results, dnorms):
            pack_one[block] = dpacked
            stage[pl.ds(16 * block, 16)] = dnorm.reshape(16, 16, D)
        for block in blocks:
            send_block(block, stage, mix_back, sem_dn)
        return carry

    lax.fori_loop(0, 8 // BLOCKS, temporal_back, 0)
    for step in range(STEPS):
        prob_home(step).start()
    flat = (2048, D)
    dout_one = low(dot_tn(mix_one[...].reshape(flat), dout_pix[...].reshape(flat)))
    din_one = low(dot_tn(spread_norm[...].reshape(flat), pack_one[...].reshape(2048, 3 * D)))
    put_proj_grad(1, din_one, dout_one, wall, 4)
    wait_blocks(stage, mix_back, sem_dn)

    def slab(k):
        return (wall, 2 * k) if k >= 2 else (dslab, 2 * k)

    top, low_half = pl.ds(0, HALF), pl.ds(HALF, HALF)

    def red_one(k):
        src, row = slab(k)
        return remote(
            src.at[:, pl.ds(row, 2), oc, pl.ds(0, ROW_GRAD)], red_sib.at[k], sem_red, (k, 0), (k, 0), sibling
        )

    def red_two(k):
        src, row = slab(k)
        return (
            remote(src.at[:, row + ox, c, top], red_a.at[k], sem_red, (k, 1), (k, 1), x_peer),
            remote(src.at[oy, pl.ds(row, 2), c, low_half], red_b.at[k], sem_red, (k, 2), (k, 2), y_peer),
        )

    def red_three(k):
        src, row = slab(k)
        return (
            remote(src.at[oy, row + x, c, top], red_c.at[k], sem_red, (k, 3), (k, 3), y_peer),
            remote(src.at[y, row + ox, c, low_half], red_d.at[k], sem_red, (k, 4), (k, 4), x_peer),
        )

    def both(left, right):
        return low(left.astype(jnp.float32) + right.astype(jnp.float32))

    def finish(copies):
        for copy in copies:
            copy.wait_send()
            copy.wait_recv()

    def add_one(k):
        src, row = slab(k)
        for row_y in range(2):
            for row_x in range(2):
                src[row_y, row + row_x, c, 0:ROW_GRAD] = both(
                    src[row_y, row + row_x, c, 0:ROW_GRAD], red_sib[k, row_y, row_x]
                )

    def add_two(k):
        src, row = slab(k)
        for part in range(2):
            src[part, row + x, c, 0:HALF] = both(src[part, row + x, c, 0:HALF], red_a[k, part])
            src[y, row + part, c, HALF:ROW_GRAD] = both(
                src[y, row + part, c, HALF:ROW_GRAD], red_b[k, part]
            )

    def add_three(k):
        src, row = slab(k)
        part_z[k, 0:HALF] = both(src[y, row + x, c, 0:HALF], red_c[k])
        part_z[k, HALF:ROW_GRAD] = both(src[y, row + x, c, HALF:ROW_GRAD], red_d[k])

    def z_copy(k):
        slot = (z + 3 - k) % 4
        return remote(part_z.at[k], red_z.at[slot], sem_fin, (k,), (slot,), (2 * k + x, ba))

    def send_z(k):
        @pl.when(z != k)
        def _():
            z_copy(k).start()

    def start_all(copies):
        for copy in copies:
            copy.start()

    def spatial_back(step, carry):
        rows = step_rows(step)
        bases = step_bases(step)
        lanes = step_rows(step)
        dnormed = unweave_all(from_pairs(step, mix_back).astype(jnp.float32))
        hidden = hid_two[rows, :]
        _, inverse = rms(hidden, gain[3])
        dhidden, dgain = rms_back(hidden, inverse, gain[3], dnormed)
        add_row(3, dgain)
        dhidden = dhidden + dhid[rows, :]
        grad_low = low(dhidden)
        dout_pix[pl.ds(len(frames) * step, len(frames))] = grad_low.reshape(len(frames), 16, 16, D)
        dmix = low(dot_nt(grad_low, outp[0]))
        packed = pack_zero[rows, :]
        dpacked = []
        prob_home(step).wait()
        for k in frames:
            part = packed[256 * k : 256 * k + 256]
            dpacked.append(
                attend_back(
                    part[:, :D],
                    part[:, D : 2 * D],
                    part[:, 2 * D :],
                    dmix[256 * k : 256 * k + 256],
                    lambda h, k=k: prob_one[len(frames) * step + k, h],
                    None,
                )
            )
        dpacked = jnp.concatenate(dpacked, 0)
        pack_zero[rows, :] = dpacked
        hidden = hid_one[rows, :]
        normed, inverse = rms(hidden, gain[2])
        spread_norm[pl.ds(len(frames) * step, len(frames))] = low(normed).reshape(
            len(frames), 16, 16, D
        )
        dnormed = dot_nt(dpacked, proj[0])
        dprev, dgain = rms_back(hidden, inverse, gain[2], dnormed)
        add_row(2, dgain)
        dhidden = dhidden + dprev
        dhid[rows, :] = dhidden
        put_shifts(shift_two, bases, low(dhidden).astype(jnp.float32))
        normed, _ = rms(inner_zero[rows, :], gain[1])
        act_two[:, lanes] = low(normed * jax.nn.sigmoid(normed)).T
        at_step(step, 1, lambda: one_to_two(3))
        at_step(step, 2, lambda: one_to_two(2))
        at_step(step, 3, lambda: two_to_three(3))
        return carry

    def one_to_two(k):
        finish([red_one(k)])
        add_one(k)
        start_all(red_two(k))

    def two_to_three(k):
        finish(red_two(k))
        add_two(k)
        start_all(red_three(k))

    def three_to_z(k):
        finish(red_three(k))
        add_three(k)
        send_z(k)

    start_all([red_one(3), red_one(2)])
    lax.fori_loop(0, STEPS, spatial_back, 0)
    two_to_three(2)
    din_zero = low(dot_tn(spread_norm[...].reshape(flat), pack_zero[...]))
    dout_zero = low(dot_tn(mix_zero[...], dout_pix[...].reshape(flat)))
    put_proj_grad(0, din_zero, dout_zero, dslab, 0)
    conv_grad(act_two, shift_two, 1, dslab, 2)
    start_all([red_one(1)])

    def first_back(step, carry):
        rows = step_rows(step)
        bases = step_bases(step)
        lanes = step_rows(step)
        inner = inner_zero[rows, :]
        normed, inverse = rms(inner, gain[1])
        sig = jax.nn.sigmoid(normed)
        dnormed = conv_back(shift_two, bases, 1) * (sig * (1.0 + normed * (1.0 - sig)))
        dinner, dgain = rms_back(inner, inverse, gain[1], dnormed)
        add_row(1, dgain)
        add_row(14, jnp.sum(dinner, 0, keepdims=True))
        put_shifts(shift_one, bases, low(dinner).astype(jnp.float32))
        hidden, _ = embed_input(rows)
        normed, _ = rms(hidden, gain[0])
        act_one[:, lanes] = low(normed * jax.nn.sigmoid(normed)).T
        at_step(step, 0, lambda: three_to_z(3))
        at_step(step, 1, lambda: one_to_two(1))
        at_step(step, 2, lambda: three_to_z(2))
        return carry

    lax.fori_loop(0, STEPS, first_back, 0)
    conv_grad(act_one, shift_one, 0, dslab, 0)
    start_all([red_one(0)])
    two_to_three(1)

    def input_back(step, carry):
        rows = step_rows(step)
        bases = step_bases(step)
        hidden, clip = embed_input(rows)
        normed, inverse = rms(hidden, gain[0])
        sig = jax.nn.sigmoid(normed)
        dnormed = conv_back(shift_one, bases, 0) * (sig * (1.0 + normed * (1.0 - sig)))
        dhidden, dgain = rms_back(hidden, inverse, gain[0], dnormed)
        add_row(0, dgain)
        dhidden = dhidden + dhid[rows, :]
        for channel in range(3):
            add_row(
                8 + channel,
                jnp.sum(clip[:, 3 + channel : 4 + channel] * dhidden, 0, keepdims=True),
            )
        at_step(step, 0, lambda: one_to_two(0))
        at_step(step, 1, lambda: three_to_z(1))
        at_step(step, 3, lambda: two_to_three(0))
        return carry

    lax.fori_loop(0, STEPS, input_back, 0)
    vec_acc[11:14, :] = acc_out[0:3, :]
    fold = lax.broadcasted_iota(jnp.int32, (256, 128), 0) // 8
    fold_lane = lax.broadcasted_iota(jnp.int32, (256, 128), 1)
    left = jnp.where(fold == fold_lane, 1.0, 0.0)
    table = None
    for h in range(HEADS):
        right = jnp.where(fold + 32 * h == fold_lane, 1.0, 0.0)
        wide = lax.dot_general(
            bias_acc[h], right, (((1,), (0,)), ((), ())), precision=HIGH, preferred_element_type=jnp.float32
        )
        part = lax.dot_general(
            left, wide, (((0,), (0,)), ((), ())), precision=HIGH, preferred_element_type=jnp.float32
        )
        table = part if table is None else table + part
    away = fold_lane[0:32] % 32 - lax.broadcasted_iota(jnp.int32, (32, 128), 0)
    bucket = jnp.minimum(jnp.abs(away), 15) + jnp.where(away > 0, 16, 0)
    bucket_rows = lax.broadcasted_iota(jnp.int32, (32, 128), 0)
    by_bucket = jnp.zeros((32, 128), jnp.float32)
    for k in range(32):
        one = jnp.sum(jnp.where(bucket == k, table[0:32], 0.0), 0, keepdims=True)
        by_bucket = jnp.where(bucket_rows == k, one, by_bucket)
    head_row = lax.broadcasted_iota(jnp.int32, (8, 128), 0)
    head_lane = lax.broadcasted_iota(jnp.int32, (8, 128), 1)
    pick = jnp.where(head_lane // 32 == head_row, 1.0, 0.0)
    table_sum = lax.dot_general(
        pick, by_bucket, (((1,), (1,)), ((), ())), precision=HIGH, preferred_element_type=jnp.float32
    )
    vec_acc[32:40, 0:32] = table_sum
    row_ids = lax.broadcasted_iota(jnp.int32, (16, D), 0)
    slots = jnp.zeros((16, D), jnp.float32)
    for layer in range(2):
        pre = (pre_zero, pre_one)[layer]
        sig = jax.nn.sigmoid(pre)
        dpre = vec_acc[14 + layer : 15 + layer, :] * (sig * (1.0 + pre * (1.0 - sig)))
        slots = jnp.where(row_ids == 8 * layer + video, dpre, slots)
    vec_acc[16:32, :] = slots

    spot = 4 * x + 2 * y + c

    def plane_copies(values, received, sems):
        return [
            remote(values, received.at[spot], sems, (k,), (spot,), peer)
            for k, peer in enumerate(plane)
        ]

    def plane_total(values, received, sems):
        for px, py, pc in (
            (x, y, oc), (x, oy, c), (x, oy, oc), (ox, y, c), (ox, y, oc), (ox, oy, c), (ox, oy, oc)
        ):
            slot = 4 * px + 2 * py + pc
            remote(values, received.at[slot], sems, (0,), (slot,), sibling).wait_recv()
        for copy in plane_copies(values, received, sems):
            copy.wait_send()
        received[spot] = values[...]
        total = received[0]
        for k in range(1, 8):
            total = total + received[k]
        values[...] = total

    def z_total_copies(values, received, sems):
        return [
            remote(values, received.at[8 + 2 - k], sems, (8 + k,), (8 + 2 - k,), peer)
            for k, peer in enumerate(z_peers)
        ]

    def z_total(values, received, sems):
        finish(z_total_copies(values, received, sems))
        return (values[...] + received[9]) + (received[8] + received[10])

    start_all(plane_copies(vec_acc, vec_recv, sem_vec))
    three_to_z(0)
    plane_total(vec_acc, vec_recv, sem_vec)
    start_all(z_total_copies(vec_acc, vec_recv, sem_vec))
    vector = z_total(vec_acc, vec_recv, sem_vec)
    vector_ref[...] = vector
    small = jnp.sum(vector[0:7] * vector[0:7]) + jnp.sum(vector[8:14] * vector[8:14])
    small = small + jnp.sum(vector[32:36, 0:32] * vector[32:36, 0:32])
    for layer in range(2):
        dtime = lax.dot_general(
            video_ref[:, 0:D],
            vector[16 + 8 * layer : 24 + 8 * layer],
            (((0,), (0,)), ((), ())),
            precision=HIGH,
            preferred_element_type=jnp.float32,
        )
        dtime_ref[layer] = dtime
        small = small + jnp.sum(dtime * dtime)
    total = part_z[z].astype(jnp.float32)
    for slot in range(3):
        arrive(red_z.at[slot], sem_fin, (slot,))
        total = total + red_z[slot].astype(jnp.float32)
    grads_ref[c] = total
    final[...] = total
    own_sums = remote(final, final_recv, sem_fin, (4,), (4,), sibling)
    own_sums.start()
    square = jnp.sum(jnp.sum(total * total, 0, keepdims=True), 1, keepdims=True)
    sq_acc[...] = jnp.broadcast_to(square, (8, 128))
    start_all(plane_copies(sq_acc, sq_recv, sem_sq))
    plane_total(sq_acc, sq_recv, sem_sq)
    start_all(z_total_copies(sq_acc, sq_recv, sem_sq))
    own_sums.wait_send()
    arrive(final_recv, sem_fin, (4,))
    grads_ref[oc] = final_recv[...]
    for k in range(4):

        @pl.when(z != k)
        def _():
            z_copy(k).wait_send()

    squares_ref[...] = z_total(sq_acc, sq_recv, sem_sq) + small


def dot_exact(lhs, rhs, dims):
    return lax.dot_general(
        lhs, rhs, (dims, ((), ())), precision=HIGH, preferred_element_type=jnp.float32
    )


def update_kernel(*refs):
    sums_ref, vector_ref, squares_ref, dtime_ref, count_ref = refs[:5]
    state, outs = refs[5:29], refs[29:]
    fr = lax.axis_index("frame")
    ba = lax.axis_index("batch")
    c = ba % 2

    def spots(rows, columns, shift):
        row = lax.broadcasted_iota(jnp.int32, (rows, columns), 0)
        column = lax.broadcasted_iota(jnp.int32, (rows, columns), 1)
        return jnp.where(row + shift == column, 1.0, 0.0)

    norm = jnp.sqrt(squares_ref[0:1, 0:1])
    clip_scale = CLIP / jnp.maximum(norm, CLIP)
    frames_all = frames_total(count_ref)
    outs[0][...] = jnp.sum(vector_ref[7:8, :], 1, keepdims=True)
    outs[1][...] = jnp.full((1, 1), frames_all, jnp.int32).astype(jnp.float32) * 256.0
    outs[2][...] = norm
    pick = spots(64, 128, 64 * c)
    conv_rows = jnp.concatenate([sums_ref[0, 0:ROW_CONV], sums_ref[1, 0:ROW_CONV]], 0)
    pin, pout = [], []
    for half in range(2):
        rows = None
        for j in range(3):
            part = dot_exact(
                sums_ref[half, ROW_CONV + 32 * j : ROW_CONV + 32 * j + 32],
                spots(192, 128, 192 * c - 128 * j),
                ((1,), (1,)),
            )
            rows = part if rows is None else rows + part
        pin.append(rows)
        pout.append(dot_exact(sums_ref[half, 672:704], pick, ((1,), (1,))))
    time_rows = dtime_ref[fr // 4, pl.ds(pl.multiple_of(64 * (fr % 4), 64), 64), :]
    grads = [
        dot_exact(pick, conv_rows, ((1,), (1,))),
        jnp.concatenate(pin, 0),
        jnp.concatenate(pout, 0),
        dot_exact(time_rows, spots(64, 256, 64 * ba), ((1,), (1,))),
        vector_ref[8:11, :],
        vector_ref[11:14, :],
        vector_ref[0:7, :],
        vector_ref[32:36, 0:32],
    ]
    for k, grad in enumerate(grads):
        weight, first, second = (ref[...] for ref in state[3 * k : 3 * k + 3])
        news = adamw(weight, first, second, grad, clip_scale, RATES[k])
        for ref, value in zip(outs[3 + 3 * k : 6 + 3 * k], news):
            ref[...] = value


def shards_pairs(
    clean,
    noise,
    timesteps,
    frame_counts,
    conv_weight,
    conv_first,
    conv_second,
    proj_in,
    proj_in_first,
    proj_in_second,
    proj_out,
    proj_out_first,
    proj_out_second,
    time_weight,
    time_first,
    time_second,
    in_weight,
    in_first,
    in_second,
    out_weight,
    out_first,
    out_second,
    gains,
    gains_first,
    gains_second,
    rel_bias,
    rel_bias_first,
    rel_bias_second,
):

    bf16, f32 = jnp.bfloat16, jnp.float32
    vmem = pl.BlockSpec(memory_space=pltpu.VMEM)
    smem = pl.BlockSpec(memory_space=pltpu.SMEM)
    scratch = [
        pltpu.VMEM((2, 8, 2, ROW_ALL, 128), bf16),
        pltpu.VMEM((2, 4, 2, ROW_GRAD, 128), bf16),
        pltpu.VMEM((2, D, 3 * D), bf16),
        pltpu.VMEM((2, D, D), bf16),
        pltpu.VMEM((ROW_ALL, 128), bf16),
        pltpu.VMEM((2, ROW_ALL, 128), bf16),
        pltpu.VMEM((2, 2, 3, 4, 256), f32),
        pltpu.VMEM((8, 8, 256), f32),
        pltpu.VMEM((2048, 128), f32),
        pltpu.VMEM((8, 384), f32),
        pltpu.VMEM((HEADS, 256, 256), f32),
        pltpu.VMEM((128, D), f32),
        pltpu.VMEM((2048, D), f32),
        pltpu.VMEM((2048, D), f32),
        pltpu.VMEM((2048, D), f32),
        pltpu.VMEM((2048, D), f32),
        pltpu.VMEM((2048, 3 * D), bf16),
        pltpu.VMEM((2048, D), bf16),
        pltpu.VMEM((8, 16, 16, D), bf16),
        pltpu.VMEM((8, 256, 3 * D), bf16),
        pltpu.VMEM((8, HEADS, 256, 256), bf16),
        pltpu.VMEM((128, 16, D), bf16),
        pltpu.VMEM((PAIRS, 4, 8, 16, D), bf16),
        pltpu.VMEM((8, 16, 16, D), bf16),
        pltpu.VMEM((128, 16, D), bf16),
        pltpu.VMEM((3, ROWS // 256 * GAP + 16, D), bf16),
        pltpu.VMEM((3, 8 * GAP + 16, D), bf16),
        pltpu.VMEM((3, 8 * GAP + 16, D), bf16),
        pltpu.VMEM((D, 2048), bf16),
        pltpu.VMEM((D, 2048), bf16),
        pltpu.VMEM((128, D), f32),
        pltpu.VMEM((4, 2, 2, ROW_GRAD, 128), bf16),
        pltpu.VMEM((4, 2, HALF, 128), bf16),
        pltpu.VMEM((4, 2, HALF, 128), bf16),
        pltpu.VMEM((4, HALF, 128), bf16),
        pltpu.VMEM((4, HALF, 128), bf16),
        pltpu.VMEM((3, ROW_GRAD, 128), bf16),
        pltpu.VMEM((4, ROW_GRAD, 128), bf16),
        pltpu.VMEM((ROW_GRAD, 128), f32),
        pltpu.VMEM((ROW_GRAD, 128), f32),
        pltpu.VMEM((40, D), f32),
        pltpu.VMEM((11, 40, D), f32),
        pltpu.VMEM((8, 128), f32),
        pltpu.VMEM((11, 8, 128), f32),
        pltpu.SemaphoreType.DMA((2, 4, 2, 2)),
        pltpu.SemaphoreType.DMA((2, 4, 2)),
        pltpu.SemaphoreType.DMA((2, 4, 2)),
        pltpu.SemaphoreType.DMA((2, 4, 2)),
        pltpu.SemaphoreType.DMA((2, 4, 2)),
        pltpu.SemaphoreType.DMA((2, 4)),
        pltpu.SemaphoreType.DMA((2, 4)),
        pltpu.SemaphoreType.DMA((2, PAIRS, 3)),
        pltpu.SemaphoreType.DMA((2, 8, 3)),
        pltpu.SemaphoreType.DMA((2, PAIRS, 3)),
        pltpu.SemaphoreType.DMA((2, 8, 3)),
        pltpu.SemaphoreType.DMA((2, 4, 5)),
        pltpu.SemaphoreType.DMA((2, 5)),
        pltpu.SemaphoreType.DMA((2, 12)),
        pltpu.SemaphoreType.DMA((2, 12)),
        pltpu.SemaphoreType.DMA((2, 2, 2)),
        pltpu.SemaphoreType.DMA((2, STEPS)),
    ]
    sums, vector, squares, dtime, _ = pl.pallas_call(
        step_kernel,
        out_shape=(
            jax.ShapeDtypeStruct((2, ROW_GRAD, 128), f32),
            jax.ShapeDtypeStruct((40, D), f32),
            jax.ShapeDtypeStruct((8, 128), f32),
            jax.ShapeDtypeStruct((2, D, D), f32),
            jax.ShapeDtypeStruct((8, HEADS, 256, 256), bf16),
        ),
        in_specs=[vmem, vmem, smem, smem] + [vmem] * 7 + [smem],
        out_specs=(vmem,) * 4 + (pl.BlockSpec(memory_space=pl.ANY),),
        scratch_shapes=scratch,
        compiler_params=pltpu.CompilerParams(
            collective_id=0, has_side_effects=True, vmem_limit_bytes=64 * 2**20 - 2**16
        ),
        name="train_step",
    )(
        clean.transpose(0, 1, 3, 2, 4),
        noise.transpose(0, 1, 3, 2, 4),
        frame_counts,
        timesteps,
        conv_weight.T,
        proj_in,
        proj_out,
        time_weight,
        in_weight,
        out_weight,
        gains,
        rel_bias,
    )
    state = (
        conv_weight.T,
        conv_first.T,
        conv_second.T,
        proj_in,
        proj_in_first,
        proj_in_second,
        proj_out,
        proj_out_first,
        proj_out_second,
        time_weight,
        time_first,
        time_second,
        in_weight,
        in_first,
        in_second,
        out_weight,
        out_first,
        out_second,
        gains,
        gains_first,
        gains_second,
        rel_bias,
        rel_bias_first,
        rel_bias_second,
    )
    scalar = jax.ShapeDtypeStruct((1, 1), f32)
    results = pl.pallas_call(
        update_kernel,
        out_shape=[scalar] * 3 + [jax.ShapeDtypeStruct(value.shape, f32) for value in state],
        in_specs=[vmem] * 4 + [smem] + [vmem] * 24,
        out_specs=[vmem] * 27,
        compiler_params=pltpu.CompilerParams(vmem_limit_bytes=64 * 2**20 - 2**16),
        name="update",
    )(sums, vector, squares, dtime, frame_counts, *state)
    return (
        *(value.reshape(()) for value in results[:3]),
        *(value.T for value in results[3:6]),
        *results[6:],
    )


def shards(
    clean,
    noise,
    timesteps,
    frame_counts,
    conv_weight,
    conv_first,
    conv_second,
    proj_in,
    proj_in_first,
    proj_in_second,
    proj_out,
    proj_out_first,
    proj_out_second,
    time_weight,
    time_first,
    time_second,
    in_weight,
    in_first,
    in_second,
    out_weight,
    out_first,
    out_second,
    gains,
    gains_first,
    gains_second,
    rel_bias,
    rel_bias_first,
    rel_bias_second,
):
    fr_dev = clean.shape[2]
    pixels = clean.shape[4]
    videos = timesteps.shape[2]
    pix_dev = pixels // lax.axis_size("frame")
    group_idx = lax.axis_index("batch")
    frame_ids = lax.axis_index("frame") * fr_dev + jnp.arange(fr_dev)
    member = (frame_ids[:, None] // FRAMES == jnp.arange(videos)[None, :]).astype(jnp.float32)
    frame_place = frame_ids % FRAMES
    pixel_total = jnp.sum(frame_counts).astype(jnp.float32) * pixels
    offsets = jnp.arange(FRAMES)
    distance = offsets[None, :] - offsets[:, None]
    bucket = jnp.minimum(jnp.abs(distance), 15) + 16 * (distance > 0).astype(jnp.int32)
    onehot = (bucket[:, :, None] == jnp.arange(rel_bias.shape[1])[None, None, :]).astype(
        jnp.float32
    )
    bias_mat = jnp.einsum("hk,lmk->hlm", rel_bias, onehot, precision=HIGH)
    half_width = D // 2
    frequency = jnp.exp(-math.log(10000.0) * jnp.arange(half_width, dtype=jnp.float32) / half_width)
    out_low = out_weight.astype(jnp.bfloat16)
    matrix_acc = None
    vector_acc = None
    loss_local = jnp.zeros((), jnp.float32)
    for micro_idx in range(MICRO):
        gathered = fetch(conv_weight, proj_in, proj_out, time_weight)
        kernels = gathered[0].reshape(4, 9 * D, D)
        w_in = gathered[1].reshape(2, D, 3 * D)
        w_out = gathered[2].reshape(2, D, D)
        w_time = gathered[3].reshape(2, D, D)
        steps_grp = lax.dynamic_index_in_dim(timesteps[micro_idx], group_idx, 0, keepdims=False)
        count_grp = lax.dynamic_index_in_dim(frame_counts[micro_idx], group_idx, 0, keepdims=False)
        levels = steps_grp.astype(jnp.float32)
        embedding = jnp.concatenate(
            [jnp.sin(levels[:, None] * frequency), jnp.cos(levels[:, None] * frequency)], -1
        ).astype(jnp.bfloat16)
        time_pre = jnp.einsum("vd,jde->jve", embedding, w_time, preferred_element_type=jnp.float32)
        frame_bias = jnp.einsum("fv,jvd->jfd", member, swish(time_pre), precision=HIGH)[
            :, :, None, :
        ]
        frame_level = jnp.dot(member, levels, precision=HIGH)
        alpha_bar = jnp.cos(0.5 * math.pi * (frame_level + 1.0) / (TSTEPS + 1.0)) ** 2
        target = noise[micro_idx, 0]
        noisy_input = (
            jnp.sqrt(alpha_bar)[:, None, None] * clean[micro_idx, 0]
            + jnp.sqrt(1.0 - alpha_bar)[:, None, None] * target
        )
        frame_count = jnp.sum(member * count_grp.astype(jnp.float32)[None, :], 1)
        live_frames = (frame_place.astype(jnp.float32) < frame_count).astype(jnp.float32)
        valid_video = offsets[None, :] < count_grp[:, None]
        valid_rows = jnp.broadcast_to(valid_video[:, None, :], (videos, pix_dev, FRAMES)).reshape(
            videos * pix_dev, FRAMES
        )
        context = (videos, bias_mat, valid_rows, onehot)
        hidden_zero = jnp.einsum("fcp,cd->fpd", noisy_input, in_weight, precision=HIGH)
        hidden_one, saved_zero = res_fwd(
            hidden_zero, kernels[0], kernels[1], gains[0], gains[1], frame_bias[0]
        )
        hidden_two, saved_spatial = mixer_fwd(hidden_one, gains[2], w_in[0], w_out[0], None)
        hidden_three, saved_temporal = mixer_fwd(hidden_two, gains[3], w_in[1], w_out[1], context)
        hidden_four, saved_last = res_fwd(
            hidden_three, kernels[2], kernels[3], gains[4], gains[5], frame_bias[1]
        )
        normed, inverse = norm_fwd(hidden_four, gains[6])
        normed_low = normed.astype(jnp.bfloat16)
        predicted = jnp.einsum(
            "fpd,cd->fcp", normed_low, out_low, preferred_element_type=jnp.float32
        )
        pred_error = predicted - target
        weighted = live_frames[:, None, None] * pred_error
        loss_local = loss_local + jnp.sum(weighted * pred_error)
        dpred = 2.0 * weighted / pixel_total
        d_out = jnp.einsum("fcp,fpd->cd", dpred, normed_low.astype(jnp.float32), precision=HIGH)
        dnormed = jnp.einsum("fcp,cd->fpd", dpred, out_low.astype(jnp.float32), precision=HIGH)
        dhid_four, dgain_six = norm_bwd(hidden_four, inverse, gains[6], dnormed)
        dhid_three, dkern_two, dkern_three, dgain_four, dgain_five, dbias_one = res_bwd(
            hidden_three, dhid_four, kernels[2], kernels[3], gains[4], gains[5], saved_last
        )
        dhid_two, din_one, dout_one, dgain_three, dtable = mixer_bwd(
            hidden_two, dhid_three, gains[3], w_in[1], w_out[1], context, saved_temporal
        )
        dhid_one, din_zero, dout_zero, dgain_two, _ = mixer_bwd(
            hidden_one, dhid_two, gains[2], w_in[0], w_out[0], None, saved_spatial
        )
        dhid_zero, dkern_zero, dkern_one, dgain_zero, dgain_one, dbias_zero = res_bwd(
            hidden_zero, dhid_one, kernels[0], kernels[1], gains[0], gains[1], saved_zero
        )
        dtime_pre = jnp.einsum(
            "fv,jfd->jvd", member, jnp.stack([dbias_zero, dbias_one]), precision=HIGH
        ) * swish_grad(time_pre)
        dtime = jnp.einsum("vd,jve->jde", embedding.astype(jnp.float32), dtime_pre, precision=HIGH)
        d_in = jnp.einsum("fcp,fpd->cd", noisy_input, dhid_zero, precision=HIGH)
        matrix_grads = (
            jnp.stack([dkern_zero, dkern_one, dkern_two, dkern_three]).reshape(36 * D, D),
            jnp.stack([din_zero, din_one]).reshape(2 * D, 3 * D),
            jnp.stack([dout_zero, dout_one]).reshape(2 * D, D),
            dtime.reshape(2 * D, D),
        )
        vector_grads = (
            d_in,
            d_out,
            jnp.stack(
                [dgain_zero, dgain_one, dgain_two, dgain_three, dgain_four, dgain_five, dgain_six]
            ),
            dtable,
        )
        matrix_acc = (
            matrix_grads if matrix_acc is None else jax.tree.map(jnp.add, matrix_acc, matrix_grads)
        )
        vector_acc = (
            vector_grads if vector_acc is None else jax.tree.map(jnp.add, vector_acc, vector_grads)
        )
    matrix_acc = reduce_rows(matrix_acc)
    sum_in, sum_out, sum_gains, sum_table, loss_sum = lax.psum(
        (vector_acc[0], vector_acc[1], vector_acc[2], vector_acc[3], loss_local), ("frame", "batch")
    )
    local_square = sum((jnp.sum(grad * grad) for grad in matrix_acc))
    square = lax.psum(local_square, ("frame", "batch")) + sum(
        (jnp.sum(grad * grad) for grad in (sum_in, sum_out, sum_gains, sum_table))
    )
    grad_norm = jnp.sqrt(square)
    clip_scale = CLIP / jnp.maximum(grad_norm, CLIP)
    conv_new, conv_first_new, conv_second_new = adamw(
        conv_weight, conv_first, conv_second, matrix_acc[0], clip_scale, RATES[0]
    )
    pin_new, pin_first_new, pin_second_new = adamw(
        proj_in, proj_in_first, proj_in_second, matrix_acc[1], clip_scale, RATES[1]
    )
    pout_new, pout_first_new, pout_second_new = adamw(
        proj_out, proj_out_first, proj_out_second, matrix_acc[2], clip_scale, RATES[2]
    )
    time_new, time_first_new, time_second_new = adamw(
        time_weight, time_first, time_second, matrix_acc[3], clip_scale, RATES[3]
    )
    in_new, in_first_new, in_second_new = adamw(
        in_weight, in_first, in_second, sum_in, clip_scale, RATES[4]
    )
    out_new, out_first_new, out_second_new = adamw(
        out_weight, out_first, out_second, sum_out, clip_scale, RATES[5]
    )
    gains_new, gains_first_new, gains_second_new = adamw(
        gains, gains_first, gains_second, sum_gains, clip_scale, RATES[6]
    )
    bias_new, bias_first_new, bias_second_new = adamw(
        rel_bias, rel_bias_first, rel_bias_second, sum_table, clip_scale, RATES[7]
    )
    return (
        loss_sum,
        pixel_total,
        grad_norm,
        conv_new,
        conv_first_new,
        conv_second_new,
        pin_new,
        pin_first_new,
        pin_second_new,
        pout_new,
        pout_first_new,
        pout_second_new,
        time_new,
        time_first_new,
        time_second_new,
        in_new,
        in_first_new,
        in_second_new,
        out_new,
        out_first_new,
        out_second_new,
        gains_new,
        gains_first_new,
        gains_second_new,
        bias_new,
        bias_first_new,
        bias_second_new,
    )


def solution(mesh):
    in_specs = (
        P(None, "batch", "frame", None, None),
        P(None, "batch", "frame", None, None),
        P(),
        P(),
        P("frame", "batch"),
        P("frame", "batch"),
        P("frame", "batch"),
        P("frame", "batch"),
        P("frame", "batch"),
        P("frame", "batch"),
        P("frame", "batch"),
        P("frame", "batch"),
        P("frame", "batch"),
        P("frame", "batch"),
        P("frame", "batch"),
        P("frame", "batch"),
        P(),
        P(),
        P(),
        P(),
        P(),
        P(),
        P(),
        P(),
        P(),
        P(),
        P(),
        P(),
    )
    out_specs = (
        P(),
        P(),
        P(),
        P("frame", "batch"),
        P("frame", "batch"),
        P("frame", "batch"),
        P("frame", "batch"),
        P("frame", "batch"),
        P("frame", "batch"),
        P("frame", "batch"),
        P("frame", "batch"),
        P("frame", "batch"),
        P("frame", "batch"),
        P("frame", "batch"),
        P("frame", "batch"),
        P(),
        P(),
        P(),
        P(),
        P(),
        P(),
        P(),
        P(),
        P(),
        P(),
        P(),
        P(),
    )
    sizes = tuple(mesh.shape[name] for name in ("frame", "batch"))
    local = shards_pairs if sizes == (8, 4) else shards
    return jax.shard_map(local, mesh=mesh, in_specs=in_specs, out_specs=out_specs, check_vma=False)
```

```python
import math

import jax
import jax.numpy as jnp
from jax import lax
from jax.experimental import pallas as pl
from jax.experimental.pallas import tpu as pltpu
from jax.sharding import PartitionSpec as P

D = 256
HEADS = 4
FRAMES = 32
SIDE = 16
MICRO = 2
TSTEPS = 1000
STEP = 10


HIGH = lax.Precision.HIGHEST
EPS_NORM = 1e-06
CLIP = 0.05
BETA_ONE = 0.9
BETA_TWO = 0.999
ADAM_EPS = 1e-08
DECAY = 0.01
RATES = (0.02, 0.06, 0.18, 0.06, 0.6, 0.06, 1.0, 1.0)
NEG = -1000000000.0


def swish(values):
    return values * jax.nn.sigmoid(values)


def swish_grad(values):
    sigma_v = jax.nn.sigmoid(values)
    return sigma_v * (1.0 + values * (1.0 - sigma_v))


def norm_fwd(values, gain_vec):
    inverse = lax.rsqrt(jnp.mean(values * values, -1, keepdims=True) + EPS_NORM)
    return (values * inverse * gain_vec, inverse)


def norm_bwd(values, inverse, gain_vec, upstream):
    scaled = upstream * gain_vec
    dvalues = inverse * scaled - values * inverse**3 * jnp.mean(values * scaled, -1, keepdims=True)
    return (dvalues, jnp.sum(upstream * values * inverse, axis=(0, 1)))


def patches(acts):
    frames, pixels, width = acts.shape
    frame_grid = acts.reshape(frames, SIDE, SIDE, width)
    padded = jnp.pad(frame_grid, ((0, 0), (1, 1), (1, 1), (0, 0)))
    columns = [
        padded[:, offset // 3 : offset // 3 + SIDE, offset % 3 : offset % 3 + SIDE]
        for offset in range(9)
    ]
    return jnp.concatenate(columns, -1).reshape(frames * pixels, 9 * width)


def conv_fwd(acts, kernel):
    frames, pixels, width = acts.shape
    return jnp.dot(patches(acts), kernel, preferred_element_type=jnp.float32).reshape(
        frames, pixels, width
    )


def conv_bwd(acts, grad_low, kernel):
    frames, pixels, width = grad_low.shape
    flat_grad = grad_low.reshape(frames * pixels, width)
    dkernel = lax.dot_general(
        patches(acts), flat_grad, (((0,), (0,)), ((), ())), preferred_element_type=jnp.float32
    )
    tap_terms = lax.dot_general(
        flat_grad, kernel, (((1,), (1,)), ((), ())), preferred_element_type=jnp.float32
    )
    padded = jnp.pad(
        tap_terms.reshape(frames, SIDE, SIDE, 9, width), ((0, 0), (1, 1), (1, 1), (0, 0), (0, 0))
    )
    dacts = sum(
        (
            padded[
                :,
                2 - offset // 3 : 2 - offset // 3 + SIDE,
                2 - offset % 3 : 2 - offset % 3 + SIDE,
                offset,
            ]
            for offset in range(9)
        )
    )
    return (dacts.reshape(frames, pixels, width), dkernel)


def res_fwd(hidden, kern_one, kern_two, gain_one, gain_two, frame_bias):
    normed, inverse_one = norm_fwd(hidden, gain_one)
    acts_one = swish(normed).astype(jnp.bfloat16)
    inner_act = conv_fwd(acts_one, kern_one) + frame_bias
    second_norm, inverse_two = norm_fwd(inner_act, gain_two)
    acts_two = swish(second_norm).astype(jnp.bfloat16)
    saved = (normed, inverse_one, acts_one, inner_act, second_norm, inverse_two, acts_two)
    return (hidden + conv_fwd(acts_two, kern_two), saved)


def res_bwd(hidden, upstream, kern_one, kern_two, gain_one, gain_two, saved):
    normed, inverse_one, acts_one, inner_act, second_norm, inverse_two, acts_two = saved
    dacts_two, dkern_two = conv_bwd(acts_two, upstream.astype(jnp.bfloat16), kern_two)
    dinner, dgain_two = norm_bwd(
        inner_act, inverse_two, gain_two, dacts_two * swish_grad(second_norm)
    )
    dacts_one, dkern_one = conv_bwd(acts_one, dinner.astype(jnp.bfloat16), kern_one)
    dhidden, dgain_one = norm_bwd(hidden, inverse_one, gain_one, dacts_one * swish_grad(normed))
    return (upstream + dhidden, dkern_one, dkern_two, dgain_one, dgain_two, jnp.sum(dinner, 1))


def attend_probs(packed, bias_mat, valid):
    batch, length, _ = packed.shape
    split_heads = packed.reshape(batch, length, 3, HEADS, D // HEADS)
    scores = (
        jnp.einsum(
            "blhe,bmhe->bhlm",
            split_heads[:, :, 0],
            split_heads[:, :, 1],
            preferred_element_type=jnp.float32,
        )
        / math.sqrt(D // HEADS)
        + bias_mat
    )
    if valid is not None:
        scores = jnp.where(valid[:, None, None, :], scores, NEG)
    shifted = jnp.exp(scores - jnp.max(scores, -1, keepdims=True))
    return (shifted / jnp.sum(shifted, -1, keepdims=True), split_heads)


def attend_fwd(packed, bias_mat, valid):
    attn_probs, split_heads = attend_probs(packed, bias_mat, valid)
    mixture = jnp.einsum(
        "bhlm,bmhe->blhe",
        attn_probs.astype(jnp.bfloat16),
        split_heads[:, :, 2],
        preferred_element_type=jnp.float32,
    )
    return mixture.reshape(packed.shape[0], packed.shape[1], D).astype(jnp.bfloat16)


def attend_bwd(packed, dmixture, bias_mat, valid):
    batch, length, _ = packed.shape
    attn_probs, split_heads = attend_probs(packed, bias_mat, valid)
    grad_heads = dmixture.reshape(batch, length, HEADS, D // HEADS)
    dattn_probs = jnp.einsum(
        "blhe,bmhe->bhlm", grad_heads, split_heads[:, :, 2], preferred_element_type=jnp.float32
    )
    dvalues = jnp.einsum(
        "bhlm,blhe->bmhe",
        attn_probs.astype(jnp.bfloat16),
        grad_heads,
        preferred_element_type=jnp.float32,
    )
    dscores = attn_probs * (dattn_probs - jnp.sum(attn_probs * dattn_probs, -1, keepdims=True))
    dscore_low = dscores.astype(jnp.bfloat16)
    root_dim = math.sqrt(D // HEADS)
    dquery = (
        jnp.einsum(
            "bhlm,bmhe->blhe", dscore_low, split_heads[:, :, 1], preferred_element_type=jnp.float32
        )
        / root_dim
    )
    dkey_vals = (
        jnp.einsum(
            "bhlm,blhe->bmhe", dscore_low, split_heads[:, :, 0], preferred_element_type=jnp.float32
        )
        / root_dim
    )
    dpacked = (
        jnp.stack([dquery, dkey_vals, dvalues], 2)
        .reshape(batch, length, 3 * D)
        .astype(jnp.bfloat16)
    )
    return (dpacked, jnp.sum(dscores, 0))


def to_rows(spread, videos):
    slots, pix_dev, width = spread.shape
    return (
        spread.reshape(videos, slots // videos, pix_dev, width)
        .transpose(0, 2, 1, 3)
        .reshape(videos * pix_dev, slots // videos, width)
    )


def from_rows(rows, videos):
    count_rows, length, width = rows.shape
    pix_dev = count_rows // videos
    return (
        rows.reshape(videos, pix_dev, length, width)
        .transpose(0, 2, 1, 3)
        .reshape(videos * length, pix_dev, width)
    )


def mixer_fwd(hidden, gain_vec, w_in, w_out, context):
    normed, inverse = norm_fwd(hidden, gain_vec)
    normed_low = normed.astype(jnp.bfloat16)
    packed = jnp.dot(normed_low, w_in, preferred_element_type=jnp.float32).astype(jnp.bfloat16)
    if context is None:
        return (
            hidden
            + jnp.dot(attend_fwd(packed, 0.0, None), w_out, preferred_element_type=jnp.float32),
            (normed_low, inverse, packed, None),
        )
    videos, bias_mat, valid_rows, onehot = context
    spread = lax.all_to_all(packed, "frame", split_axis=1, concat_axis=0, tiled=True)
    mixture = from_rows(attend_fwd(to_rows(spread, videos), bias_mat, valid_rows), videos)
    gathered_back = lax.all_to_all(mixture, "frame", split_axis=0, concat_axis=1, tiled=True)
    return (
        hidden + jnp.dot(gathered_back, w_out, preferred_element_type=jnp.float32),
        (normed_low, inverse, packed, spread),
    )


def mixer_bwd(hidden, upstream, gain_vec, w_in, w_out, context, saved):
    normed_low, inverse, packed, kept_pixels = saved
    grad_low = upstream.astype(jnp.bfloat16)
    dtable_sum = None
    if context is None:
        inputs, grads_out, bias_mat, valid_rows = (packed, grad_low, 0.0, None)
    else:
        videos, bias_mat, valid_rows, onehot = context
        spread, grad_spread = (
            lax.all_to_all(packed, "frame", split_axis=1, concat_axis=0, tiled=True),
            lax.all_to_all(grad_low, "frame", split_axis=1, concat_axis=0, tiled=True),
        )
        inputs, grads_out = (to_rows(spread, videos), to_rows(grad_spread, videos))
    mixture = attend_fwd(inputs, bias_mat, valid_rows)
    dw_out = jnp.einsum("bld,ble->de", mixture, grads_out, preferred_element_type=jnp.float32)
    dmixture = jnp.einsum(
        "ble,de->bld", grads_out, w_out, preferred_element_type=jnp.float32
    ).astype(jnp.bfloat16)
    dpacked, dbias_sum = attend_bwd(inputs, dmixture, bias_mat, valid_rows)
    if context is not None:
        dpacked = lax.all_to_all(
            from_rows(dpacked, videos), "frame", split_axis=0, concat_axis=1, tiled=True
        )
        dtable_sum = jnp.einsum("hlm,lmk->hk", dbias_sum, onehot, precision=HIGH)
    dw_in = jnp.einsum("fpd,fpk->dk", normed_low, dpacked, preferred_element_type=jnp.float32)
    dnormed = jnp.einsum("fpk,dk->fpd", dpacked, w_in, preferred_element_type=jnp.float32)
    dhidden, dgain_vec = norm_bwd(hidden, inverse, gain_vec, dnormed)
    return (upstream + dhidden, dw_in, dw_out, dgain_vec, dtable_sum)


def fetch(conv_weight, proj_in, proj_out, time_weight):
    columns = (
        lax.all_gather(conv_weight.astype(jnp.bfloat16), "batch", axis=1, tiled=True),
        lax.all_gather(proj_in.astype(jnp.bfloat16), "batch", axis=1, tiled=True),
        lax.all_gather(proj_out.astype(jnp.bfloat16), "batch", axis=1, tiled=True),
        lax.all_gather(time_weight.astype(jnp.bfloat16), "batch", axis=1, tiled=True),
    )
    return (
        lax.all_gather(columns[0], "frame", axis=0, tiled=True),
        lax.all_gather(columns[1], "frame", axis=0, tiled=True),
        lax.all_gather(columns[2], "frame", axis=0, tiled=True),
        lax.all_gather(columns[3], "frame", axis=0, tiled=True),
    )


def reduce_rows(matrix_grads):
    row_parts = (
        lax.psum_scatter(matrix_grads[0], "frame", scatter_dimension=0, tiled=True),
        lax.psum_scatter(matrix_grads[1], "frame", scatter_dimension=0, tiled=True),
        lax.psum_scatter(matrix_grads[2], "frame", scatter_dimension=0, tiled=True),
        lax.psum_scatter(matrix_grads[3], "frame", scatter_dimension=0, tiled=True),
    )
    return (
        lax.psum_scatter(row_parts[0], "batch", scatter_dimension=1, tiled=True),
        lax.psum_scatter(row_parts[1], "batch", scatter_dimension=1, tiled=True),
        lax.psum_scatter(row_parts[2], "batch", scatter_dimension=1, tiled=True),
        lax.psum_scatter(row_parts[3], "batch", scatter_dimension=1, tiled=True),
    )


def adamw(weight, moment_one, moment_two, grad, clip_scale, step_rate):
    grad = grad * clip_scale
    moment_one = BETA_ONE * moment_one + (1.0 - BETA_ONE) * grad
    moment_two = BETA_TWO * moment_two + (1.0 - BETA_TWO) * grad * grad
    update = (
        moment_one
        / (1.0 - BETA_ONE**STEP)
        / (jnp.sqrt(moment_two / (1.0 - BETA_TWO**STEP)) + ADAM_EPS)
    )
    return (weight - step_rate * (update + DECAY * weight), moment_one, moment_two)


ROW_CONV = 576
ROW_GRAD = 704
ROW_ALL = 736
HALF = 352
QUARTER = 176
PAIRS = 4
BLOCKS = 2
N_CONV = 4
N_FORWARD = 2
N_LAST = 4
N_BACK = 2
N_FIRST = 2
N_INPUT = 2
GAP = 272
NEVER = -1e30
MESH_ID = pl.DeviceIdType.MESH


def dot_nn(lhs, rhs):
    return jnp.dot(lhs, rhs, preferred_element_type=jnp.float32)


def dot_nt(lhs, rhs):
    return lax.dot_general(lhs, rhs, (((1,), (1,)), ((), ())), preferred_element_type=jnp.float32)


def dot_tn(lhs, rhs):
    return lax.dot_general(lhs, rhs, (((0,), (0,)), ((), ())), preferred_element_type=jnp.float32)


def low(values):
    return values.astype(jnp.bfloat16)


def rms(values, gain_row):
    inverse = lax.rsqrt(jnp.mean(values * values, -1, keepdims=True) + EPS_NORM)
    return values * inverse * gain_row, inverse


def rms_back(values, inverse, gain_row, upstream):
    scaled = upstream * gain_row
    unit = values * inverse
    mean = jnp.mean(unit * scaled, -1, keepdims=True)
    return inverse * (scaled - unit * mean), jnp.sum(upstream * unit, 0, keepdims=True)


def weave(block):
    first = block[:256].reshape(32, 1, 8, D)
    second = block[256:].reshape(32, 1, 8, D)
    return jnp.concatenate([first, second], 1).reshape(512, D)


def unweave(block):
    parts = block.reshape(32, 2, 8, D)
    return jnp.concatenate([parts[:, 0].reshape(256, D), parts[:, 1].reshape(256, D)], 0)


def tap_pieces(tap):
    start, stop = 256 * tap, 256 * tap + 256
    pieces = []
    while start < stop:
        block, offset = divmod(start, ROW_CONV)
        size = min(ROW_CONV - offset, stop - start)
        pieces.append((block // 2, block % 2, offset, size))
        start += size
    return pieces


def frames_total(count_ref):
    total = 0
    for micro in range(2):
        for group in range(4):
            total = total + count_ref[micro, 0, group]
    return total


def step_kernel(
    clean_ref,
    noise_ref,
    count_ref,
    steps_ref,
    conv_ref,
    pin_ref,
    pout_ref,
    time_ref,
    win_ref,
    wout_ref,
    gains_ref,
    rel_ref,
    grads_ref,
    vector_ref,
    squares_ref,
    dtime_ref,
    prob_far,
    wall,
    dslab,
    proj,
    outp,
    mine,
    ready,
    frames_in,
    eight,
    clip_ref,
    video_ref,
    table_ref,
    head_pad,
    hid_one,
    hid_two,
    inner_zero,
    dhid,
    pack_zero,
    mix_zero,
    spread_norm,
    pack_one,
    prob_one,
    mix_one,
    mix_back,
    dout_pix,
    stage,
    shift_one,
    shift_two,
    act_one,
    act_two,
    acc_out,
    red_sib,
    red_a,
    red_b,
    red_c,
    red_d,
    red_z,
    final_recv,
    red_q,
    red_back,
    quarter_sum,
    vec_acc,
    vec_recv,
    sq_acc,
    sq_recv,
    sem_sib,
    sem_zu,
    sem_zd,
    sem_x,
    sem_y,
    sem_xf,
    sem_yf,
    sem_n,
    sem_m,
    sem_dy,
    sem_dn,
    sem_red,
    sem_fin,
    sem_q,
    sem_back,
    sem_vec,
    sem_sq,
    sem_in,
    sem_prob,
):
    fr = lax.axis_index("frame")
    ba = lax.axis_index("batch")
    z, x = fr // 2, fr % 2
    y, c = ba // 2, ba % 2
    ox, oy, oc = 1 - x, 1 - y, 1 - c
    quarter = 2 * x + c
    sibling = (fr, 2 * y + oc)
    x_peer = (2 * z + ox, ba)
    y_peer = (fr, 2 * oy + c)
    xs_peer = (2 * z + ox, 2 * y + oc)
    z_ids = [(z + k) % 4 for k in (1, 2, 3)]
    z_peers = [(2 * k + x, ba) for k in z_ids]
    up_peer = (2 * jnp.minimum(z + 1, 3) + x, ba)
    down_peer = (2 * jnp.maximum(z - 1, 0) + x, ba)
    plane = [(2 * z + px, 2 * py + pc) for px, py, pc in (
        (x, y, oc), (x, oy, c), (x, oy, oc), (ox, y, c), (ox, y, oc), (ox, oy, c), (ox, oy, oc)
    )]
    group = [(sibling, 2 * x + oc), (x_peer, 2 * ox + c), (xs_peer, 2 * ox + oc)]

    def remote(src, dst, sems, send_at, recv_at, device):
        return pltpu.make_async_remote_copy(
            src_ref=src,
            dst_ref=dst,
            send_sem=sems.at[(0,) + send_at],
            recv_sem=sems.at[(1,) + recv_at],
            device_id=device,
            device_id_type=MESH_ID,
        )

    video = 4 * (z // 2) + 2 * y + z % 2
    in_dst = [(4 * (x if t == 0 else ox) + 2 * c + z // 2, 2 * y + z % 2) for t in range(2)]
    in_src = [(2 * quarter + (z // 2 if t == 0 else 1 - z // 2), 2 * y + z % 2) for t in range(2)]
    moves = [(dst[0] != fr) | (dst[1] != ba) for dst in in_dst]

    barrier = pltpu.get_barrier_semaphore()
    everyone = plane + z_peers
    for peer in everyone:
        pl.semaphore_signal(barrier, inc=1, device_id=peer, device_id_type=MESH_ID)
    for turn in range(2):

        @pl.when(moves[turn])
        def _(turn=turn):
            pl.semaphore_signal(barrier, inc=1, device_id=in_src[turn], device_id_type=MESH_ID)

    def spots(rows, columns, shift):
        row = lax.broadcasted_iota(jnp.int32, (rows, columns), 0)
        column = lax.broadcasted_iota(jnp.int32, (rows, columns), 1)
        return low(jnp.where(row + shift == column, 1.0, 0.0))

    narrow = spots(64, 128, 64 * c)
    conv_own = low(dot_tn(low(conv_ref[...]), narrow))
    pin_own = low(dot_nn(low(pin_ref[...]), spots(192, 384, 192 * c)))
    pout_own = low(dot_nn(low(pout_ref[...]), narrow))
    time_own = low(dot_nn(low(time_ref[...]), narrow))
    for half in range(2):
        rows = slice(32 * half, 32 * half + 32)
        ready[half, 0:ROW_CONV] = conv_own[ROW_CONV * half : ROW_CONV * half + ROW_CONV]
        for j in range(3):
            ready[half, ROW_CONV + 32 * j : ROW_CONV + 32 * j + 32] = pin_own[
                rows, 128 * j : 128 * j + 128
            ]
        ready[half, 672:704] = pout_own[rows]
        ready[half, 704:736] = time_own[rows]

    pl.semaphore_wait(
        barrier, len(everyone) + moves[0].astype(jnp.int32) + moves[1].astype(jnp.int32)
    )
    first = remote(ready.at[oc], mine, sem_vec, (11,), (11,), sibling)
    first.start()

    def input_copies(turn):
        micro = x if turn == 0 else ox
        return [
            remote(
                src.at[micro, 0],
                frames_in.at[x, k],
                sem_in,
                (turn, k),
                (turn, k),
                in_dst[turn],
            )
            for k, src in enumerate((clean_ref, noise_ref))
        ]

    for turn in range(2):

        @pl.when(moves[turn])
        def _(turn=turn):
            for copy in input_copies(turn):
                copy.start()

        @pl.when(jnp.logical_not(moves[turn]))
        def _(turn=turn):
            for k, src in enumerate((clean_ref, noise_ref)):
                frames_in[x, k] = src[x if turn == 0 else ox, 0]

    def arrive(dst, sems, at):
        remote(dst, dst, sems, at, at, sibling).wait_recv()

    def push(block, sems, at, device):
        remote(block, block, sems, at, at, device).start()

    parts = [pl.ds(0, 368), pl.ds(368, 368)]

    def to_sibling(row_z, row_x, row_y):
        at = (row_z, row_x, row_y)
        push(wall.at[row_y, 2 * row_z + row_x, c], sem_sib, at, sibling)

    def turn_row(turn):
        return jnp.where(turn <= z, z - turn, turn)

    def gather_one(turn):
        row_z = turn_row(turn)
        for k, part in enumerate(parts):
            block = wall.at[y, 2 * row_z + x, c, part]
            at = (row_z, k)
            if turn > 0:

                @pl.when(turn <= z)
                def _():
                    arrive(block, sem_zu, at)

                @pl.when(turn > z)
                def _():
                    arrive(block, sem_zd, at)

            @pl.when((turn <= z) & (z < 3))
            def _():
                push(block, sem_zu, at, up_peer)

            @pl.when(((turn > z) | (turn == 0)) & (z > 0))
            def _():
                push(block, sem_zd, at, down_peer)

            push(block, sem_x, at, x_peer)
            push(block, sem_y, at, y_peer)
        to_sibling(row_z, x, y)

    def gather_two(turn):
        row_z = turn_row(turn)
        from_x = [wall.at[y, 2 * row_z + ox, c, part] for part in parts]
        from_y = [wall.at[oy, 2 * row_z + x, c, part] for part in parts]
        arrive(from_x[0], sem_x, (row_z, 0))
        push(from_x[0], sem_yf, (row_z,), y_peer)
        arrive(from_y[0], sem_y, (row_z, 0))
        arrive(from_y[1], sem_y, (row_z, 1))
        push(from_y[1], sem_xf, (row_z,), x_peer)
        to_sibling(row_z, x, oy)
        arrive(from_x[1], sem_x, (row_z, 1))
        to_sibling(row_z, ox, y)

    def gather_three(row_z):
        arrive(wall.at[oy, 2 * row_z + ox, c, parts[0]], sem_yf, (row_z,))
        arrive(wall.at[oy, 2 * row_z + ox, c, parts[1]], sem_xf, (row_z,))
        to_sibling(row_z, ox, oy)

    def gather_four(row_z):
        for row_x in range(2):
            for row_y in range(2):
                arrive(wall.at[row_y, 2 * row_z + row_x, oc], sem_sib, (row_z, row_x, row_y))

    def gather_sent():
        part = wall.at[y, fr, c, parts[0]]

        def sent(block, sems, at):
            remote(block, block, sems, at, at, sibling).wait_send()

        for row_z in range(4):
            for k in range(2):
                sent(part, sem_x, (row_z, k))
                sent(part, sem_y, (row_z, k))

                @pl.when((row_z <= z) & (z < 3))
                def _():
                    sent(part, sem_zu, (row_z, k))

                @pl.when((row_z >= z) & (z > 0))
                def _():
                    sent(part, sem_zd, (row_z, k))

            sent(part, sem_xf, (row_z,))
            sent(part, sem_yf, (row_z,))
            for row_x in range(2):
                for row_y in range(2):
                    sent(wall.at[y, fr, c], sem_sib, (row_z, row_x, row_y))

    zeros_row = jnp.zeros((3, 16, D), jnp.bfloat16)
    for frame in range(9):
        shift_one[:, GAP * frame : GAP * frame + 16, :] = zeros_row
        shift_two[:, GAP * frame : GAP * frame + 16, :] = zeros_row
    vec_acc[...] = jnp.zeros_like(vec_acc)
    acc_out[...] = jnp.zeros_like(acc_out)
    eight[...] = jnp.zeros_like(eight)
    head_pad[...] = jnp.zeros_like(head_pad)
    head_pad[0:3, :] = wout_ref[...]
    first.wait()
    wall[y, fr, c] = ready[c] + mine[...]

    gather_one(0)

    count = count_ref[z // 2, 0, 2 * y + z % 2]

    def table_rows(part, carry):
        rows = pl.ds(pl.multiple_of(32 * part, 32), 32)
        row = lax.broadcasted_iota(jnp.int32, (32, 256), 0) + 32 * part
        column = lax.broadcasted_iota(jnp.int32, (32, 256), 1)
        away = column // 8 - row // 8
        bucket = jnp.minimum(jnp.abs(away), 15) + jnp.where(away > 0, 16, 0)
        usable = (row % 8 == column % 8) & (column // 8 < count)
        bucket = jnp.where(usable, bucket, -1)
        biases = [jnp.full((32, 256), NEVER, jnp.float32) for _ in range(HEADS)]
        for k in range(32):
            here = bucket == k
            biases = [jnp.where(here, rel_ref[h, k], biases[h]) for h in range(HEADS)]
        for h in range(HEADS):
            table_ref[h, rows, :] = biases[h]
        return carry

    gather_one(1)
    gather_two(0)
    lax.fori_loop(0, 4, table_rows, 0)
    gather_one(2)
    gather_two(1)
    lax.fori_loop(4, 8, table_rows, 0)
    gather_one(3)
    gather_two(2)

    for turn in range(2):

        @pl.when(moves[turn])
        def _(turn=turn):
            for copy in input_copies(turn):
                copy.wait_send()
                copy.wait_recv()

    row = lax.broadcasted_iota(jnp.int32, (8, 384), 0)
    lane = lax.broadcasted_iota(jnp.int32, (8, 384), 1)
    levels = jnp.zeros((8, 384), jnp.int32)
    for k in range(8):
        levels = jnp.where(row == k, steps_ref[k // 4, 0, k % 4], levels)
    levels = levels.astype(jnp.float32)
    half_width = D // 2
    frequency = jnp.exp(-math.log(10000.0) * (lane % half_width).astype(jnp.float32) / half_width)
    angles = jnp.where(
        lane < D, levels * frequency, 0.5 * math.pi * (levels + 1.0) / (TSTEPS + 1.0)
    )
    cosines = jnp.cos(angles)
    embedding = low(jnp.where(lane < half_width, jnp.sin(angles), cosines)).astype(jnp.float32)
    alpha_bar = cosines * cosines
    alphas = jnp.where(lane == D, jnp.sqrt(alpha_bar), jnp.sqrt(1.0 - alpha_bar))
    video_ref[...] = jnp.where(lane < D, embedding, alphas)
    video_row = video_ref[pl.ds(video, 1), :]
    keep, add = video_row[:, 256:257], video_row[:, 257:258]
    place = spots(8, 128, 0).astype(jnp.float32)
    for frame in range(8):
        for channel in range(3):
            here = (channel, slice(frame % 4, frame % 4 + 1))
            noise_row = frames_in[(frame // 4, 1) + here]
            eight[frame, channel : channel + 1] = noise_row
            eight[frame, 3 + channel : 4 + channel] = (
                keep * frames_in[(frame // 4, 0) + here] + add * noise_row
            )
        clip_ref[256 * frame : 256 * frame + 256, :] = lax.dot_general(
            eight[frame],
            place,
            (((0,), (0,)), ((), ())),
            precision=HIGH,
            preferred_element_type=jnp.float32,
        )

    gather_two(3)
    gather_three(0)
    gather_four(0)

    def unpack(rows_of):
        for row_y in range(2):
            for row in rows_of:
                for half in range(2):
                    block = wall.at[row_y, row, half]
                    rows = slice(64 * (row % 4) + 32 * half, 64 * (row % 4) + 32 * half + 32)
                    for j in range(3):
                        cols = slice(384 * row_y + 128 * j, 384 * row_y + 128 * j + 128)
                        proj[row // 4, rows, cols] = block[
                            ROW_CONV + 32 * j : ROW_CONV + 32 * j + 32
                        ]
                    outp[row // 4, rows, 128 * row_y : 128 * row_y + 128] = block[672:704]

    def time_tile(layer):
        rows = []
        for row in range(4 * layer, 4 * layer + 4):
            for half in range(2):
                rows.append(
                    jnp.concatenate(
                        [wall[0, row, half, 704:736, :], wall[1, row, half, 704:736, :]], 1
                    )
                )
        return jnp.concatenate(rows, 0)

    def conv_tile(kernel, tap):
        rows = []
        for row, half, offset, size in tap_pieces(tap):
            block = (2 * kernel + row, half)
            rows.append(
                jnp.concatenate(
                    [
                        wall[(0,) + block + (slice(offset, offset + size),)],
                        wall[(1,) + block + (slice(offset, offset + size),)],
                    ],
                    1,
                )
            )
        return rows[0] if len(rows) == 1 else jnp.concatenate(rows, 0)

    embed = low(jnp.broadcast_to(video_row[:, 0:D], (16, D)))

    def time_project(layer):
        pre = dot_nn(embed, time_tile(layer))[0:1]
        return pre, pre * jax.nn.sigmoid(pre)

    gain = [gains_ref[k : k + 1, :] for k in range(7)]
    column = lax.broadcasted_iota(jnp.int32, (1, D), 1)
    heads = [
        jnp.where(column // 64 == h, 1.0, 0.0).astype(jnp.bfloat16) for h in range(HEADS)
    ]
    pixel_x = lax.broadcasted_iota(jnp.int32, (256, 1), 0) % SIDE
    not_left = jnp.where(pixel_x != 0, 1.0, 0.0)
    not_right = jnp.where(pixel_x != SIDE - 1, 1.0, 0.0)

    def put_shifts(dst, bases, values):
        for k, base in enumerate(bases):
            frame = values[256 * k : 256 * k + 256]
            rows = pl.ds(base, 256)
            dst[0, rows, :] = low(pltpu.roll(frame, 1, 0) * not_left)
            dst[1, rows, :] = low(frame)
            dst[2, rows, :] = low(pltpu.roll(frame, 255, 0) * not_right)

    def aligned(value, multiple):
        return value if isinstance(value, int) else pl.multiple_of(value, multiple)

    def shifted(src, bases, dy, dx):
        return jnp.concatenate(
            [src[dx, pl.ds(aligned(base + 16 * (dy - 1), 16), 256), :] for base in bases], 0
        )

    def conv(src, bases, kernel):
        totals = []
        for base in bases:
            total = None
            for tap in range(9):
                part = dot_nn(shifted(src, [base], tap // 3, tap % 3), conv_tile(kernel, tap))
                total = part if total is None else total + part
            totals.append(total)
        return jnp.concatenate(totals, 0)

    def conv_back(src, bases, kernel):
        totals = []
        for base in bases:
            total = None
            for tap in range(9):
                here = shifted(src, [base], 2 - tap // 3, 2 - tap % 3)
                part = dot_nt(here, conv_tile(kernel, tap))
                total = part if total is None else total + part
            totals.append(total)
        return jnp.concatenate(totals, 0)

    def conv_grad(act, src, kernel, dst, first_row):
        for tap in range(9):
            grads = shifted(src, [16 + GAP * k for k in range(8)], 2 - tap // 3, 2 - tap % 3)
            total = low(dot_nn(act[...], grads))
            start = 0
            for row, half, offset, size in tap_pieces(tap):
                for row_y in range(2):
                    dst[row_y, first_row + row, half, offset : offset + size] = total[
                        start : start + size, 128 * row_y : 128 * row_y + 128
                    ]
                start += size

    def put_proj_grad(layer, din, dout, dst, first_row):
        for row in range(4):
            for half in range(2):
                rows = slice(64 * row + 32 * half, 64 * row + 32 * half + 32)
                for row_y in range(2):
                    for j in range(3):
                        cols = slice(384 * row_y + 128 * j, 384 * row_y + 128 * j + 128)
                        dst[
                            row_y,
                            first_row + row,
                            half,
                            ROW_CONV + 32 * j : ROW_CONV + 32 * j + 32,
                        ] = din[rows, cols]
                    dst[row_y, first_row + row, half, 672:704] = dout[
                        rows, 128 * row_y : 128 * row_y + 128
                    ]

    def softmax(scores):
        powers = jnp.exp(scores - jnp.max(scores, -1, keepdims=True))
        return low(powers * (1.0 / jnp.sum(powers, -1, keepdims=True)))

    def attend(query, key, value, bias):
        probs = []
        for h in range(HEADS):
            scores = dot_nt(query * heads[h], key) * 0.125
            if bias is not None:
                scores = scores + bias[h]
            probs.append(softmax(scores))
        values = jnp.concatenate([value * heads[h] for h in range(HEADS)], 0)
        return low(dot_nn(jnp.concatenate(probs, 1), values)), probs

    def attend_back(query, key, value, dmix, probs, add_bias):
        dmix_t, query_t = dmix.T, query.T
        dscores, dkey_t, dvalue_t = [], [], []
        for h in range(HEADS):
            prob_low = probs(h)
            prob = prob_low.astype(jnp.float32)
            dprob = dot_nt(dmix * heads[h], value)
            dscore = prob * (dprob - jnp.sum(prob * dprob, -1, keepdims=True))
            if add_bias is not None:
                add_bias(h, dscore)
            dscore_low = low(dscore)
            dscores.append(dscore_low)
            rows = slice(64 * h, 64 * h + 64)
            dvalue_t.append(dot_nn(dmix_t[rows], prob_low))
            dkey_t.append(dot_nn(query_t[rows], dscore_low))
        keys = jnp.concatenate([key * heads[h] for h in range(HEADS)], 0)
        dquery = low(dot_nn(jnp.concatenate(dscores, 1), keys) * 0.125)
        dkey = low(jnp.concatenate(dkey_t, 0) * 0.125).T
        dvalue = low(jnp.concatenate(dvalue_t, 0)).T
        return jnp.concatenate([dquery, dkey, dvalue], 1)

    def slope_of(normed):
        sig = jax.nn.sigmoid(normed)
        return sig * (1.0 + normed * (1.0 - sig))

    def add_row(row, value):
        vec_acc[row : row + 1, :] += value

    def embed_input(rows):
        clip = clip_ref[rows, :]
        total = None
        for channel in range(3):
            part = clip[:, 3 + channel : 4 + channel] * win_ref[channel : channel + 1, :]
            total = part if total is None else total + part
        return total, clip

    fwd_bases = [16 + GAP * k for k in range(4)]

    def step_rows(step, n):
        return pl.ds(pl.multiple_of(step * 256 * n, 256 * n), 256 * n)

    def step_bases(step, n):
        return [pl.multiple_of(16 + GAP * (n * step + k), 16) for k in range(n)]

    def put_stage(step, values, n):
        for k in range(n // 2):
            pair = n // 2 * step + k
            woven = low(weave(values[512 * k : 512 * k + 512]))
            stage[pl.ds(32 * pair, 32)] = woven.reshape(32, 16, D)

    def from_pairs(step, src, n):
        return src[pl.ds(n // 2 * step, n // 2)].reshape(256 * n, D)

    def unweave_all(values):
        return jnp.concatenate(
            [unweave(values[start : start + 512]) for start in range(0, values.shape[0], 512)], 0
        )

    def send_pair(pair, dst, sems):
        for k, (peer, part) in enumerate(group):
            remote(
                stage.at[pl.ds(32 * pair + 8 * part, 8)],
                dst.at[:, 4 * quarter + pair],
                sems,
                (pair, k),
                (pair, k),
                peer,
            ).start()
        dst[:, 4 * quarter + pair] = stage[pl.ds(32 * pair + 8 * quarter, 8)]

    def wait_pairs(dst, sems):
        for pair in range(PAIRS):
            for k, (peer, part) in enumerate(group):
                copy = remote(
                    stage.at[pl.ds(32 * pair + 8 * part, 8)],
                    dst.at[:, 4 * part + pair],
                    sems,
                    (pair, k),
                    (pair, k),
                    peer,
                )
                copy.wait_send()
                copy.wait_recv()

    def block_tiles(src, block, part):
        return src.at[pl.ds(16 * block + 4 * part, 4)]

    def send_block(block, src, dst, sems):
        for k, (peer, part) in enumerate(group):
            remote(
                block_tiles(src, block, part),
                dst.at[:, quarter, block],
                sems,
                (block, k),
                (block, k),
                peer,
            ).start()
        dst[:, quarter, block] = block_tiles(src, block, quarter)[...]

    def wait_blocks(src, dst, sems):
        for block in range(8):
            for k, (peer, part) in enumerate(group):
                copy = remote(
                    block_tiles(src, block, part),
                    dst.at[:, part, block],
                    sems,
                    (block, k),
                    (block, k),
                    peer,
                )
                copy.wait_send()
                copy.wait_recv()

    def at_step(step, when, work):
        @pl.when(step == when)
        def _():
            work()

    def prob_away(step, n):
        some = pl.ds(n * step, n)
        return pltpu.make_async_copy(prob_one.at[some], prob_far.at[some], sem_prob.at[0, step])

    def prob_home(step, n):
        some = pl.ds(n * step, n)
        return pltpu.make_async_copy(prob_far.at[some], prob_one.at[some], sem_prob.at[1, step])

    def first_conv(step, carry):
        rows = step_rows(step, N_CONV)
        hidden, _ = embed_input(rows)
        normed, _ = rms(hidden, gain[0])
        put_shifts(shift_one, fwd_bases[:N_CONV], normed * jax.nn.sigmoid(normed))
        inner_zero[rows, :] = conv(shift_one, fwd_bases[:N_CONV], 0)
        at_step(step, 0 * (8 // N_CONV) // 4, lambda: gather_three(1))
        at_step(step, 2 * (8 // N_CONV) // 4, lambda: gather_three(2))
        at_step(step, 3 * (8 // N_CONV) // 4, lambda: gather_three(3))
        return carry

    lax.fori_loop(0, 8 // N_CONV, first_conv, 0)
    gather_four(1)
    unpack(range(4))
    pre_zero, bias_zero = time_project(0)

    def forward_step(step, carry):
        rows = step_rows(step, N_FORWARD)
        hidden, _ = embed_input(rows)
        inner = inner_zero[rows, :] + bias_zero
        inner_zero[rows, :] = inner
        normed, _ = rms(inner, gain[1])
        put_shifts(shift_two, fwd_bases[:N_FORWARD], normed * jax.nn.sigmoid(normed))
        hidden = hidden + conv(shift_two, fwd_bases[:N_FORWARD], 1)
        hid_one[rows, :] = hidden
        normed, _ = rms(hidden, gain[2])
        packed = low(dot_nn(low(normed), proj[0]))
        pack_zero[rows, :] = packed
        mixed = []
        for k in range(N_FORWARD):
            part = packed[256 * k : 256 * k + 256]
            one, probs = attend(part[:, :D], part[:, D : 2 * D], part[:, 2 * D :], None)
            for h in range(HEADS):
                prob_one[N_FORWARD * step + k, h] = probs[h]
            mixed.append(one)
        prob_away(step, N_FORWARD).start()
        mixed = jnp.concatenate(mixed, 0)
        mix_zero[rows, :] = mixed
        hidden = hidden + dot_nn(mixed, outp[0])
        hid_two[rows, :] = hidden
        normed, _ = rms(hidden, gain[3])
        put_stage(step, normed, N_FORWARD)
        for k in range(N_FORWARD // 2):
            send_pair(N_FORWARD // 2 * step + k, spread_norm, sem_n)
        return carry

    lax.fori_loop(0, 8 // N_FORWARD, forward_step, 0)
    gather_four(2)
    gather_four(3)
    gather_sent()
    unpack(range(4, 8))
    pre_one, bias_one = time_project(1)
    wait_pairs(spread_norm, sem_n)
    for step in range(8 // N_FORWARD):
        prob_away(step, N_FORWARD).wait()

    def temporal_blocks(turn, carry):
        blocks = [BLOCKS * turn + k for k in range(BLOCKS)]
        tables = [table_ref[h] for h in range(HEADS)]
        packs = [
            low(dot_nn(spread_norm[block].reshape(256, D), proj[1])) for block in blocks
        ]
        results = [
            attend(packed[:, :D], packed[:, D : 2 * D], packed[:, 2 * D :], tables)
            for packed in packs
        ]
        for block, packed, (mixed, probs) in zip(blocks, packs, results):
            pack_one[block] = packed
            for h in range(HEADS):
                prob_one[block, h] = probs[h]
            mix_one[pl.ds(16 * block, 16)] = mixed.reshape(16, 16, D)
        for block in blocks:
            send_block(block, mix_one, mix_back, sem_m)
        return carry

    lax.fori_loop(0, 8 // BLOCKS, temporal_blocks, 0)
    wait_blocks(mix_one, mix_back, sem_m)

    pixel_total = jnp.full((1, 1), frames_total(count_ref), jnp.int32).astype(jnp.float32) * 256.0
    scale = 2.0 / pixel_total
    wout_low = low(wout_ref[...]).astype(jnp.float32)

    def last_step(step, carry):
        rows = step_rows(step, N_LAST)
        bases = step_bases(step, N_LAST)
        lanes = step_rows(step, N_LAST)
        hidden = hid_two[rows, :] + unweave_all(dot_nn(from_pairs(step, mix_back, N_LAST), outp[1]))
        dhid[rows, :] = hidden
        normed, inverse = rms(hidden, gain[4])
        sig = jax.nn.sigmoid(normed)
        acts = normed * sig
        put_shifts(shift_one, bases, acts)
        act_one[:, lanes] = low(acts).T
        inner = conv(shift_one, bases, 2) + bias_one
        normed_two, inverse_two = rms(inner, gain[5])
        sig_two = jax.nn.sigmoid(normed_two)
        acts_two = normed_two * sig_two
        put_shifts(shift_two, bases, acts_two)
        act_two[:, lanes] = low(acts_two).T
        last = dhid[rows, :] + conv(shift_two, bases, 3)
        normed, inverse_six = rms(last, gain[6])
        normed_low = low(normed)
        pred = dot_nt(normed_low, low(head_pad[...]))
        clip = clip_ref[rows, :]
        frame_id = lax.broadcasted_iota(jnp.int32, (256 * N_LAST, 128), 0) // 256
        frame_id = frame_id + (8 * quarter + N_LAST * step)
        valid = jnp.where(frame_id < count, 1.0, 0.0)
        lane = lax.broadcasted_iota(jnp.int32, (256 * N_LAST, 128), 1)
        error = jnp.where(lane < 3, pred - clip, 0.0)
        weighted = error * valid
        vec_acc[7:8, 0:128] += jnp.sum(weighted * error, 0, keepdims=True)
        dpred = weighted * scale
        dpred_hi = low(dpred)
        dpred_lo = low(dpred - dpred_hi.astype(jnp.float32))
        acc_out[...] += (dot_tn(dpred_hi, normed_low) + dot_tn(dpred_lo, normed_low))[0:8]
        dnormed = None
        for channel in range(3):
            part = dpred[:, channel : channel + 1] * wout_low[channel : channel + 1, :]
            dnormed = part if dnormed is None else dnormed + part
        dlast, dgain = rms_back(last, inverse_six, gain[6], dnormed)
        add_row(6, dgain)
        put_shifts(shift_two, bases, low(dlast).astype(jnp.float32))
        dnormed = conv_back(shift_two, bases, 3) * slope_of(rms(inner, gain[5])[0])
        dinner, dgain = rms_back(inner, inverse_two, gain[5], dnormed)
        add_row(5, dgain)
        add_row(15, jnp.sum(dinner, 0, keepdims=True))
        put_shifts(shift_one, bases, low(dinner).astype(jnp.float32))
        dnormed = conv_back(shift_one, bases, 2) * slope_of(rms(dhid[rows, :], gain[4])[0])
        dhidden, dgain = rms_back(dhid[rows, :], inverse, gain[4], dnormed)
        add_row(4, dgain)
        dhidden = dhidden + dlast
        dhid[rows, :] = dhidden
        put_stage(step, dhidden, N_LAST)
        for k in range(N_LAST // 2):
            send_pair(N_LAST // 2 * step + k, dout_pix, sem_dy)
        return carry

    lax.fori_loop(0, 8 // N_LAST, last_step, 0)
    conv_grad(act_two, shift_two, 3, wall, 6)
    conv_grad(act_one, shift_one, 2, wall, 4)
    wait_pairs(dout_pix, sem_dy)

    bias_acc = table_ref
    bias_acc[...] = jnp.zeros_like(bias_acc)

    def temporal_back(turn, carry):
        blocks = [BLOCKS * turn + k for k in range(BLOCKS)]
        sums = [[] for _ in range(HEADS)]
        results = []
        for block in blocks:
            dmix = low(dot_nt(dout_pix[block].reshape(256, D), outp[1]))
            packed = pack_one[block]
            results.append(
                attend_back(
                    packed[:, :D],
                    packed[:, D : 2 * D],
                    packed[:, 2 * D :],
                    dmix,
                    lambda h, block=block: prob_one[block, h],
                    lambda h, dscore: sums[h].append(dscore),
                )
            )
        for h in range(HEADS):
            bias_acc[h] += sum(sums[h][1:], sums[h][0])
        dnorms = [low(dot_nt(dpacked, proj[1])) for dpacked in results]
        for block, dpacked, dnorm in zip(blocks, results, dnorms):
            pack_one[block] = dpacked
            stage[pl.ds(16 * block, 16)] = dnorm.reshape(16, 16, D)
        for block in blocks:
            send_block(block, stage, mix_back, sem_dn)
        return carry

    lax.fori_loop(0, 8 // BLOCKS, temporal_back, 0)
    for step in range(8 // N_BACK):
        prob_home(step, N_BACK).start()
    flat = (2048, D)
    dout_one = low(dot_tn(mix_one[...].reshape(flat), dout_pix[...].reshape(flat)))
    din_one = low(dot_tn(spread_norm[...].reshape(flat), pack_one[...].reshape(2048, 3 * D)))
    put_proj_grad(1, din_one, dout_one, wall, 4)
    wait_blocks(stage, mix_back, sem_dn)

    def slab(k):
        return (wall, 2 * k) if k >= 2 else (dslab, 2 * k)

    top, low_half = pl.ds(0, HALF), pl.ds(HALF, HALF)

    def red_one(k):
        src, row = slab(k)
        return remote(
            src.at[:, pl.ds(row, 2), oc, pl.ds(0, ROW_GRAD)], red_sib.at[k], sem_red, (k, 0), (k, 0), sibling
        )

    def red_two(k):
        src, row = slab(k)
        return (
            remote(src.at[:, row + ox, c, top], red_a.at[k], sem_red, (k, 1), (k, 1), x_peer),
            remote(src.at[oy, pl.ds(row, 2), c, low_half], red_b.at[k], sem_red, (k, 2), (k, 2), y_peer),
        )

    def red_three(k):
        src, row = slab(k)
        return (
            remote(src.at[oy, row + x, c, top], red_c.at[k], sem_red, (k, 3), (k, 3), y_peer),
            remote(src.at[y, row + ox, c, low_half], red_d.at[k], sem_red, (k, 4), (k, 4), x_peer),
        )

    def both(left, right):
        return low(left.astype(jnp.float32) + right.astype(jnp.float32))

    def finish(copies):
        for copy in copies:
            copy.wait_send()
            copy.wait_recv()

    def add_one(k):
        src, row = slab(k)
        for row_y in range(2):
            for row_x in range(2):
                src[row_y, row + row_x, c, 0:ROW_GRAD] = both(
                    src[row_y, row + row_x, c, 0:ROW_GRAD], red_sib[k, row_y, row_x]
                )

    def add_two(k):
        src, row = slab(k)
        for part in range(2):
            src[part, row + x, c, 0:HALF] = both(src[part, row + x, c, 0:HALF], red_a[k, part])
            src[y, row + part, c, HALF:ROW_GRAD] = both(
                src[y, row + part, c, HALF:ROW_GRAD], red_b[k, part]
            )

    def add_three(k):
        src, row = slab(k)
        src[y, row + x, c, 0:HALF] = both(src[y, row + x, c, 0:HALF], red_c[k])
        src[y, row + x, c, HALF:ROW_GRAD] = both(src[y, row + x, c, HALF:ROW_GRAD], red_d[k])

    def z_copy(k):
        slot = (z + 3 - k) % 4
        src, row = slab(k)
        here = src.at[y, row + x, c, pl.ds(0, ROW_GRAD)]
        return remote(here, red_z.at[slot], sem_fin, (k,), (slot,), (2 * k + x, ba))

    def send_z(k):
        @pl.when(z != k)
        def _():
            z_copy(k).start()

    def start_all(copies):
        for copy in copies:
            copy.start()

    def spatial_back(step, carry):
        rows = step_rows(step, N_BACK)
        bases = step_bases(step, N_BACK)
        lanes = step_rows(step, N_BACK)
        dnormed = unweave_all(from_pairs(step, mix_back, N_BACK).astype(jnp.float32))
        hidden = hid_two[rows, :]
        _, inverse = rms(hidden, gain[3])
        dhidden, dgain = rms_back(hidden, inverse, gain[3], dnormed)
        add_row(3, dgain)
        dhidden = dhidden + dhid[rows, :]
        grad_low = low(dhidden)
        dout_pix[pl.ds(N_BACK * step, N_BACK)] = grad_low.reshape(N_BACK, 16, 16, D)
        dmix = low(dot_nt(grad_low, outp[0]))
        packed = pack_zero[rows, :]
        dpacked = []
        prob_home(step, N_BACK).wait()
        for k in range(N_BACK):
            part = packed[256 * k : 256 * k + 256]
            dpacked.append(
                attend_back(
                    part[:, :D],
                    part[:, D : 2 * D],
                    part[:, 2 * D :],
                    dmix[256 * k : 256 * k + 256],
                    lambda h, k=k: prob_one[N_BACK * step + k, h],
                    None,
                )
            )
        dpacked = jnp.concatenate(dpacked, 0)
        pack_zero[rows, :] = dpacked
        hidden = hid_one[rows, :]
        normed, inverse = rms(hidden, gain[2])
        spread_norm[pl.ds(N_BACK * step, N_BACK)] = low(normed).reshape(
            N_BACK, 16, 16, D
        )
        dnormed = dot_nt(dpacked, proj[0])
        dprev, dgain = rms_back(hidden, inverse, gain[2], dnormed)
        add_row(2, dgain)
        dhidden = dhidden + dprev
        dhid[rows, :] = dhidden
        put_shifts(shift_two, bases, low(dhidden).astype(jnp.float32))
        normed, _ = rms(inner_zero[rows, :], gain[1])
        act_two[:, lanes] = low(normed * jax.nn.sigmoid(normed)).T
        at_step(step, 1 * (8 // N_BACK) // 4, lambda: one_to_two(3))
        at_step(step, 2 * (8 // N_BACK) // 4, lambda: one_to_two(2))
        at_step(step, 3 * (8 // N_BACK) // 4, lambda: two_to_three(3))
        return carry

    def one_to_two(k):
        finish([red_one(k)])
        add_one(k)
        start_all(red_two(k))

    def two_to_three(k):
        finish(red_two(k))
        add_two(k)
        start_all(red_three(k))

    def three_to_z(k):
        finish(red_three(k))
        add_three(k)
        send_z(k)

    start_all([red_one(3), red_one(2)])
    lax.fori_loop(0, 8 // N_BACK, spatial_back, 0)
    two_to_three(2)
    din_zero = low(dot_tn(spread_norm[...].reshape(flat), pack_zero[...]))
    dout_zero = low(dot_tn(mix_zero[...], dout_pix[...].reshape(flat)))
    put_proj_grad(0, din_zero, dout_zero, dslab, 0)
    conv_grad(act_two, shift_two, 1, dslab, 2)
    start_all([red_one(1)])

    def first_back(step, carry):
        rows = step_rows(step, N_FIRST)
        bases = step_bases(step, N_FIRST)
        lanes = step_rows(step, N_FIRST)
        inner = inner_zero[rows, :]
        normed, inverse = rms(inner, gain[1])
        sig = jax.nn.sigmoid(normed)
        dnormed = conv_back(shift_two, bases, 1) * (sig * (1.0 + normed * (1.0 - sig)))
        dinner, dgain = rms_back(inner, inverse, gain[1], dnormed)
        add_row(1, dgain)
        add_row(14, jnp.sum(dinner, 0, keepdims=True))
        put_shifts(shift_one, bases, low(dinner).astype(jnp.float32))
        hidden, _ = embed_input(rows)
        normed, _ = rms(hidden, gain[0])
        act_one[:, lanes] = low(normed * jax.nn.sigmoid(normed)).T
        at_step(step, 0 * (8 // N_FIRST) // 4, lambda: three_to_z(3))
        at_step(step, 1 * (8 // N_FIRST) // 4, lambda: one_to_two(1))
        at_step(step, 2 * (8 // N_FIRST) // 4, lambda: three_to_z(2))
        return carry

    lax.fori_loop(0, 8 // N_FIRST, first_back, 0)
    conv_grad(act_one, shift_one, 0, dslab, 0)
    start_all([red_one(0)])
    two_to_three(1)

    def input_back(step, carry):
        rows = step_rows(step, N_INPUT)
        bases = step_bases(step, N_INPUT)
        hidden, clip = embed_input(rows)
        normed, inverse = rms(hidden, gain[0])
        sig = jax.nn.sigmoid(normed)
        dnormed = conv_back(shift_one, bases, 0) * (sig * (1.0 + normed * (1.0 - sig)))
        dhidden, dgain = rms_back(hidden, inverse, gain[0], dnormed)
        add_row(0, dgain)
        dhidden = dhidden + dhid[rows, :]
        for channel in range(3):
            add_row(
                8 + channel,
                jnp.sum(clip[:, 3 + channel : 4 + channel] * dhidden, 0, keepdims=True),
            )
        at_step(step, 0 * (8 // N_INPUT) // 4, lambda: one_to_two(0))
        at_step(step, 1 * (8 // N_INPUT) // 4, lambda: three_to_z(1))
        at_step(step, 3 * (8 // N_INPUT) // 4, lambda: two_to_three(0))
        return carry

    lax.fori_loop(0, 8 // N_INPUT, input_back, 0)
    vec_acc[11:14, :] = acc_out[0:3, :]
    fold = lax.broadcasted_iota(jnp.int32, (256, 128), 0) // 8
    fold_lane = lax.broadcasted_iota(jnp.int32, (256, 128), 1)
    left = jnp.where(fold == fold_lane, 1.0, 0.0)
    table = None
    for h in range(HEADS):
        right = jnp.where(fold + 32 * h == fold_lane, 1.0, 0.0)
        wide = lax.dot_general(
            bias_acc[h], right, (((1,), (0,)), ((), ())), precision=HIGH, preferred_element_type=jnp.float32
        )
        part = lax.dot_general(
            left, wide, (((0,), (0,)), ((), ())), precision=HIGH, preferred_element_type=jnp.float32
        )
        table = part if table is None else table + part
    away = fold_lane[0:32] % 32 - lax.broadcasted_iota(jnp.int32, (32, 128), 0)
    bucket = jnp.minimum(jnp.abs(away), 15) + jnp.where(away > 0, 16, 0)
    bucket_rows = lax.broadcasted_iota(jnp.int32, (32, 128), 0)
    by_bucket = jnp.zeros((32, 128), jnp.float32)
    for k in range(32):
        one = jnp.sum(jnp.where(bucket == k, table[0:32], 0.0), 0, keepdims=True)
        by_bucket = jnp.where(bucket_rows == k, one, by_bucket)
    head_row = lax.broadcasted_iota(jnp.int32, (8, 128), 0)
    head_lane = lax.broadcasted_iota(jnp.int32, (8, 128), 1)
    pick = jnp.where(head_lane // 32 == head_row, 1.0, 0.0)
    table_sum = lax.dot_general(
        pick, by_bucket, (((1,), (1,)), ((), ())), precision=HIGH, preferred_element_type=jnp.float32
    )
    vec_acc[32:40, 0:32] = table_sum
    row_ids = lax.broadcasted_iota(jnp.int32, (16, D), 0)
    slots = jnp.zeros((16, D), jnp.float32)
    for layer in range(2):
        pre = (pre_zero, pre_one)[layer]
        sig = jax.nn.sigmoid(pre)
        dpre = vec_acc[14 + layer : 15 + layer, :] * (sig * (1.0 + pre * (1.0 - sig)))
        slots = jnp.where(row_ids == 8 * layer + video, dpre, slots)
    vec_acc[16:32, :] = slots

    spot = 4 * x + 2 * y + c

    def plane_copies(values, received, sems):
        return [
            remote(values, received.at[spot], sems, (k,), (spot,), peer)
            for k, peer in enumerate(plane)
        ]

    def plane_total(values, received, sems):
        for px, py, pc in (
            (x, y, oc), (x, oy, c), (x, oy, oc), (ox, y, c), (ox, y, oc), (ox, oy, c), (ox, oy, oc)
        ):
            slot = 4 * px + 2 * py + pc
            remote(values, received.at[slot], sems, (0,), (slot,), sibling).wait_recv()
        for copy in plane_copies(values, received, sems):
            copy.wait_send()
        received[spot] = values[...]
        total = received[0]
        for k in range(1, 8):
            total = total + received[k]
        values[...] = total

    def z_total_copies(values, received, sems):
        return [
            remote(values, received.at[8 + 2 - k], sems, (8 + k,), (8 + 2 - k,), peer)
            for k, peer in enumerate(z_peers)
        ]

    def z_total(values, received, sems):
        finish(z_total_copies(values, received, sems))
        return (values[...] + received[9]) + (received[8] + received[10])

    def quarter_copies():
        return [
            remote(
                dslab.at[y, x, c, pl.ds(pl.multiple_of(QUARTER * z_ids[k], 16), QUARTER)],
                red_q.at[2 - k],
                sem_q,
                (k,),
                (2 - k,),
                peer,
            )
            for k, peer in enumerate(z_peers)
        ]

    def quarter_home():
        slot = jnp.maximum(z - 1, 0)
        return remote(quarter_sum, red_back.at[slot], sem_back, (0,), (slot,), (x, ba))

    start_all(plane_copies(vec_acc, vec_recv, sem_vec))
    finish(red_three(0))
    add_three(0)
    start_all(quarter_copies())
    plane_total(vec_acc, vec_recv, sem_vec)
    start_all(z_total_copies(vec_acc, vec_recv, sem_vec))
    vector = z_total(vec_acc, vec_recv, sem_vec)
    vector_ref[...] = vector
    small = jnp.sum(vector[0:7] * vector[0:7]) + jnp.sum(vector[8:14] * vector[8:14])
    small = small + jnp.sum(vector[32:36, 0:32] * vector[32:36, 0:32])
    for layer in range(2):
        dtime = lax.dot_general(
            video_ref[:, 0:D],
            vector[16 + 8 * layer : 24 + 8 * layer],
            (((0,), (0,)), ((), ())),
            precision=HIGH,
            preferred_element_type=jnp.float32,
        )
        hid_one[256 * layer : 256 * layer + 256, :] = dtime
        small = small + jnp.sum(dtime * dtime)
    dtime_ref[...] = hid_one[pl.ds(pl.multiple_of(64 * fr, 64), 64), :]
    finish(quarter_copies())
    quarter = dslab[y, x, c, pl.ds(pl.multiple_of(QUARTER * z, 16), QUARTER), :].astype(jnp.float32)
    for slot in range(3):
        quarter = quarter + red_q[slot].astype(jnp.float32)
    quarter_sum[...] = low(quarter)
    own_sums = remote(grads_ref.at[c], final_recv, sem_fin, (4,), (4,), sibling)

    @pl.when(z == 0)
    def _():
        grads_ref[c] = jnp.zeros((ROW_GRAD, 128), jnp.float32)

    @pl.when(z > 0)
    def _():
        quarter_home().start()
        total = jnp.where(
            z >= 2,
            wall[y, fr, c, 0:ROW_GRAD].astype(jnp.float32),
            dslab[y, jnp.minimum(fr, 3), c].astype(jnp.float32),
        )
        for slot in range(3):
            arrive(red_z.at[slot], sem_fin, (slot,))
            total = total + red_z[slot].astype(jnp.float32)
        grads_ref[c] = total
        own_sums.start()

    square = jnp.sum(quarter * quarter, 0, keepdims=True)
    square = square + jnp.sum(grads_ref[c] * grads_ref[c], 0, keepdims=True)
    sq_acc[...] = jnp.broadcast_to(jnp.sum(square, 1, keepdims=True), (8, 128))
    start_all(plane_copies(sq_acc, sq_recv, sem_sq))

    @pl.when(z == 0)
    def _():
        grads_ref[c, 0:QUARTER] = quarter
        for slot in range(3):
            arrive(red_back.at[slot], sem_back, (slot,))
            start = QUARTER * (slot + 1)
            grads_ref[c, start : start + QUARTER] = red_back[slot].astype(jnp.float32)
        own_sums.start()

    plane_total(sq_acc, sq_recv, sem_sq)
    start_all(z_total_copies(sq_acc, sq_recv, sem_sq))
    own_sums.wait_send()
    arrive(final_recv, sem_fin, (4,))
    grads_ref[oc] = final_recv[...]
    for k in range(1, 4):

        @pl.when(z != k)
        def _():
            z_copy(k).wait_send()

    @pl.when(z > 0)
    def _():
        quarter_home().wait_send()

    squares_ref[...] = z_total(sq_acc, sq_recv, sem_sq) + small


def dot_exact(lhs, rhs, dims):
    return lax.dot_general(
        lhs, rhs, (dims, ((), ())), precision=HIGH, preferred_element_type=jnp.float32
    )


def update_kernel(*refs):
    sums_ref, vector_ref, squares_ref, dtime_ref, count_ref = refs[:5]
    state, outs = refs[5:29], refs[29:]
    fr = lax.axis_index("frame")
    ba = lax.axis_index("batch")
    c = ba % 2

    def spots(rows, columns, shift):
        row = lax.broadcasted_iota(jnp.int32, (rows, columns), 0)
        column = lax.broadcasted_iota(jnp.int32, (rows, columns), 1)
        return jnp.where(row + shift == column, 1.0, 0.0)

    norm = jnp.sqrt(squares_ref[0:1, 0:1])
    clip_scale = CLIP / jnp.maximum(norm, CLIP)
    frames_all = frames_total(count_ref)
    outs[0][...] = jnp.sum(vector_ref[7:8, :], 1, keepdims=True)
    outs[1][...] = jnp.full((1, 1), frames_all, jnp.int32).astype(jnp.float32) * 256.0
    outs[2][...] = norm
    pick = spots(64, 128, 64 * c)
    conv_rows = jnp.concatenate([sums_ref[0, 0:ROW_CONV], sums_ref[1, 0:ROW_CONV]], 0)
    pin, pout = [], []
    for half in range(2):
        rows = None
        for j in range(3):
            part = dot_exact(
                sums_ref[half, ROW_CONV + 32 * j : ROW_CONV + 32 * j + 32],
                spots(192, 128, 192 * c - 128 * j),
                ((1,), (1,)),
            )
            rows = part if rows is None else rows + part
        pin.append(rows)
        pout.append(dot_exact(sums_ref[half, 672:704], pick, ((1,), (1,))))
    time_rows = dtime_ref[...]
    grads = [
        dot_exact(pick, conv_rows, ((1,), (1,))),
        jnp.concatenate(pin, 0),
        jnp.concatenate(pout, 0),
        dot_exact(time_rows, spots(64, 256, 64 * ba), ((1,), (1,))),
        vector_ref[8:11, :],
        vector_ref[11:14, :],
        vector_ref[0:7, :],
        vector_ref[32:36, 0:32],
    ]
    for k, grad in enumerate(grads):
        weight, first, second = (ref[...] for ref in state[3 * k : 3 * k + 3])
        news = adamw(weight, first, second, grad, clip_scale, RATES[k])
        for ref, value in zip(outs[3 + 3 * k : 6 + 3 * k], news):
            ref[...] = value


def shards_pairs(
    clean,
    noise,
    timesteps,
    frame_counts,
    conv_weight,
    conv_first,
    conv_second,
    proj_in,
    proj_in_first,
    proj_in_second,
    proj_out,
    proj_out_first,
    proj_out_second,
    time_weight,
    time_first,
    time_second,
    in_weight,
    in_first,
    in_second,
    out_weight,
    out_first,
    out_second,
    gains,
    gains_first,
    gains_second,
    rel_bias,
    rel_bias_first,
    rel_bias_second,
):

    counts = frame_counts.transpose(0, 2, 1)
    bf16, f32 = jnp.bfloat16, jnp.float32
    vmem = pl.BlockSpec(memory_space=pltpu.VMEM)
    smem = pl.BlockSpec(memory_space=pltpu.SMEM)
    scratch = [
        pltpu.VMEM((2, 8, 2, ROW_ALL, 128), bf16),
        pltpu.VMEM((2, 4, 2, ROW_GRAD, 128), bf16),
        pltpu.VMEM((2, D, 3 * D), bf16),
        pltpu.VMEM((2, D, D), bf16),
        pltpu.VMEM((ROW_ALL, 128), bf16),
        pltpu.VMEM((2, ROW_ALL, 128), bf16),
        pltpu.VMEM((2, 2, 3, 4, 256), f32),
        pltpu.VMEM((8, 8, 256), f32),
        pltpu.VMEM((2048, 128), f32),
        pltpu.VMEM((8, 384), f32),
        pltpu.VMEM((HEADS, 256, 256), f32),
        pltpu.VMEM((128, D), f32),
        pltpu.VMEM((2048, D), f32),
        pltpu.VMEM((2048, D), f32),
        pltpu.VMEM((2048, D), f32),
        pltpu.VMEM((2048, D), f32),
        pltpu.VMEM((2048, 3 * D), bf16),
        pltpu.VMEM((2048, D), bf16),
        pltpu.VMEM((8, 16, 16, D), bf16),
        pltpu.VMEM((8, 256, 3 * D), bf16),
        pltpu.VMEM((8, HEADS, 256, 256), bf16),
        pltpu.VMEM((128, 16, D), bf16),
        pltpu.VMEM((PAIRS, 4, 8, 16, D), bf16),
        pltpu.VMEM((8, 16, 16, D), bf16),
        pltpu.VMEM((128, 16, D), bf16),
        pltpu.VMEM((3, 8 * GAP + 16, D), bf16),
        pltpu.VMEM((3, 8 * GAP + 16, D), bf16),
        pltpu.VMEM((D, 2048), bf16),
        pltpu.VMEM((D, 2048), bf16),
        pltpu.VMEM((8, D), f32),
        pltpu.VMEM((4, 2, 2, ROW_GRAD, 128), bf16),
        pltpu.VMEM((4, 2, HALF, 128), bf16),
        pltpu.VMEM((4, 2, HALF, 128), bf16),
        pltpu.VMEM((4, HALF, 128), bf16),
        pltpu.VMEM((4, HALF, 128), bf16),
        pltpu.VMEM((3, ROW_GRAD, 128), bf16),
        pltpu.VMEM((ROW_GRAD, 128), f32),
        pltpu.VMEM((3, QUARTER, 128), bf16),
        pltpu.VMEM((3, QUARTER, 128), bf16),
        pltpu.VMEM((QUARTER, 128), bf16),
        pltpu.VMEM((40, D), f32),
        pltpu.VMEM((11, 40, D), f32),
        pltpu.VMEM((8, 128), f32),
        pltpu.VMEM((11, 8, 128), f32),
        pltpu.SemaphoreType.DMA((2, 4, 2, 2)),
        pltpu.SemaphoreType.DMA((2, 4, 2)),
        pltpu.SemaphoreType.DMA((2, 4, 2)),
        pltpu.SemaphoreType.DMA((2, 4, 2)),
        pltpu.SemaphoreType.DMA((2, 4, 2)),
        pltpu.SemaphoreType.DMA((2, 4)),
        pltpu.SemaphoreType.DMA((2, 4)),
        pltpu.SemaphoreType.DMA((2, PAIRS, 3)),
        pltpu.SemaphoreType.DMA((2, 8, 3)),
        pltpu.SemaphoreType.DMA((2, PAIRS, 3)),
        pltpu.SemaphoreType.DMA((2, 8, 3)),
        pltpu.SemaphoreType.DMA((2, 4, 5)),
        pltpu.SemaphoreType.DMA((2, 5)),
        pltpu.SemaphoreType.DMA((2, 3)),
        pltpu.SemaphoreType.DMA((2, 3)),
        pltpu.SemaphoreType.DMA((2, 12)),
        pltpu.SemaphoreType.DMA((2, 12)),
        pltpu.SemaphoreType.DMA((2, 2, 2)),
        pltpu.SemaphoreType.DMA((2, 4)),
    ]
    sums, vector, squares, dtime, _ = pl.pallas_call(
        step_kernel,
        out_shape=(
            jax.ShapeDtypeStruct((2, ROW_GRAD, 128), f32),
            jax.ShapeDtypeStruct((40, D), f32),
            jax.ShapeDtypeStruct((8, 128), f32),
            jax.ShapeDtypeStruct((64, D), f32),
            jax.ShapeDtypeStruct((8, HEADS, 256, 256), bf16),
        ),
        in_specs=[vmem, vmem, smem, smem] + [vmem] * 7 + [smem],
        out_specs=(vmem,) * 4 + (pl.BlockSpec(memory_space=pl.ANY),),
        scratch_shapes=scratch,
        compiler_params=pltpu.CompilerParams(
            collective_id=0, has_side_effects=True, vmem_limit_bytes=64 * 2**20 - 2**16
        ),
        name="train_step",
    )(
        clean.transpose(0, 1, 3, 2, 4),
        noise.transpose(0, 1, 3, 2, 4),
        counts,
        timesteps.transpose(0, 2, 1),
        conv_weight.T,
        proj_in,
        proj_out,
        time_weight,
        in_weight,
        out_weight,
        gains,
        rel_bias,
    )
    state = (
        conv_weight.T,
        conv_first.T,
        conv_second.T,
        proj_in,
        proj_in_first,
        proj_in_second,
        proj_out,
        proj_out_first,
        proj_out_second,
        time_weight,
        time_first,
        time_second,
        in_weight,
        in_first,
        in_second,
        out_weight,
        out_first,
        out_second,
        gains,
        gains_first,
        gains_second,
        rel_bias,
        rel_bias_first,
        rel_bias_second,
    )
    scalar = jax.ShapeDtypeStruct((1, 1), f32)
    results = pl.pallas_call(
        update_kernel,
        out_shape=[scalar] * 3 + [jax.ShapeDtypeStruct(value.shape, f32) for value in state],
        in_specs=[vmem] * 4 + [smem] + [vmem] * 24,
        out_specs=[vmem] * 27,
        compiler_params=pltpu.CompilerParams(vmem_limit_bytes=64 * 2**20 - 2**16),
        name="update",
    )(sums, vector, squares, dtime, counts, *state)
    return (
        *(value.reshape(()) for value in results[:3]),
        *(value.T for value in results[3:6]),
        *results[6:],
    )


def shards(
    clean,
    noise,
    timesteps,
    frame_counts,
    conv_weight,
    conv_first,
    conv_second,
    proj_in,
    proj_in_first,
    proj_in_second,
    proj_out,
    proj_out_first,
    proj_out_second,
    time_weight,
    time_first,
    time_second,
    in_weight,
    in_first,
    in_second,
    out_weight,
    out_first,
    out_second,
    gains,
    gains_first,
    gains_second,
    rel_bias,
    rel_bias_first,
    rel_bias_second,
):
    fr_dev = clean.shape[2]
    pixels = clean.shape[4]
    videos = timesteps.shape[2]
    pix_dev = pixels // lax.axis_size("frame")
    group_idx = lax.axis_index("batch")
    frame_ids = lax.axis_index("frame") * fr_dev + jnp.arange(fr_dev)
    member = (frame_ids[:, None] // FRAMES == jnp.arange(videos)[None, :]).astype(jnp.float32)
    frame_place = frame_ids % FRAMES
    pixel_total = jnp.sum(frame_counts).astype(jnp.float32) * pixels
    offsets = jnp.arange(FRAMES)
    distance = offsets[None, :] - offsets[:, None]
    bucket = jnp.minimum(jnp.abs(distance), 15) + 16 * (distance > 0).astype(jnp.int32)
    onehot = (bucket[:, :, None] == jnp.arange(rel_bias.shape[1])[None, None, :]).astype(
        jnp.float32
    )
    bias_mat = jnp.einsum("hk,lmk->hlm", rel_bias, onehot, precision=HIGH)
    half_width = D // 2
    frequency = jnp.exp(-math.log(10000.0) * jnp.arange(half_width, dtype=jnp.float32) / half_width)
    out_low = out_weight.astype(jnp.bfloat16)
    matrix_acc = None
    vector_acc = None
    loss_local = jnp.zeros((), jnp.float32)
    for micro_idx in range(MICRO):
        gathered = fetch(conv_weight, proj_in, proj_out, time_weight)
        kernels = gathered[0].reshape(4, 9 * D, D)
        w_in = gathered[1].reshape(2, D, 3 * D)
        w_out = gathered[2].reshape(2, D, D)
        w_time = gathered[3].reshape(2, D, D)
        steps_grp = lax.dynamic_index_in_dim(timesteps[micro_idx], group_idx, 0, keepdims=False)
        count_grp = lax.dynamic_index_in_dim(frame_counts[micro_idx], group_idx, 0, keepdims=False)
        levels = steps_grp.astype(jnp.float32)
        embedding = jnp.concatenate(
            [jnp.sin(levels[:, None] * frequency), jnp.cos(levels[:, None] * frequency)], -1
        ).astype(jnp.bfloat16)
        time_pre = jnp.einsum("vd,jde->jve", embedding, w_time, preferred_element_type=jnp.float32)
        frame_bias = jnp.einsum("fv,jvd->jfd", member, swish(time_pre), precision=HIGH)[
            :, :, None, :
        ]
        frame_level = jnp.dot(member, levels, precision=HIGH)
        alpha_bar = jnp.cos(0.5 * math.pi * (frame_level + 1.0) / (TSTEPS + 1.0)) ** 2
        target = noise[micro_idx, 0]
        noisy_input = (
            jnp.sqrt(alpha_bar)[:, None, None] * clean[micro_idx, 0]
            + jnp.sqrt(1.0 - alpha_bar)[:, None, None] * target
        )
        frame_count = jnp.sum(member * count_grp.astype(jnp.float32)[None, :], 1)
        live_frames = (frame_place.astype(jnp.float32) < frame_count).astype(jnp.float32)
        valid_video = offsets[None, :] < count_grp[:, None]
        valid_rows = jnp.broadcast_to(valid_video[:, None, :], (videos, pix_dev, FRAMES)).reshape(
            videos * pix_dev, FRAMES
        )
        context = (videos, bias_mat, valid_rows, onehot)
        hidden_zero = jnp.einsum("fcp,cd->fpd", noisy_input, in_weight, precision=HIGH)
        hidden_one, saved_zero = res_fwd(
            hidden_zero, kernels[0], kernels[1], gains[0], gains[1], frame_bias[0]
        )
        hidden_two, saved_spatial = mixer_fwd(hidden_one, gains[2], w_in[0], w_out[0], None)
        hidden_three, saved_temporal = mixer_fwd(hidden_two, gains[3], w_in[1], w_out[1], context)
        hidden_four, saved_last = res_fwd(
            hidden_three, kernels[2], kernels[3], gains[4], gains[5], frame_bias[1]
        )
        normed, inverse = norm_fwd(hidden_four, gains[6])
        normed_low = normed.astype(jnp.bfloat16)
        predicted = jnp.einsum(
            "fpd,cd->fcp", normed_low, out_low, preferred_element_type=jnp.float32
        )
        pred_error = predicted - target
        weighted = live_frames[:, None, None] * pred_error
        loss_local = loss_local + jnp.sum(weighted * pred_error)
        dpred = 2.0 * weighted / pixel_total
        d_out = jnp.einsum("fcp,fpd->cd", dpred, normed_low.astype(jnp.float32), precision=HIGH)
        dnormed = jnp.einsum("fcp,cd->fpd", dpred, out_low.astype(jnp.float32), precision=HIGH)
        dhid_four, dgain_six = norm_bwd(hidden_four, inverse, gains[6], dnormed)
        dhid_three, dkern_two, dkern_three, dgain_four, dgain_five, dbias_one = res_bwd(
            hidden_three, dhid_four, kernels[2], kernels[3], gains[4], gains[5], saved_last
        )
        dhid_two, din_one, dout_one, dgain_three, dtable = mixer_bwd(
            hidden_two, dhid_three, gains[3], w_in[1], w_out[1], context, saved_temporal
        )
        dhid_one, din_zero, dout_zero, dgain_two, _ = mixer_bwd(
            hidden_one, dhid_two, gains[2], w_in[0], w_out[0], None, saved_spatial
        )
        dhid_zero, dkern_zero, dkern_one, dgain_zero, dgain_one, dbias_zero = res_bwd(
            hidden_zero, dhid_one, kernels[0], kernels[1], gains[0], gains[1], saved_zero
        )
        dtime_pre = jnp.einsum(
            "fv,jfd->jvd", member, jnp.stack([dbias_zero, dbias_one]), precision=HIGH
        ) * swish_grad(time_pre)
        dtime = jnp.einsum("vd,jve->jde", embedding.astype(jnp.float32), dtime_pre, precision=HIGH)
        d_in = jnp.einsum("fcp,fpd->cd", noisy_input, dhid_zero, precision=HIGH)
        matrix_grads = (
            jnp.stack([dkern_zero, dkern_one, dkern_two, dkern_three]).reshape(36 * D, D),
            jnp.stack([din_zero, din_one]).reshape(2 * D, 3 * D),
            jnp.stack([dout_zero, dout_one]).reshape(2 * D, D),
            dtime.reshape(2 * D, D),
        )
        vector_grads = (
            d_in,
            d_out,
            jnp.stack(
                [dgain_zero, dgain_one, dgain_two, dgain_three, dgain_four, dgain_five, dgain_six]
            ),
            dtable,
        )
        matrix_acc = (
            matrix_grads if matrix_acc is None else jax.tree.map(jnp.add, matrix_acc, matrix_grads)
        )
        vector_acc = (
            vector_grads if vector_acc is None else jax.tree.map(jnp.add, vector_acc, vector_grads)
        )
    matrix_acc = reduce_rows(matrix_acc)
    sum_in, sum_out, sum_gains, sum_table, loss_sum = lax.psum(
        (vector_acc[0], vector_acc[1], vector_acc[2], vector_acc[3], loss_local), ("frame", "batch")
    )
    local_square = sum((jnp.sum(grad * grad) for grad in matrix_acc))
    square = lax.psum(local_square, ("frame", "batch")) + sum(
        (jnp.sum(grad * grad) for grad in (sum_in, sum_out, sum_gains, sum_table))
    )
    grad_norm = jnp.sqrt(square)
    clip_scale = CLIP / jnp.maximum(grad_norm, CLIP)
    conv_new, conv_first_new, conv_second_new = adamw(
        conv_weight, conv_first, conv_second, matrix_acc[0], clip_scale, RATES[0]
    )
    pin_new, pin_first_new, pin_second_new = adamw(
        proj_in, proj_in_first, proj_in_second, matrix_acc[1], clip_scale, RATES[1]
    )
    pout_new, pout_first_new, pout_second_new = adamw(
        proj_out, proj_out_first, proj_out_second, matrix_acc[2], clip_scale, RATES[2]
    )
    time_new, time_first_new, time_second_new = adamw(
        time_weight, time_first, time_second, matrix_acc[3], clip_scale, RATES[3]
    )
    in_new, in_first_new, in_second_new = adamw(
        in_weight, in_first, in_second, sum_in, clip_scale, RATES[4]
    )
    out_new, out_first_new, out_second_new = adamw(
        out_weight, out_first, out_second, sum_out, clip_scale, RATES[5]
    )
    gains_new, gains_first_new, gains_second_new = adamw(
        gains, gains_first, gains_second, sum_gains, clip_scale, RATES[6]
    )
    bias_new, bias_first_new, bias_second_new = adamw(
        rel_bias, rel_bias_first, rel_bias_second, sum_table, clip_scale, RATES[7]
    )
    return (
        loss_sum,
        pixel_total,
        grad_norm,
        conv_new,
        conv_first_new,
        conv_second_new,
        pin_new,
        pin_first_new,
        pin_second_new,
        pout_new,
        pout_first_new,
        pout_second_new,
        time_new,
        time_first_new,
        time_second_new,
        in_new,
        in_first_new,
        in_second_new,
        out_new,
        out_first_new,
        out_second_new,
        gains_new,
        gains_first_new,
        gains_second_new,
        bias_new,
        bias_first_new,
        bias_second_new,
    )


def solution(mesh):
    in_specs = (
        P(None, "batch", "frame", None, None),
        P(None, "batch", "frame", None, None),
        P(),
        P(),
        P("frame", "batch"),
        P("frame", "batch"),
        P("frame", "batch"),
        P("frame", "batch"),
        P("frame", "batch"),
        P("frame", "batch"),
        P("frame", "batch"),
        P("frame", "batch"),
        P("frame", "batch"),
        P("frame", "batch"),
        P("frame", "batch"),
        P("frame", "batch"),
        P(),
        P(),
        P(),
        P(),
        P(),
        P(),
        P(),
        P(),
        P(),
        P(),
        P(),
        P(),
    )
    out_specs = (
        P(),
        P(),
        P(),
        P("frame", "batch"),
        P("frame", "batch"),
        P("frame", "batch"),
        P("frame", "batch"),
        P("frame", "batch"),
        P("frame", "batch"),
        P("frame", "batch"),
        P("frame", "batch"),
        P("frame", "batch"),
        P("frame", "batch"),
        P("frame", "batch"),
        P("frame", "batch"),
        P(),
        P(),
        P(),
        P(),
        P(),
        P(),
        P(),
        P(),
        P(),
        P(),
        P(),
        P(),
    )
    sizes = tuple(mesh.shape[name] for name in ("frame", "batch"))
    local = shards_pairs if sizes == (8, 4) else shards
    return jax.shard_map(local, mesh=mesh, in_specs=in_specs, out_specs=out_specs, check_vma=False)
```
